32 devices in a mesh: slab: 4 (over z), front: 8 (over y, x, core).
Axes of the slice: x: 2, y: 2, z: 4, core: 2. Of those that a mesh axis runs over, the one named last changes fastest.
Arguments:
- leaf_rhs: bfloat16 [4, 2, 128, 128, 512], P('slab', None, 'front'), may hold values from -6 to 6
- leaf_inv: bfloat16 [4, 128, 2, 128, 128], P('slab', 'front'), may hold values from -0.375 to 0.375
- leaf_off: bfloat16 [4, 128, 2, 128, 128], P('slab', 'front'), may hold values from -0.125 to 0.125
- parent: int32 [4, 128, 1], P('slab', 'front'), may hold values from 0 to 7; in each aligned block of 16 rows (0 to 15, 16 to 31, ..., all dimensions but the last counted through in order) at most 2 rows name the same one
- ancestors: int32 [4, 128, 128], P('slab', 'front'), may hold values from 0 to 255
- root_rhs: bfloat16 [4, 2, 2048, 512], P('slab', None, 'front'), may hold values from -6 to 6
- root_inv: float32 [4, 16, 2, 128, 128], P('slab', 'front'), may hold values from -2 to 2.5
- coupling: float32 [4, 2048], P('slab', 'front'), may hold values from 0.6 to 1.3
Outputs:
- leaf_sol: bfloat16 [4, 2, 128, 128, 512], P('slab', None, 'front')
- root_sol: float32 [4, 2, 2048, 512], P('slab', None, 'front')
The draws below stay inside these ranges and needn't reach their ends.
Inputs may be any that keep to these rules, and one draw needn't show every extreme that they name: Each front index's 16 leaf blocks of a slab name any one parent at most 2 times. `ancestors`: rows may repeat within a block.
All inputs are finite; a program needn't handle non-finite values.
Results may differ from the reference program's by a relative error of at most 0.0057.
Values may be sent and summed in bfloat16 or wider, within the bound.
No kernel may reach another device: no remote copies, remote signals or barrier semaphores. Data moves between devices by JAX's collectives and lax.ppermute only.
A program may use at most 128 MiB of HBM per device.

```python
import math
import jax
import jax.numpy as jnp
import numpy as np
from jax import lax

BLK = 128
ROOT_DEV = 256
LEAF_DEV = 16
SLABS = 4
LEAVES = 128
TRACE = 2048
PCOLS = 512
CAP = 2
N_FRONT = 8


def draw_root_inv(key, part):
    shape = (SLABS, TRACE // BLK, 2, BLK, BLK)
    noise = jax.random.truncated_normal(key, -4.0, 4.0, shape, jnp.float32)
    eye = jnp.eye(BLK, dtype=jnp.float32)
    diagonal = jnp.stack([0.8 * eye, 0.0 * eye])
    return diagonal + noise * (0.35 / BLK ** 0.5)


def plant(values, own_key, low, top_value):
    index_at = [jax.random.randint(jax.random.fold_in(own_key, axis), (), 0, length) for axis, length in enumerate(values.shape)]
    widest = values.shape.index(max(values.shape))
    neighbour = index_at[:widest] + [(index_at[widest] + 1) % values.shape[widest]] + index_at[widest + 1:]
    return values.at[tuple(index_at)].set(low).at[tuple(neighbour)].set(top_value)


def steps_of(rng, dims, cuts, low, top_value):
    gain = 1.0
    for position, parts in cuts:
        heights = jax.random.uniform(jax.random.fold_in(jax.random.fold_in(rng, 6), position), (parts,), jnp.float32, low / len(cuts), top_value / len(cuts))
        gain = gain * jnp.repeat(jnp.exp(heights), dims[position] // parts).reshape((-1,) + (1,) * (len(dims) - 1 - position))
    return gain


def rank_table(amount, slope):
    loads = [(1 << 20) // math.isqrt(rank ** slope) + 1 for rank in range(1, amount + 1)]
    spread = 1 + sum(loads) // (1 << 30)
    return np.cumsum(np.array([max(1, weight // spread) for weight in loads]))


def ranked(own_key, dims, amount, lean):
    listing = rank_table(amount, lean)
    lot = jax.random.randint(jax.random.fold_in(own_key, 1), dims, 0, int(listing[amount - 1]))
    grade = jnp.searchsorted(jnp.asarray(listing, jnp.int32), lot, side="right")
    return jax.random.permutation(jax.random.fold_in(own_key, 2), amount)[grade].astype(jnp.int32)


def routed_block(rng, own, number, rows, count, top, most, lean):
    sequence = jax.random.permutation(rng, count)
    packed, ordinary = load_shares(count, rows * top, most, lean, True), load_shares(count, rows * top, most, lean, False)
    places = jnp.arange(count)

    def named(sizes, turn):
        used = int((sizes > 0).sum())
        fixed = max(1, used // 4)
        passed = fixed + (places - fixed + turn * (used - fixed)) % max(1, count - fixed)
        return jnp.zeros((count,), jnp.int32).at[sequence[jnp.where(places < fixed, places, passed)]].set(jnp.asarray(sizes, jnp.int32))

    sizes = jnp.where(number % 4 == 0, named(packed, number // 4), named(ordinary, number - number // 4 - 1))
    mixed = jax.random.permutation(jax.random.fold_in(own, 3), count)
    giver, taker = mixed[0:count // 2 * 2:2], mixed[1:count // 2 * 2:2]
    slack = jnp.minimum(sizes[giver] - 1, most - sizes[taker]) // 2
    slack = jnp.where((giver == sequence[0]) | (taker == sequence[0]) | (sizes[taker] == 0), 0, jnp.maximum(slack, 0))
    passed = jax.random.randint(jax.random.fold_in(own, 4), (count // 2,), 0, 1 << 20) % (slack + 1)
    sizes = sizes.at[giver].add(-passed).at[taker].add(passed)
    items = jnp.searchsorted(jnp.cumsum(sizes), jnp.arange(rows * top), side="right").astype(jnp.int32)
    table = items.reshape(top, rows).T
    table = table[jax.random.permutation(jax.random.fold_in(own, 1), rows)]
    turn = jax.random.randint(jax.random.fold_in(own, 2), (rows, 1), 0, top)
    return jnp.take_along_axis(table, (jnp.arange(top)[None, :] + turn) % top, axis=1)


def load_shares(count, total, most, skew, full):
    portions = [(1 << 20) // math.isqrt(standing ** skew) + 1 for standing in range(1, count + 1)]
    largest = most if full else min(most, max(-(-total // count), total * portions[0] // sum(portions)))
    least = 1 if total - largest >= count - 1 else 0
    given, surplus = [largest] + [least] * (count - 1), total - largest - least * (count - 1)
    while surplus > 0:
        candidates = [i for i in range(1, count) if given[i] < largest] or [i for i in range(1, count) if given[i] < most]
        pool, budget = sum([portions[i] for i in candidates]), surplus
        for i in candidates:
            extra = min(most - given[i], max(1, budget * portions[i] // pool), surplus)
            given[i] = given[i] + extra
            surplus = surplus - extra
    return np.array(given)


def centred(rng, shape, deviation, reach, pieces=(), held_as=jnp.bfloat16):
    factor_of = steps_of(rng, shape, pieces, -0.22, 0.18) if pieces else 1.0
    drawn = jax.random.normal(rng, shape, jnp.float32) * deviation * factor_of
    return jnp.minimum(jnp.maximum(drawn, -reach), reach).astype(held_as)


def setup_inputs(seed: int = 0) -> dict:
    key_of = jax.random.split(jax.random.key(seed), 9)
    leaf_rhs = centred(key_of[0], (SLABS, 2, LEAVES, BLK, PCOLS), 1.0, 6.0, ((0, 4), (2, 8)))
    leaf_inv = centred(key_of[1], (SLABS, LEAVES, 2, BLK, BLK), (2 * BLK) ** -0.5, 0.375, ((0, 4), (1, 8)))
    leaf_off = centred(key_of[2], (SLABS, LEAVES, 2, BLK, BLK), (16 * BLK) ** -0.5, 0.125, ((0, 4), (1, 8)))
    parent_keys = jax.random.split(jax.random.fold_in(key_of[3], 1), SLABS * LEAVES // LEAF_DEV)
    parent_turns = jax.random.permutation(jax.random.fold_in(key_of[3], 3), SLABS * LEAVES // LEAF_DEV)
    parent = jax.vmap(lambda own, number: routed_block(jax.random.fold_in(key_of[3], 2), own, number, LEAF_DEV, N_FRONT, 1, CAP, 2))(parent_keys, parent_turns).reshape((SLABS, LEAVES, 1))
    ancestors = plant(ranked(key_of[4], (SLABS, LEAVES, BLK), ROOT_DEV, 1), jax.random.fold_in(key_of[4], 3), 0, ROOT_DEV - 1).astype(jnp.int32)
    root_rhs = centred(key_of[5], (SLABS, 2, TRACE, PCOLS), 1.0, 6.0, ((0, 4), (2, 8)))
    root_inv = draw_root_inv(jax.random.fold_in(key_of[8], 71), 0)
    coupling = jnp.clip(jnp.exp(math.log(1.3) - 0.7731898 * jax.random.uniform(key_of[7], (SLABS, TRACE), jnp.float32) ** steps_of(key_of[7], (SLABS, TRACE), ((0, 4), (1, 8)), -0.2, 0.2)), 0.6, 1.3)
    return {"leaf_rhs": leaf_rhs, "leaf_inv": leaf_inv, "leaf_off": leaf_off, "parent": parent, "ancestors": ancestors, "root_rhs": root_rhs, "root_inv": root_inv, "coupling": coupling}


def cplx(mat, vec, form):
    real = jnp.einsum(form, mat[:, 0], vec[0]) - jnp.einsum(form, mat[:, 1], vec[1])
    imag = jnp.einsum(form, mat[:, 0], vec[1]) + jnp.einsum(form, mat[:, 1], vec[0])
    return jnp.stack([real, imag])


def block_solve(blocks, field):
    highest = lax.Precision.HIGHEST
    shaped = field.reshape(2, blocks.shape[0], blocks.shape[2], field.shape[-1])
    real = jnp.einsum("kij,kjc->kic", blocks[:, 0], shaped[0], precision=highest) - jnp.einsum("kij,kjc->kic", blocks[:, 1], shaped[1], precision=highest)
    imag = jnp.einsum("kij,kjc->kic", blocks[:, 0], shaped[1], precision=highest) + jnp.einsum("kij,kjc->kic", blocks[:, 1], shaped[0], precision=highest)
    return jnp.stack([real, imag]).reshape(field.shape)


def reference(leaf_rhs, leaf_inv, leaf_off, parent, ancestors, root_rhs, root_inv, coupling):
    forward_form = "lij,ljc->lic"
    back_form = "lji,ljc->lic"

    def leaf_forward(item):
        rhs, inv, off, par, anc, right = item
        fwd = lax.optimization_barrier(cplx(inv.astype(jnp.float32), rhs.astype(jnp.float32), forward_form).astype(jnp.bfloat16))
        part = lax.optimization_barrier(cplx(off.astype(jnp.float32), fwd.astype(jnp.float32), forward_form).astype(jnp.bfloat16))
        rows = (par[:, 0:1] * ROOT_DEV + anc).astype(jnp.int32).reshape(-1)
        flat = part.astype(jnp.float32).reshape(2, -1, PCOLS)
        summed = jnp.zeros((2, TRACE, PCOLS), jnp.float32).at[:, rows].add(flat)
        return fwd, right.astype(jnp.float32) - summed

    fwd_all, reduced = lax.map(leaf_forward, (leaf_rhs, leaf_inv, leaf_off, parent, ancestors, root_rhs))

    def link(previous, item):
        right, blocks, cpl = item
        state = block_solve(blocks, right - cpl[None, :, None] * previous)
        return state, state

    start = jnp.zeros((2, TRACE, PCOLS), jnp.float32)
    _, roots = lax.scan(link, start, (reduced, root_inv, coupling))

    def leaf_back(item):
        fwd, inv, off, par, anc, root = item
        half = lax.optimization_barrier(root.astype(jnp.bfloat16))
        rows = (par[:, 0:1] * ROOT_DEV + anc).astype(jnp.int32).reshape(-1)
        picked = half.astype(jnp.float32)[:, rows].reshape(2, LEAVES, BLK, PCOLS)
        back = lax.optimization_barrier(cplx(off.astype(jnp.float32), picked, back_form).astype(jnp.bfloat16))
        return (fwd.astype(jnp.float32) - cplx(inv.astype(jnp.float32), back.astype(jnp.float32), forward_form)).astype(jnp.bfloat16)

    leaves = lax.map(leaf_back, (fwd_all, leaf_inv, leaf_off, parent, ancestors, roots))
    return leaves, roots
```

```python
import functools

import jax
import jax.numpy as jnp
from jax import lax
from jax.experimental import pallas as pl
from jax.experimental.pallas import tpu as pltpu
from jax.sharding import PartitionSpec as P

HALVES = 2
BF = jnp.bfloat16
F32 = jnp.float32
VMEM = pl.BlockSpec(memory_space=pltpu.VMEM)


def params():
    return pltpu.CompilerParams(vmem_limit_bytes=40 * 1024 * 1024)


def crossed(x, axis, mask):
    return lax.ppermute(x, axis, [(i, i ^ mask) for i in range(lax.axis_size(axis))])


def spread(vec):
    half = vec.shape[1] // 2
    return jnp.concatenate([vec, jnp.concatenate([-vec[:, half:], vec[:, :half]], axis=1)], axis=0)


def dot(a, b, dims=((1,), (0,)), precision=None):
    return lax.dot_general(a, b, (dims, ((), ())), precision=precision, preferred_element_type=F32)


def table_of(anc_row, rows):
    ids = lax.broadcasted_iota(jnp.int32, (rows, anc_row.shape[1]), 0)
    return (ids == anc_row).astype(F32).astype(BF)


def forward_kernel(group, cap, fronts, rows, owners, place, rhs, inv, off, anc, fwd, keep, send, part, ids, seen):
    step = pl.program_id(0)
    me = place[1]
    blk = rhs.shape[3]

    @pl.when(step == 0)
    def _():
        ids[...] = jnp.full(ids.shape, -1, jnp.int32)

        def clear(i, carry):
            seen[i] = 0
            return carry

        lax.fori_loop(0, fronts, clear, 0)

    for j in range(group):
        leaf = step * group + j
        dist = owners[leaf] ^ me
        rank = seen[dist]
        seen[dist] = rank + 1
        mat = jnp.concatenate([inv[0, j, 0], inv[0, j, 1]], axis=1)
        vec = jnp.concatenate([rhs[0, 0, j], rhs[0, 1, j]], axis=1)
        value = dot(mat, spread(vec)).astype(BF)
        fwd[j] = value
        mat = jnp.concatenate([off[0, j, 0], off[0, j, 1]], axis=1)
        part[dist, rank] = dot(mat, spread(value)).astype(BF)
        ids[pl.ds(dist * cap + rank, 1), :] = anc[0, pl.ds(leaf, 1), :]

    @pl.when(step == pl.num_programs(0) - 1)
    def _():
        for dist in range(fronts):
            for rank in range(cap):

                @pl.when(seen[dist] <= rank)
                def _():
                    part[dist, rank] = jnp.zeros(part.shape[2:], BF)

            row = jnp.concatenate([ids[dist * cap + rank : dist * cap + rank + 1, :] for rank in range(cap)], axis=1)
            total = dot(table_of(row, rows), part[dist].reshape(cap * blk, part.shape[3]))
            if dist % 2:
                send[dist // 2] = total.astype(BF)
            else:
                keep[dist // 2] = total.astype(BF)


def forward(h, owners, place, leaf_rhs, leaf_inv, leaf_off, ancestors, fronts, rows):
    _, _, leaves, blk, width = leaf_rhs.shape
    cols = width // HALVES
    cap = -(-leaves // fronts)
    group = 4
    spec = pltpu.PrefetchScalarGridSpec(
        num_scalar_prefetch=2,
        grid=(leaves // group,),
        in_specs=[
            pl.BlockSpec((1, 2, group, blk, cols), lambda i, o, p: (0, 0, i, 0, h)),
            pl.BlockSpec((1, group, 2, blk, blk), lambda i, o, p: (0, i, 0, 0, 0)),
            pl.BlockSpec((1, group, 2, blk, blk), lambda i, o, p: (0, i, 0, 0, 0)),
            pl.BlockSpec((1, leaves, blk), lambda i, o, p: (0, 0, 0)),
        ],
        out_specs=[pl.BlockSpec((group, blk, 2 * cols), lambda i, o, p: (i, 0, 0)), VMEM, VMEM],
        scratch_shapes=[
            pltpu.VMEM((fronts, cap, blk, 2 * cols), BF),
            pltpu.VMEM((fronts * cap, blk), jnp.int32),
            pltpu.SMEM((fronts,), jnp.int32),
        ],
    )
    block = jax.ShapeDtypeStruct((fronts // 2, rows, 2 * cols), BF)
    return pl.pallas_call(
        functools.partial(forward_kernel, group, cap, fronts, rows),
        grid_spec=spec,
        out_shape=[jax.ShapeDtypeStruct((leaves, blk, 2 * cols), BF), block, block],
        compiler_params=params(),
        cost_estimate=pl.CostEstimate(flops=6 * leaves * blk * 2 * blk * 2 * cols, bytes_accessed=6 << 20, transcendentals=0),
        name="leaf_forward",
    )(owners, place, leaf_rhs, leaf_inv, leaf_off, ancestors)


def fold_kernel(group, rows, inv, off, anc, out):
    step = pl.program_id(0)
    for j in range(group):
        leaf = step * group + j
        mat = jnp.concatenate([inv[0, j, 0], inv[0, j, 1]], axis=1)
        real, imag = off[0, j, 0], off[0, j, 1]
        other = jnp.concatenate([jnp.concatenate([real, -imag], axis=1), jnp.concatenate([imag, real], axis=1)], axis=0)
        both = dot(mat, other, ((1,), (1,))).astype(BF)
        blk = real.shape[0]
        table = table_of(anc[0, pl.ds(leaf, 1), :], rows)
        out[j, :, :rows] = dot(both[:, :blk], table, ((1,), (1,))).astype(BF)
        out[j, :, rows:] = dot(both[:, blk:], table, ((1,), (1,))).astype(BF)


def fold(leaf_inv, leaf_off, ancestors, rows):
    _, leaves, _, blk, _ = leaf_inv.shape
    group = 4
    return pl.pallas_call(
        functools.partial(fold_kernel, group, rows),
        grid=(leaves // group,),
        in_specs=[
            pl.BlockSpec((1, group, 2, blk, blk), lambda i: (0, i, 0, 0, 0)),
            pl.BlockSpec((1, group, 2, blk, blk), lambda i: (0, i, 0, 0, 0)),
            pl.BlockSpec((1, leaves, blk), lambda i: (0, 0, 0)),
        ],
        out_specs=pl.BlockSpec((group, blk, 2 * rows), lambda i: (i, 0, 0)),
        out_shape=jax.ShapeDtypeStruct((leaves, blk, 2 * rows), BF),
        compiler_params=params(),
        cost_estimate=pl.CostEstimate(flops=2 * leaves * blk * 2 * blk * 4 * blk, bytes_accessed=4 << 20, transcendentals=0),
        name="leaf_fold",
    )(leaf_inv, leaf_off, ancestors)


def pack_kernel(place, inv, cpl, same, other):
    blocks = inv.shape[1]
    blk = inv.shape[3]
    mine = place[0] % blocks
    for kind, out in enumerate((same, other)):
        block = mine ^ kind
        out[:blk, :] = inv[0, block, 0]
        out[blk : 2 * blk, :] = inv[0, block, 1]
        out[2 * blk :, :] = jnp.broadcast_to(cpl[0, pl.ds(block, 1), :], (8, blk))


def pack(place, root_inv, coupling):
    _, blocks, _, blk, _ = root_inv.shape
    shape = jax.ShapeDtypeStruct((2 * blk + 8, blk), F32)
    return pl.pallas_call(
        pack_kernel,
        in_specs=[pl.BlockSpec(memory_space=pltpu.SMEM), VMEM, VMEM],
        out_specs=[VMEM, VMEM],
        out_shape=[shape, shape],
        compiler_params=params(),
        name="solve_pack",
    )(place, root_inv, coupling.reshape(1, blocks, blk))


def piece_of(index, blk, blocks, part):
    low, left = (index % blocks) * blk, (index // blocks) * part
    return slice(low, low + blk), left


def reduce_kernel(slabs, blk, part, terms, place, rhs, keep, near, *refs):
    cols = rhs.shape[3]
    blocks = rhs.shape[2] // blk
    total = keep[0].astype(F32) + near[0].astype(F32)
    for ref in refs[:terms]:
        total = total + ref[...].astype(F32)
    real = (rhs[0, 0].astype(F32) - total[:, :cols]).astype(BF)
    imag = (rhs[0, 1].astype(F32) - total[:, cols:]).astype(BF)
    outs = refs[terms:]
    for index in range(slabs):
        rows, left = piece_of(index, blk, blocks, part)
        piece = jnp.concatenate([real[rows, left : left + part], imag[rows, left : left + part]], axis=1)
        for mask, out in enumerate(outs):

            @pl.when(place[0] ^ mask == index)
            def _(piece=piece, out=out):
                out[...] = piece


def reduce(h, place, root_rhs, keep, near, far, slabs, blk):
    _, _, rows, width = root_rhs.shape
    cols = width // HALVES
    part = cols * (rows // blk) // slabs
    spec = pltpu.PrefetchScalarGridSpec(
        num_scalar_prefetch=1,
        grid=(1,),
        in_specs=[
            pl.BlockSpec((1, 2, rows, cols), lambda i, p: (0, 0, 0, h)),
            pl.BlockSpec((1, rows, 2 * cols), lambda i, p: (0, 0, 0)),
            pl.BlockSpec((1, rows, 2 * cols), lambda i, p: (0, 0, 0)),
        ]
        + [VMEM] * len(far),
        out_specs=[VMEM] * slabs,
    )
    return pl.pallas_call(
        functools.partial(reduce_kernel, slabs, blk, part, len(far)),
        grid_spec=spec,
        out_shape=[jax.ShapeDtypeStruct((blk, 2 * part), BF)] * slabs,
        compiler_params=params(),
        name="interface_reduce",
    )(place, root_rhs, keep, near, *far)


def chain_kernel(slabs, place, *refs):
    pieces, mats = refs[:slabs], refs[slabs : 2 * slabs]
    outs = refs[2 * slabs : 3 * slabs]
    held, solver = refs[3 * slabs :]
    me = place[0]
    for mask in range(slabs):
        held[mask] = pieces[mask][...]
        solver[mask] = mats[mask][...]
    blk = held.shape[1]
    part = held.shape[2] // 2
    state = None
    for slab in range(slabs):
        at = me ^ slab
        field = held[at].astype(F32)
        packed = solver[at]
        if state is not None:
            scale = jnp.broadcast_to(packed[2 * blk : 2 * blk + 1, :], (blk, blk)).T
            field = field - scale[:, :1] * state
        mat = jnp.concatenate([packed[:blk], packed[blk : 2 * blk]], axis=1)
        state = dot(mat, spread(field), precision=lax.Precision.HIGHEST)
        half = state.astype(BF)
        for mask, out in enumerate(outs):

            @pl.when(at == mask)
            def _(half=half, out=out):
                out[...] = half


def chain(place, pieces, mats):
    slabs = len(pieces)
    return pl.pallas_call(
        functools.partial(chain_kernel, slabs),
        in_specs=[pl.BlockSpec(memory_space=pltpu.SMEM)] + [VMEM] * (2 * slabs),
        out_specs=[VMEM] * slabs,
        out_shape=[jax.ShapeDtypeStruct(pieces[0].shape, BF)] * slabs,
        scratch_shapes=[
            pltpu.VMEM((slabs,) + pieces[0].shape, BF),
            pltpu.VMEM((slabs,) + mats[0].shape, F32),
        ],
        compiler_params=params(),
        name="sweep_chain",
    )(place, *pieces, *mats)


def collect_kernel(slabs, blk, part, blocks, aliased, place, *refs):
    pieces = refs[:slabs]
    own, root = refs[slabs + aliased :]
    cols = own.shape[1] // 2
    for mask, piece in enumerate(pieces):
        for index in range(slabs):
            rows, left = piece_of(index, blk, blocks, part)

            @pl.when(place[0] ^ mask == index)
            def _(piece=piece, rows=rows, left=left):
                real, imag = piece[:, :part], piece[:, part:]
                own[rows, left : left + part] = real
                own[rows, cols + left : cols + left + part] = imag
                root[0, 0, rows, left : left + part] = real.astype(F32)
                root[0, 1, rows, left : left + part] = imag.astype(F32)


def collect(h, place, pieces, before, rows, width):
    slabs = len(pieces)
    blk, part = pieces[0].shape[0], pieces[0].shape[1] // 2
    cols = width // HALVES
    aliased = [] if before is None else [before]
    spec = pltpu.PrefetchScalarGridSpec(
        num_scalar_prefetch=1,
        grid=(1,),
        in_specs=[VMEM] * slabs + [pl.BlockSpec(memory_space=pl.ANY)] * len(aliased),
        out_specs=[VMEM, pl.BlockSpec((1, 2, rows, cols), lambda i, p: (0, 0, 0, h))],
    )
    return pl.pallas_call(
        functools.partial(collect_kernel, slabs, blk, part, rows // blk, len(aliased)),
        grid_spec=spec,
        out_shape=[
            jax.ShapeDtypeStruct((rows, 2 * cols), BF),
            jax.ShapeDtypeStruct((1, 2, rows, width), F32),
        ],
        input_output_aliases={1 + slabs: 1} if aliased else {},
        compiler_params=params(),
        name="interface_collect",
    )(place, *pieces, *aliased)


def backward_kernel(group, fronts, aliased, owners, place, fwd, mats, *refs):
    fields = refs[:fronts]
    out, wide = refs[fronts + aliased :]
    step = pl.program_id(0)
    cols = fwd.shape[2] // 2

    @pl.when(step == 0)
    def _():
        for dist in range(fronts):
            wide[dist] = spread(fields[dist][...])

    for j in range(group):
        dist = owners[step * group + j] ^ place[1]
        value = fwd[j].astype(F32) - dot(mats[j], wide[dist])
        out[0, 0, j] = value[:, :cols].astype(BF)
        out[0, 1, j] = value[:, cols:].astype(BF)


def backward(h, owners, place, fwd, mats, fields, before, width):
    leaves, blk, wide = fwd.shape
    cols = wide // 2
    rows = fields[0].shape[0]
    fronts = len(fields)
    group = 4
    aliased = [] if before is None else [before]
    spec = pltpu.PrefetchScalarGridSpec(
        num_scalar_prefetch=2,
        grid=(leaves // group,),
        in_specs=[
            pl.BlockSpec((group, blk, wide), lambda i, o, p: (i, 0, 0)),
            pl.BlockSpec((group, blk, 2 * rows), lambda i, o, p: (i, 0, 0)),
        ]
        + [VMEM] * fronts
        + [pl.BlockSpec(memory_space=pl.ANY)] * len(aliased),
        out_specs=pl.BlockSpec((1, 2, group, blk, cols), lambda i, o, p: (0, 0, i, 0, h)),
        scratch_shapes=[pltpu.VMEM((fronts, 2 * rows, wide), BF)],
    )
    return pl.pallas_call(
        functools.partial(backward_kernel, group, fronts, len(aliased)),
        grid_spec=spec,
        out_shape=jax.ShapeDtypeStruct((1, 2, leaves, blk, width), BF),
        input_output_aliases={4 + fronts: 0} if aliased else {},
        compiler_params=params(),
        cost_estimate=pl.CostEstimate(flops=2 * leaves * blk * 2 * rows * wide, bytes_accessed=8 << 20, transcendentals=0),
        name="leaf_backward",
    )(owners, place, fwd, mats, *fields, *aliased)


def body(leaf_rhs, leaf_inv, leaf_off, parent, ancestors, root_rhs, root_inv, coupling):
    fronts, slabs = lax.axis_size("front"), lax.axis_size("slab")
    rows, width = root_rhs.shape[2], root_rhs.shape[3]
    blk = leaf_rhs.shape[3]
    owners = parent.reshape(-1)
    place = jnp.stack([lax.axis_index("slab"), lax.axis_index("front")]).astype(jnp.int32)
    pairs = fronts // 2

    same, other = pack(place, root_inv, coupling)
    mats = [same] + [crossed((same, other)[mask % 2], "slab", mask) for mask in range(1, slabs)]

    leaf_fwd, fields = [], []
    for h in range(HALVES):
        fwd, keep, send = forward(h, owners, place, leaf_rhs, leaf_inv, leaf_off, ancestors, fronts, rows)
        leaf_fwd.append(fwd)
        near = crossed(send, "front", 1)
        far = []
        for j in range(1, pairs):
            total = (keep[j].astype(F32) + near[j].astype(F32)).astype(BF)
            far.append(crossed(total, "front", 2 * j))
        fields.append((keep, near, far))
    folded = fold(leaf_inv, leaf_off, ancestors, rows)

    root_sol, leaf_sol = None, None
    for h in range(HALVES):
        keep, near, far = fields[h]
        pieces = reduce(h, place, root_rhs, keep, near, far, slabs, blk)
        pieces = [pieces[0]] + [crossed(pieces[mask], "slab", mask) for mask in range(1, slabs)]
        solved = chain(place, pieces, mats)
        solved = [solved[0]] + [crossed(solved[mask], "slab", mask) for mask in range(1, slabs)]
        own, root_sol = collect(h, place, solved, root_sol, rows, width)
        mine = [own] + [crossed(own, "front", 2 * j) for j in range(1, pairs)]
        theirs = [crossed(value, "front", 1) for value in mine]
        every = [value for pair in zip(mine, theirs) for value in pair]
        leaf_sol = backward(h, owners, place, leaf_fwd[h], folded, every, leaf_sol, width)
    return leaf_sol, root_sol


def solution(mesh):
    in_specs = (
        P("slab", None, "front", None, None),
        P("slab", "front", None, None, None),
        P("slab", "front", None, None, None),
        P("slab", "front", None),
        P("slab", "front", None),
        P("slab", None, "front", None),
        P("slab", "front", None, None, None),
        P("slab", "front"),
    )
    out_specs = (P("slab", None, "front", None, None), P("slab", None, "front", None))
    return jax.shard_map(body, mesh=mesh, in_specs=in_specs, out_specs=out_specs, check_vma=False)
```

```python
import functools

import jax
import jax.numpy as jnp
from jax import lax
from jax.experimental import pallas as pl
from jax.experimental.pallas import tpu as pltpu
from jax.sharding import PartitionSpec as P

HALVES = 2
BF = jnp.bfloat16
F32 = jnp.float32
VMEM = pl.BlockSpec(memory_space=pltpu.VMEM)
SMEM = pl.BlockSpec(memory_space=pltpu.SMEM)
HBM = pl.BlockSpec(memory_space=pltpu.HBM)
ANY = pl.BlockSpec(memory_space=pl.ANY)


def shape_of(shape, dtype=BF):
    return jax.ShapeDtypeStruct(shape, dtype)


def call(kernel, name, ins, in_specs, outs, out_specs, after=(), scratch=(), aliases=None):
    count, extra = len(ins), len(after)

    def wrapped(*refs):
        kernel(*refs[:count], *refs[count + extra :])

    return pl.pallas_call(
        wrapped,
        in_specs=list(in_specs) + [ANY] * extra,
        out_specs=out_specs,
        out_shape=outs,
        scratch_shapes=list(scratch),
        input_output_aliases=aliases or {},
        compiler_params=pltpu.CompilerParams(vmem_limit_bytes=24 * 1024 * 1024),
        cost_estimate=pl.CostEstimate(flops=1, bytes_accessed=1, transcendentals=0),
        name=name,
    )(*ins, *after)


def crossed(x, axis, mask):
    return lax.ppermute(x, axis, [(i, i ^ mask) for i in range(lax.axis_size(axis))])


def stacked(real, imag):
    return jnp.concatenate(
        [jnp.concatenate([real, -imag], axis=1), jnp.concatenate([imag, real], axis=1)], axis=0
    )


def dot(a, b, dims=((1,), (0,)), precision=None):
    return lax.dot_general(a, b, (dims, ((), ())), precision=precision, preferred_element_type=F32)


def table_of(anc_row, rows):
    ids = lax.broadcasted_iota(jnp.int32, (rows, anc_row.shape[1]), 0)
    return (ids == anc_row).astype(F32).astype(BF)


def forward_kernel(h, group, cap, owners, place, rhs, inv, off, anc, fwd, keep, send,
                   vecs, invs, offs, ancs, part, ids, seen, sems):
    leaves, blk, cols = vecs.shape[1], vecs.shape[2], vecs.shape[3]
    fronts, rows = part.shape[0], keep.shape[2]
    me = place[1]
    small = pltpu.make_async_copy(anc.at[0], ancs, sems.at[leaves // group, 0])
    small.start()

    def copies(at):
        span = pl.ds(at * group, group)
        return (
            pltpu.make_async_copy(inv.at[0, span], invs.at[span], sems.at[at, 0]),
            pltpu.make_async_copy(rhs.at[0, :, span, :, pl.ds(h * cols, cols)], vecs.at[:, span], sems.at[at, 1]),
            pltpu.make_async_copy(off.at[0, span], offs.at[span], sems.at[at, 2]),
        )

    for at in range(leaves // group):
        for copy in copies(at):
            copy.start()
    ids[...] = jnp.full(ids.shape, -1, jnp.int32)
    for dist in range(fronts):
        seen[dist] = 0
    small.wait()

    def some(at, carry):
        for copy in copies(at):
            copy.wait()
        for j in range(group):
            leaf = at * group + j
            dist = owners[leaf] ^ me
            rank = seen[dist]
            seen[dist] = rank + 1
            vec = jnp.concatenate([vecs[0, leaf], vecs[1, leaf]], axis=0)
            value = dot(stacked(invs[leaf, 0], invs[leaf, 1]), vec).astype(BF)
            fwd[leaf] = value
            moved = dot(stacked(offs[leaf, 0], offs[leaf, 1]), value).astype(BF)
            part[dist, 0, rank] = moved[:blk]
            part[dist, 1, rank] = moved[blk:]
            ids[pl.ds(dist * cap + rank, 1), :] = ancs[pl.ds(leaf, 1), :]
        return carry

    lax.fori_loop(0, leaves // group, some, 0)
    for dist in range(fronts):
        for rank in range(cap):

            @pl.when(seen[dist] <= rank)
            def _(dist=dist, rank=rank):
                part[dist, 0, rank] = jnp.zeros((blk, cols), BF)
                part[dist, 1, rank] = jnp.zeros((blk, cols), BF)

        row = jnp.concatenate([ids[dist * cap + rank : dist * cap + rank + 1, :] for rank in range(cap)], axis=1)
        table = table_of(row, rows)
        out = send if dist % 2 else keep
        for plane in range(2):
            out[dist // 2, plane] = dot(table, part[dist, plane].reshape(cap * blk, cols)).astype(BF)


def forward(h, owners, place, leaf_rhs, leaf_inv, leaf_off, ancestors, fronts, rows, after):
    _, _, leaves, blk, width = leaf_rhs.shape
    cols = width // HALVES
    cap = -(-leaves // fronts)
    group = 4
    block = shape_of((fronts // 2, 2, rows, cols))
    return call(
        functools.partial(forward_kernel, h, group, cap),
        "leaf_forward",
        [owners, place, leaf_rhs, leaf_inv, leaf_off, ancestors],
        [SMEM, SMEM, HBM, HBM, HBM, HBM],
        [shape_of((leaves, 2 * blk, cols)), block, block],
        [VMEM, VMEM, VMEM],
        after,
        [
            pltpu.VMEM((2, leaves, blk, cols), BF),
            pltpu.VMEM((leaves, 2, blk, blk), BF),
            pltpu.VMEM((leaves, 2, blk, blk), BF),
            pltpu.VMEM((leaves, blk), jnp.int32),
            pltpu.VMEM((fronts, 2, cap, blk, cols), BF),
            pltpu.VMEM((fronts * cap, blk), jnp.int32),
            pltpu.SMEM((fronts,), jnp.int32),
            pltpu.SemaphoreType.DMA((leaves // group + 1, 3)),
        ],
    )


def fold_kernel(inv, off, anc, out):
    leaves, _, blk, _ = inv.shape[1:]
    rows = out.shape[2] // 2

    def one(leaf, carry):
        mat = jnp.concatenate([inv[0, leaf, 0], inv[0, leaf, 1]], axis=1)
        real, imag = off[0, leaf, 0], off[0, leaf, 1]
        other = jnp.concatenate([jnp.concatenate([real, -imag], axis=1), jnp.concatenate([imag, real], axis=1)], axis=0)
        both = dot(mat, other, ((1,), (1,))).astype(BF)
        table = table_of(anc[0, pl.ds(leaf, 1), :], rows)
        out[leaf, :, :rows] = dot(both[:, :blk], table, ((1,), (1,))).astype(BF)
        out[leaf, :, rows:] = dot(both[:, blk:], table, ((1,), (1,))).astype(BF)
        return carry

    lax.fori_loop(0, leaves, one, 0, unroll=2)


def fold(leaf_inv, leaf_off, ancestors, rows, after):
    _, leaves, _, blk, _ = leaf_inv.shape
    return call(
        fold_kernel, "leaf_fold", [leaf_inv, leaf_off, ancestors], [VMEM] * 3,
        shape_of((leaves, blk, 2 * rows)), VMEM, after,
    )


def pack_kernel(place, inv, cpl, same, other, sems):
    blocks, blk = inv.shape[1], inv.shape[3]
    mine = place[0] % blocks
    copies = []
    for kind, out in enumerate((same, other)):
        block = mine ^ kind
        for plane in range(2):
            copies.append(pltpu.make_async_copy(inv.at[0, block, plane], out.at[pl.ds(plane * blk, blk)], sems.at[kind, plane]))
            copies[-1].start()
    for kind, out in enumerate((same, other)):
        out[2 * blk :, :] = jnp.broadcast_to(cpl[0, pl.ds(mine ^ kind, 1), :], (8, blk))
    for copy in copies:
        copy.wait()


def pack(place, root_inv, coupling, after):
    _, blocks, _, blk, _ = root_inv.shape
    shape = shape_of((2 * blk + 8, blk), F32)
    return call(
        pack_kernel, "solve_pack", [place, root_inv, coupling.reshape(1, blocks, blk)], [SMEM, HBM, VMEM],
        [shape, shape], [VMEM, VMEM], after, [pltpu.SemaphoreType.DMA((2, 2))],
    )


def total_kernel(keep, near, *outs):
    for j, out in enumerate(outs):
        out[...] = (keep[j + 1].astype(F32) + near[j + 1].astype(F32)).astype(BF)


def total(keep, near, after):
    pairs = keep.shape[0]
    return call(
        total_kernel, "interface_total", [keep, near], [VMEM, VMEM],
        [shape_of(keep.shape[1:])] * (pairs - 1), [VMEM] * (pairs - 1), after,
    )


def piece_of(index, blk, blocks, part):
    low, left = (index % blocks) * blk, (index // blocks) * part
    return slice(low, low + blk), slice(left, left + part)


def reduce_kernel(h, slabs, blk, part, terms, place, rhs, keep, near, *refs):
    rows, cols = keep.shape[2], keep.shape[3]
    outs = refs[terms:]
    field = []
    for plane in range(2):
        value = keep[0, plane].astype(F32) + near[0, plane].astype(F32)
        for ref in refs[:terms]:
            value = value + ref[plane].astype(F32)
        field.append((rhs[0, plane, :, h * cols : (h + 1) * cols].astype(F32) - value).astype(BF))
    for index in range(slabs):
        at = piece_of(index, blk, rows // blk, part)
        for mask, out in enumerate(outs):

            @pl.when(place[0] ^ mask == index)
            def _(at=at, out=out):
                out[0] = field[0][at]
                out[1] = field[1][at]


def reduce(h, place, root_rhs, keep, near, far, slabs, blk, after):
    _, _, rows, width = root_rhs.shape
    cols = width // HALVES
    part = cols * (rows // blk) // slabs
    return call(
        functools.partial(reduce_kernel, h, slabs, blk, part, len(far)), "interface_reduce",
        [place, root_rhs, keep, near, *far], [SMEM] + [VMEM] * (3 + len(far)),
        [shape_of((2, blk, part))] * slabs, [VMEM] * slabs, after,
    )


def chain_kernel(slabs, place, *refs):
    pieces, mats, outs = refs[:slabs], refs[slabs : 2 * slabs], refs[2 * slabs : 3 * slabs]
    held, solver = refs[3 * slabs :]
    me = place[0]
    for mask in range(slabs):
        held[mask] = pieces[mask][...]
        solver[mask] = mats[mask][...]
    _, _, blk, part = held.shape
    state = None
    for slab in range(slabs):
        at = me ^ slab
        field = held[at].reshape(2 * blk, part).astype(F32)
        packed = solver[at]
        if state is not None:
            scale = jnp.broadcast_to(packed[2 * blk : 2 * blk + 1, :], (blk, blk)).T[:, :1]
            field = field - jnp.concatenate([scale, scale], axis=0) * state
        mat = stacked(packed[:blk], packed[blk : 2 * blk])
        state = dot(mat, field, precision=lax.Precision.HIGHEST)
        half = state.astype(BF)
        for mask, out in enumerate(outs):

            @pl.when(at == mask)
            def _(half=half, out=out):
                out[0] = half[:blk]
                out[1] = half[blk:]


def chain(place, pieces, mats, after):
    slabs = len(pieces)
    return call(
        functools.partial(chain_kernel, slabs), "sweep_chain", [place, *pieces, *mats], [SMEM] + [VMEM] * (2 * slabs),
        [shape_of(pieces[0].shape)] * slabs, [VMEM] * slabs, after,
        [pltpu.VMEM((slabs,) + pieces[0].shape, BF), pltpu.VMEM((slabs,) + mats[0].shape, F32)],
    )


def collect_kernel(h, slabs, aliased, place, *refs):
    pieces = refs[:slabs]
    own, root, full, sem = refs[slabs + aliased :]
    _, blk, part = pieces[0].shape
    rows, cols = own.shape[1], own.shape[2]
    for mask, piece in enumerate(pieces):
        for index in range(slabs):
            at = piece_of(index, blk, rows // blk, part)

            @pl.when(place[0] ^ mask == index)
            def _(piece=piece, at=at):
                for plane in range(2):
                    own[(plane,) + at] = piece[plane]
                    full[(plane,) + at] = piece[plane].astype(F32)

    copy = pltpu.make_async_copy(full, root.at[0, :, :, pl.ds(h * cols, cols)], sem)
    copy.start()
    copy.wait()


def collect(h, place, pieces, before, rows, width, after):
    slabs = len(pieces)
    cols = width // HALVES
    aliased = [] if before is None else [before]
    return call(
        functools.partial(collect_kernel, h, slabs, len(aliased)), "interface_collect",
        [place, *pieces, *aliased], [SMEM] + [VMEM] * slabs + [HBM] * len(aliased),
        [shape_of((2, rows, cols)), shape_of((1, 2, rows, width), F32)], [VMEM, HBM], after,
        [pltpu.VMEM((2, rows, cols), F32), pltpu.SemaphoreType.DMA],
        {1 + slabs: 1} if aliased else None,
    )


def backward_kernel(h, fronts, cap, aliased, owners, place, fwd, mats, *refs):
    fields = refs[:fronts]
    out, held, slots, sems = refs[fronts + aliased :]
    leaves, wide, cols = fwd.shape
    blk = wide // 2
    rows = mats.shape[2] // 2
    for dist in range(fronts):
        for rank in range(cap):
            slots[dist * cap + rank] = -1
    for leaf in range(leaves):
        first = (owners[leaf] ^ place[1]) * cap
        place_at = first
        for rank in range(cap - 1):
            place_at = jnp.where(slots[first + rank] >= 0, first + rank + 1, place_at)
        slots[place_at] = leaf

    def copy_of(leaf):
        return pltpu.make_async_copy(held.at[leaf], out.at[0, :, leaf, :, pl.ds(h * cols, cols)], sems.at[leaf])

    for dist in range(fronts):
        field = fields[dist][...].reshape(2 * rows, cols)
        names = [slots[dist * cap + rank] for rank in range(cap)]
        parts = []
        for name in names:
            leaf = jnp.maximum(name, 0)
            real, imag = mats[leaf, :, :rows], mats[leaf, :, rows:]
            parts += [jnp.concatenate([real, -imag], axis=1), jnp.concatenate([imag, real], axis=1)]
        value = dot(jnp.concatenate(parts, axis=0), field)
        for rank, name in enumerate(names):

            @pl.when(name >= 0)
            def _(rank=rank, name=name):
                result = fwd[name].astype(F32) - value[rank * wide : (rank + 1) * wide]
                held[name, 0] = result[:blk].astype(BF)
                held[name, 1] = result[blk:].astype(BF)
                copy_of(name).start()

    for leaf in range(leaves):
        copy_of(leaf).wait()


def backward(h, owners, place, fwd, mats, fields, before, width, after):
    leaves, wide, cols = fwd.shape
    blk, rows, fronts = wide // 2, mats.shape[2] // 2, len(fields)
    cap = -(-leaves // fronts)
    aliased = [] if before is None else [before]
    return call(
        functools.partial(backward_kernel, h, fronts, cap, len(aliased)), "leaf_backward",
        [owners, place, fwd, mats, *fields, *aliased], [SMEM, SMEM] + [VMEM] * (2 + fronts) + [HBM] * len(aliased),
        shape_of((1, 2, leaves, blk, width)), HBM, after,
        [
            pltpu.VMEM((leaves, 2, blk, cols), BF),
            pltpu.SMEM((fronts * cap,), jnp.int32),
            pltpu.SemaphoreType.DMA((leaves,)),
        ],
        {4 + fronts: 0} if aliased else None,
    )


def body(leaf_rhs, leaf_inv, leaf_off, parent, ancestors, root_rhs, root_inv, coupling):
    fronts, slabs = lax.axis_size("front"), lax.axis_size("slab")
    rows, width = root_rhs.shape[2], root_rhs.shape[3]
    blk = leaf_rhs.shape[3]
    owners = parent.reshape(-1)
    place = jnp.stack([lax.axis_index("slab"), lax.axis_index("front")]).astype(jnp.int32)
    pairs = fronts // 2
    masks = range(1, slabs)

    def start_forward(h, after):
        fwd, keep, send = forward(h, owners, place, leaf_rhs, leaf_inv, leaf_off, ancestors, fronts, rows, after)
        return fwd, keep, crossed(send, "front", 1)

    def send_far(keep, near, after):
        sums = total(keep, near, after)
        return sums, [crossed(value, "front", 2 * (j + 1)) for j, value in enumerate(sums)]

    def over_slabs(values):
        return [values[0]] + [crossed(values[mask], "slab", mask) for mask in masks]

    def share(own):
        mine = [own] + [crossed(own, "front", 2 * j) for j in range(1, pairs)]
        return [value for field in mine for value in (field, crossed(field, "front", 1))]

    fwd0, keep0, near0 = start_forward(0, ())
    sums0, far0 = send_far(keep0, near0, ())
    same, other = pack(place, root_inv, coupling, [sums0[0]])
    mats = [same] + [crossed((same, other)[mask % 2], "slab", mask) for mask in masks]
    fwd1, keep1, near1 = start_forward(1, [same])
    folded = fold(leaf_inv, leaf_off, ancestors, rows, [fwd1])
    sums1, far1 = send_far(keep1, near1, [folded])
    pieces0 = reduce(0, place, root_rhs, keep0, near0, far0, slabs, blk, [sums1[0]])
    solved0 = chain(place, over_slabs(pieces0), mats, ())
    pieces1 = reduce(1, place, root_rhs, keep1, near1, far1, slabs, blk, [solved0[0]])
    own0, root_sol = collect(0, place, over_slabs(solved0), None, rows, width, [pieces1[0]])
    solved1 = chain(place, over_slabs(pieces1), mats, [own0])
    fields0 = share(own0)
    own1, root_sol = collect(1, place, over_slabs(solved1), root_sol, rows, width, ())
    fields1 = share(own1)
    leaf_sol = backward(0, owners, place, fwd0, folded, fields0, None, width, [own1])
    leaf_sol = backward(1, owners, place, fwd1, folded, fields1, leaf_sol, width, ())
    return leaf_sol, root_sol


def solution(mesh):
    in_specs = (
        P("slab", None, "front", None, None),
        P("slab", "front", None, None, None),
        P("slab", "front", None, None, None),
        P("slab", "front", None),
        P("slab", "front", None),
        P("slab", None, "front", None),
        P("slab", "front", None, None, None),
        P("slab", "front"),
    )
    out_specs = (P("slab", None, "front", None, None), P("slab", None, "front", None))
    return jax.shard_map(body, mesh=mesh, in_specs=in_specs, out_specs=out_specs, check_vma=False)
```

```python
import functools

import jax
import jax.numpy as jnp
from jax import lax
from jax.experimental import pallas as pl
from jax.experimental.pallas import tpu as pltpu
from jax.sharding import PartitionSpec as P

HALVES = 2
BF = jnp.bfloat16
F32 = jnp.float32
VMEM = pl.BlockSpec(memory_space=pltpu.VMEM)
SMEM = pl.BlockSpec(memory_space=pltpu.SMEM)
HBM = pl.BlockSpec(memory_space=pltpu.HBM)
ANY = pl.BlockSpec(memory_space=pl.ANY)


def shape_of(shape, dtype=BF):
    return jax.ShapeDtypeStruct(shape, dtype)


def call(kernel, name, ins, in_specs, outs, out_specs, after=(), scratch=(), aliases=None, room=24):
    count, extra = len(ins), len(after)

    def wrapped(*refs):
        kernel(*refs[:count], *refs[count + extra :])

    return pl.pallas_call(
        wrapped,
        in_specs=list(in_specs) + [ANY] * extra,
        out_specs=out_specs,
        out_shape=outs,
        scratch_shapes=list(scratch),
        input_output_aliases=aliases or {},
        compiler_params=pltpu.CompilerParams(vmem_limit_bytes=room * 1024 * 1024),
        cost_estimate=pl.CostEstimate(flops=1, bytes_accessed=1, transcendentals=0),
        name=name,
    )(*ins, *after)


def crossed(x, axis, mask):
    return lax.ppermute(x, axis, [(i, i ^ mask) for i in range(lax.axis_size(axis))])


def stacked(real, imag):
    return jnp.concatenate(
        [jnp.concatenate([real, -imag], axis=1), jnp.concatenate([imag, real], axis=1)], axis=0
    )


def dot(a, b, dims=((1,), (0,)), precision=None):
    return lax.dot_general(a, b, (dims, ((), ())), precision=precision, preferred_element_type=F32)


def table_of(anc_row, rows):
    ids = lax.broadcasted_iota(jnp.int32, (rows, anc_row.shape[1]), 0)
    return (ids == anc_row).astype(F32).astype(BF)


def forward_kernel(h, group, cap, owners, place, rhs, inv, off, anc, fwd, keep, send,
                   vecs, invs, offs, ancs, part, ids, seen, sems):
    leaves, blk, cols = vecs.shape[1], vecs.shape[2], vecs.shape[3]
    fronts, rows, width = part.shape[0], keep.shape[3], keep.shape[4]
    me = place[1]
    small = pltpu.make_async_copy(anc.at[0], ancs, sems.at[leaves // group, 0])

    def copies(at):
        span = pl.ds(at * group, group)
        return (
            pltpu.make_async_copy(inv.at[0, span], invs.at[span], sems.at[at, 0]),
            pltpu.make_async_copy(rhs.at[0, :, span, :, pl.ds(h * cols, cols)], vecs.at[:, span], sems.at[at, 1]),
            pltpu.make_async_copy(off.at[0, span], offs.at[span], sems.at[at, 2]),
        )

    for at in range(leaves // group):
        for copy in copies(at):
            copy.start()
    small.start()
    ids[...] = jnp.full(ids.shape, -1, jnp.int32)
    for dist in range(fronts):
        seen[dist] = 0
    small.wait()

    def some(at, carry):
        for copy in copies(at):
            copy.wait()
        names = [at * group + j for j in range(group)]
        values = []
        for leaf in names:
            vec = jnp.concatenate([vecs[0, leaf], vecs[1, leaf]], axis=0)
            values.append(dot(stacked(invs[leaf, 0], invs[leaf, 1]), vec).astype(BF))
        moved = [dot(stacked(offs[leaf, 0], offs[leaf, 1]), value).astype(BF) for leaf, value in zip(names, values)]
        for leaf, value, shift in zip(names, values, moved):
            fwd[leaf] = value
            dist = owners[leaf] ^ me
            rank = seen[dist]
            seen[dist] = rank + 1
            part[dist, 0, rank] = shift[:blk]
            part[dist, 1, rank] = shift[blk:]
            ids[pl.ds(dist * cap + rank, 1), :] = ancs[pl.ds(leaf, 1), :]
        return carry

    lax.fori_loop(0, leaves // group, some, 0)
    for dist in range(fronts):
        for rank in range(cap):

            @pl.when(seen[dist] <= rank)
            def _(dist=dist, rank=rank):
                part[dist, 0, rank] = jnp.zeros((blk, cols), BF)
                part[dist, 1, rank] = jnp.zeros((blk, cols), BF)

    for dist in range(fronts):
        row = jnp.concatenate([ids[dist * cap + rank : dist * cap + rank + 1, :] for rank in range(cap)], axis=1)
        table = table_of(row, rows)
        out = send if dist % 2 else keep
        for plane in range(2):
            value = dot(table, part[dist, plane].reshape(cap * blk, cols)).astype(BF)
            for q in range(cols // width):
                out[dist // 2, q, plane] = value[:, q * width : (q + 1) * width]


def forward(h, owners, place, leaf_rhs, leaf_inv, leaf_off, ancestors, fronts, rows, part, after):
    _, _, leaves, blk, width = leaf_rhs.shape
    cols = width // HALVES
    cap = -(-leaves // fronts)
    group = 4
    block = shape_of((fronts // 2, cols // part, 2, rows, part))
    return call(
        functools.partial(forward_kernel, h, group, cap),
        "leaf_forward",
        [owners, place, leaf_rhs, leaf_inv, leaf_off, ancestors],
        [SMEM, SMEM, HBM, HBM, HBM, HBM],
        [shape_of((leaves, 2 * blk, cols)), block, block],
        [VMEM, VMEM, VMEM],
        after,
        [
            pltpu.VMEM((2, leaves, blk, cols), BF),
            pltpu.VMEM((leaves, 2, blk, blk), BF),
            pltpu.VMEM((leaves, 2, blk, blk), BF),
            pltpu.VMEM((leaves, blk), jnp.int32),
            pltpu.VMEM((fronts, 2, cap, blk, cols), BF),
            pltpu.VMEM((fronts * cap, blk), jnp.int32),
            pltpu.SMEM((fronts,), jnp.int32),
            pltpu.SemaphoreType.DMA((leaves // group + 1, 3)),
        ],
        room=50,
    )


def fold_kernel(inv, off, anc, out):
    leaves, _, blk, _ = inv.shape[1:]
    rows = out.shape[2] // 2

    def one(leaf, carry):
        mat = jnp.concatenate([inv[0, leaf, 0], inv[0, leaf, 1]], axis=1)
        real, imag = off[0, leaf, 0], off[0, leaf, 1]
        other = jnp.concatenate([jnp.concatenate([real, -imag], axis=1), jnp.concatenate([imag, real], axis=1)], axis=0)
        both = dot(mat, other, ((1,), (1,))).astype(BF)
        table = table_of(anc[0, pl.ds(leaf, 1), :], rows)
        real = dot(both[:, :blk], table, ((1,), (1,))).astype(BF)
        imag = dot(both[:, blk:], table, ((1,), (1,))).astype(BF)
        out[leaf, :blk, :rows] = real
        out[leaf, :blk, rows:] = -imag
        out[leaf, blk:, :rows] = imag
        out[leaf, blk:, rows:] = real
        return carry

    lax.fori_loop(0, leaves, one, 0, unroll=2)


def fold(leaf_inv, leaf_off, ancestors, rows, after):
    _, leaves, _, blk, _ = leaf_inv.shape
    return call(
        fold_kernel, "leaf_fold", [leaf_inv, leaf_off, ancestors], [VMEM] * 3,
        shape_of((leaves, 2 * blk, 2 * rows)), VMEM, after,
    )


def pack_kernel(place, inv, cpl, same, other):
    blocks, blk = inv.shape[1], inv.shape[3]
    for kind, out in enumerate((same, other)):
        block = (place[0] % blocks) ^ kind
        out[:blk] = inv[0, block, 0].astype(BF)
        out[blk : 2 * blk] = inv[0, block, 1].astype(BF)
        rest = jnp.broadcast_to(cpl[0, pl.ds(block, 1), :], (16, blk))
        row = lax.broadcasted_iota(jnp.int32, (16, blk), 0)
        value = jnp.zeros((16, blk), F32)
        for term in range(3):
            piece = rest.astype(BF).astype(F32)
            value = jnp.where(row == term, piece, value)
            rest = rest - piece
        out[2 * blk :] = value.astype(BF)


def pack(place, root_inv, coupling, after):
    _, blocks, _, blk, _ = root_inv.shape
    shape = shape_of((2 * blk + 16, blk))
    return call(
        pack_kernel, "solve_pack", [place, root_inv, coupling.reshape(1, blocks, blk)], [SMEM, VMEM, VMEM],
        [shape, shape], [VMEM, VMEM], after,
    )


def join_kernel(*refs):
    *parts, out = refs
    at = 0
    for ref in parts:
        out[at : at + ref.shape[0]] = ref[...]
        at += ref.shape[0]


def join(parts, after):
    rows = sum(part.shape[0] for part in parts)
    return call(
        join_kernel, "solve_join", parts, [VMEM] * len(parts), shape_of((rows,) + parts[0].shape[1:]), VMEM, after
    )


def first_kernel(names, keep, near, *outs):
    for (j, first, last), out in zip(names, outs):
        out[...] = (keep[j, first:last].astype(F32) + near[j, first:last].astype(F32)).astype(BF)


def first_sums(names, keep, near, after):
    return call(
        functools.partial(first_kernel, names), "interface_first", [keep, near], [VMEM, VMEM],
        [shape_of((last - first,) + keep.shape[2:]) for _, first, last in names], [VMEM] * len(names), after,
    )


def second_kernel(half, keep, near, by_x, by_y, out_x, out_y):
    parts = keep.shape[1]
    for j, out, extra, first, last in ((1, out_x, by_y, half, parts), (2, out_y, by_x, 0, half)):
        for q in range(parts):
            value = keep[j, q].astype(F32) + near[j, q].astype(F32)
            if first <= q < last:
                value = value + extra[q - first].astype(F32)
            out[q] = value.astype(BF)


def second_sums(half, keep, near, by_x, by_y, after):
    shape = shape_of(keep.shape[1:])
    return call(
        functools.partial(second_kernel, half), "interface_second", [keep, near, by_x, by_y], [VMEM] * 4,
        [shape, shape], [VMEM] * 2, after,
    )


def piece_of(index, blk, blocks):
    low = (index % blocks) * blk
    return index // blocks, slice(low, low + blk)


def reduce_kernel(h, slabs, blk, terms, place, rhs, keep, near, *refs):
    _, parts, _, rows, part = keep.shape
    outs = refs[terms:]
    for index in range(slabs):
        q, span = piece_of(index, blk, rows // blk)
        left = h * parts * part + q * part
        field = []
        for plane in range(2):
            value = keep[0, q, plane, span].astype(F32) + near[0, q, plane, span].astype(F32)
            for ref in refs[:terms]:
                value = value + ref[q, plane, span].astype(F32)
            field.append((rhs[0, plane, span, left : left + part].astype(F32) - value).astype(BF))
        for mask, out in enumerate(outs):

            @pl.when(place[0] ^ mask == index)
            def _(field=field, out=out):
                out[0] = field[0]
                out[1] = field[1]


def reduce(h, place, root_rhs, keep, near, far, slabs, blk, after):
    part = keep.shape[4]
    return call(
        functools.partial(reduce_kernel, h, slabs, blk, len(far)), "interface_reduce",
        [place, root_rhs, keep, near, *far], [SMEM] + [VMEM] * (3 + len(far)),
        [shape_of((2, blk, part))] * slabs, [VMEM] * slabs, after,
    )


def chain_kernel(slabs, count, place, *refs):
    pieces, mats, outs = refs[:slabs], refs[slabs : slabs + count], refs[slabs + count : 2 * slabs + count]
    held, solver = refs[2 * slabs + count :]
    me = place[0]
    for mask in range(slabs):
        held[mask] = pieces[mask][...]
    _, _, blk, part = held.shape
    tall = solver.shape[1]
    at = 0
    for mat in mats:
        for k in range(mat.shape[0] // tall):
            solver[at] = mat[k * tall : (k + 1) * tall]
            at += 1
    state = None
    for slab in range(slabs):
        at = me ^ slab
        field = held[at].reshape(2 * blk, part).astype(F32)
        packed = solver[at]
        if state is not None:
            terms = packed[2 * blk :].astype(F32)
            row = terms[0:1] + terms[1:2] + terms[2:3]
            scale = jnp.broadcast_to(row, (blk, blk)).T[:, :1]
            field = field - jnp.concatenate([scale, scale], axis=0) * state
        mat = stacked(packed[:blk], packed[blk : 2 * blk])
        high = field.astype(BF)
        state = dot(mat, high)
        if slab:
            state = state + dot(mat, (field - high.astype(F32)).astype(BF))
        half = state.astype(BF)
        for mask, out in enumerate(outs):

            @pl.when(at == mask)
            def _(half=half, out=out):
                out[0] = half[:blk]
                out[1] = half[blk:]


def chain(place, pieces, mats, after):
    slabs = len(pieces)
    tall = mats[0].shape
    return call(
        functools.partial(chain_kernel, slabs, len(mats)), "sweep_chain", [place, *pieces, *mats],
        [SMEM] + [VMEM] * (slabs + len(mats)),
        [shape_of(pieces[0].shape)] * slabs, [VMEM] * slabs, after,
        [pltpu.VMEM((slabs,) + pieces[0].shape, BF), pltpu.VMEM((slabs,) + tall, BF)],
    )


def collect_kernel(h, slabs, aliased, place, *refs):
    pieces = refs[:slabs]
    own, root, full, sem = refs[slabs + aliased :]
    _, blk, part = pieces[0].shape
    parts, _, rows, _ = own.shape
    cols = parts * part
    for mask, piece in enumerate(pieces):
        for index in range(slabs):
            q, span = piece_of(index, blk, rows // blk)

            @pl.when(place[0] ^ mask == index)
            def _(piece=piece, q=q, span=span):
                for plane in range(2):
                    own[q, plane, span] = piece[plane]
                    full[plane, span, q * part : (q + 1) * part] = piece[plane].astype(F32)

    copy = pltpu.make_async_copy(full, root.at[0, :, :, pl.ds(h * cols, cols)], sem)
    copy.start()
    copy.wait()


def collect(h, place, pieces, before, rows, width, after):
    slabs = len(pieces)
    cols = width // HALVES
    part = pieces[0].shape[2]
    aliased = [] if before is None else [before]
    return call(
        functools.partial(collect_kernel, h, slabs, len(aliased)), "interface_collect",
        [place, *pieces, *aliased], [SMEM] + [VMEM] * slabs + [HBM] * len(aliased),
        [shape_of((cols // part, 2, rows, part)), shape_of((1, 2, rows, width), F32)], [VMEM, HBM], after,
        [pltpu.VMEM((2, rows, cols), F32), pltpu.SemaphoreType.DMA],
        {1 + slabs: 1} if aliased else None,
    )


def backward_kernel(h, counts, cap, aliased, owners, place, fwd, mats, *refs):
    fronts = len(counts)
    fields = refs[: sum(counts)]
    out, held, slots, sems = refs[sum(counts) + aliased :]
    leaves, wide, cols = fwd.shape
    blk = wide // 2
    tall = mats.shape[2]
    for dist in range(fronts):
        for rank in range(cap):
            slots[dist * cap + rank] = -1
    for leaf in range(leaves):
        first = (owners[leaf] ^ place[1]) * cap
        spot = first
        for rank in range(cap - 1):
            spot = jnp.where(slots[first + rank] >= 0, first + rank + 1, spot)
        slots[spot] = leaf

    def copy_of(leaf):
        return pltpu.make_async_copy(held.at[leaf], out.at[0, :, leaf, :, pl.ds(h * cols, cols)], sems.at[leaf])

    for dist in range(fronts):
        mine, fields = fields[: counts[dist]], fields[counts[dist] :]
        columns = [ref[q].reshape(tall, ref.shape[3]) for ref in mine for q in range(ref.shape[0])]
        field = jnp.concatenate(columns, axis=1)
        for rank in range(cap):
            name = slots[dist * cap + rank]

            @pl.when(name >= 0)
            def _(name=name, field=field):
                result = fwd[name].astype(F32) - dot(mats[name], field)
                held[name, 0] = result[:blk].astype(BF)
                held[name, 1] = result[blk:].astype(BF)
                copy_of(name).start()

    for leaf in range(leaves):
        copy_of(leaf).wait()


def backward(h, owners, place, fwd, mats, fields, before, width, after):
    leaves, wide, cols = fwd.shape
    blk, fronts = wide // 2, len(fields)
    cap = -(-leaves // fronts)
    counts = [len(field) for field in fields]
    flat = [part for field in fields for part in field]
    aliased = [] if before is None else [before]
    return call(
        functools.partial(backward_kernel, h, counts, cap, len(aliased)), "leaf_backward",
        [owners, place, fwd, mats, *flat, *aliased], [SMEM, SMEM] + [VMEM] * (2 + len(flat)) + [HBM] * len(aliased),
        shape_of((1, 2, leaves, blk, width)), HBM, after,
        [
            pltpu.VMEM((leaves, 2, blk, cols), BF),
            pltpu.SMEM((fronts * cap,), jnp.int32),
            pltpu.SemaphoreType.DMA((leaves,)),
        ],
        {4 + len(flat): 0} if aliased else None,
    )


def body(leaf_rhs, leaf_inv, leaf_off, parent, ancestors, root_rhs, root_inv, coupling):
    fronts, slabs = lax.axis_size("front"), lax.axis_size("slab")
    rows, width = root_rhs.shape[2], root_rhs.shape[3]
    blk = leaf_rhs.shape[3]
    owners = parent.reshape(-1)
    place = jnp.stack([lax.axis_index("slab"), lax.axis_index("front")]).astype(jnp.int32)
    pairs = fronts // 2
    parts = slabs // (rows // blk)
    part = width // HALVES // parts
    square = pairs == 4

    def start_forward(h, after):
        fwd, keep, send = forward(
            h, owners, place, leaf_rhs, leaf_inv, leaf_off, ancestors, fronts, rows, part, after
        )
        return fwd, keep, crossed(send, "front", 1)

    def send_first(keep, near, after):
        if not square:
            sums = first_sums([(j, 0, parts) for j in range(1, pairs)], keep, near, after)
            return sums[0], [crossed(value, "front", 2 * (j + 1)) for j, value in enumerate(sums)]
        to_x, to_y = first_sums([(3, 0, parts // 2), (3, parts // 2, parts)], keep, near, after)
        return to_x, [crossed(to_x, "front", 2), crossed(to_y, "front", 4)]

    def send_second(keep, near, got, after):
        if not square:
            return got[0], got
        to_x, to_y = second_sums(parts // 2, keep, near, *got, after)
        return to_x, [crossed(to_x, "front", 2), crossed(to_y, "front", 4)]

    def over_slabs(values):
        return [values[0]] + [crossed(values[mask], "slab", mask) for mask in range(1, slabs)]

    def share(own):
        if square:
            by_x, by_y = crossed(own, "front", 2), crossed(own, "front", 4)
            far = [crossed(by_x[: parts // 2], "front", 4), crossed(by_y[parts // 2 :], "front", 2)]
            mine = [[own], [by_x], [by_y], far]
        else:
            mine = [[own]] + [[crossed(own, "front", 2 * j)] for j in range(1, pairs)]
        return [field for group in mine for field in (group, [crossed(value, "front", 1) for value in group])]

    fwd0, keep0, near0 = start_forward(0, ())
    same, other = pack(place, root_inv, coupling, [fwd0])
    have = [same, crossed(other, "slab", 1)]
    token, got0 = send_first(keep0, near0, [same])
    fwd1, keep1, near1 = start_forward(1, [token])
    token, far0 = send_second(keep0, near0, got0, [fwd1])
    step = 2
    while step < slabs:
        joined = join(have, [token])
        have = have + [crossed(joined, "slab", step)]
        step *= 2
        token = joined
    token, got1 = send_first(keep1, near1, [token])
    folded = fold(leaf_inv, leaf_off, ancestors, rows, [token])
    pieces0 = reduce(0, place, root_rhs, keep0, near0, far0, slabs, blk, [folded])
    token, far1 = send_second(keep1, near1, got1, [pieces0[0]])
    solved0 = chain(place, over_slabs(pieces0), have, [token])
    pieces1 = reduce(1, place, root_rhs, keep1, near1, far1, slabs, blk, [solved0[0]])
    own0, root_sol = collect(0, place, over_slabs(solved0), None, rows, width, [pieces1[0]])
    solved1 = chain(place, over_slabs(pieces1), have, [own0])
    fields0 = share(own0)
    own1, root_sol = collect(1, place, over_slabs(solved1), root_sol, rows, width, ())
    fields1 = share(own1)
    leaf_sol = backward(0, owners, place, fwd0, folded, fields0, None, width, [own1])
    leaf_sol = backward(1, owners, place, fwd1, folded, fields1, leaf_sol, width, ())
    return leaf_sol, root_sol


def solution(mesh):
    in_specs = (
        P("slab", None, "front", None, None),
        P("slab", "front", None, None, None),
        P("slab", "front", None, None, None),
        P("slab", "front", None),
        P("slab", "front", None),
        P("slab", None, "front", None),
        P("slab", "front", None, None, None),
        P("slab", "front"),
    )
    out_specs = (P("slab", None, "front", None, None), P("slab", None, "front", None))
    return jax.shard_map(body, mesh=mesh, in_specs=in_specs, out_specs=out_specs, check_vma=False)
```

```python
import functools

import jax
import jax.numpy as jnp
from jax import lax
from jax.experimental import pallas as pl
from jax.experimental.pallas import tpu as pltpu
from jax.sharding import PartitionSpec as P

HALVES = 2
BF = jnp.bfloat16
F32 = jnp.float32
VMEM = pl.BlockSpec(memory_space=pltpu.VMEM)
SMEM = pl.BlockSpec(memory_space=pltpu.SMEM)
HBM = pl.BlockSpec(memory_space=pltpu.HBM)
ANY = pl.BlockSpec(memory_space=pl.ANY)


def shape_of(shape, dtype=BF):
    return jax.ShapeDtypeStruct(shape, dtype)


def call(kernel, name, ins, in_specs, outs, out_specs, after=(), scratch=(), aliases=None, room=24):
    count, extra = len(ins), len(after)

    def wrapped(*refs):
        kernel(*refs[:count], *refs[count + extra :])

    return pl.pallas_call(
        wrapped,
        in_specs=list(in_specs) + [ANY] * extra,
        out_specs=out_specs,
        out_shape=outs,
        scratch_shapes=list(scratch),
        input_output_aliases=aliases or {},
        compiler_params=pltpu.CompilerParams(vmem_limit_bytes=room * 1024 * 1024),
        cost_estimate=pl.CostEstimate(flops=10**10, bytes_accessed=1, transcendentals=0),
        name=name,
    )(*ins, *after)


def crossed(x, axis, mask):
    return lax.ppermute(x, axis, [(i, i ^ mask) for i in range(lax.axis_size(axis))])


def stacked(real, imag):
    return jnp.concatenate(
        [jnp.concatenate([real, -imag], axis=1), jnp.concatenate([imag, real], axis=1)], axis=0
    )


def dot(a, b, dims=((1,), (0,)), precision=None):
    return lax.dot_general(a, b, (dims, ((), ())), precision=precision, preferred_element_type=F32)


def table_of(anc_row, rows):
    ids = lax.broadcasted_iota(jnp.int32, (rows, anc_row.shape[1]), 0)
    return (ids == anc_row).astype(F32).astype(BF)


def forward_kernel(h, group, cap, owners, place, rhs, inv, off, anc, fwd, keep, send,
                   vecs, invs, offs, ancs, part, ids, seen, sems):
    leaves, blk, cols = vecs.shape[1], vecs.shape[2], vecs.shape[3]
    fronts, rows, width = part.shape[0], keep.shape[3], keep.shape[4]
    me = place[1]
    small = pltpu.make_async_copy(anc.at[0], ancs, sems.at[leaves // group, 0])

    def copies(at):
        span = pl.ds(at * group, group)
        return (
            pltpu.make_async_copy(inv.at[0, span], invs.at[span], sems.at[at, 0]),
            pltpu.make_async_copy(rhs.at[0, :, span, :, pl.ds(h * cols, cols)], vecs.at[:, span], sems.at[at, 1]),
            pltpu.make_async_copy(off.at[0, span], offs.at[span], sems.at[at, 2]),
        )

    for at in range(leaves // group):
        for copy in copies(at):
            copy.start()
    small.start()
    ids[...] = jnp.full(ids.shape, -1, jnp.int32)
    for dist in range(fronts):
        seen[dist] = 0
    small.wait()

    def some(at, carry):
        for copy in copies(at):
            copy.wait()
        names = [at * group + j for j in range(group)]
        values = []
        for leaf in names:
            vec = jnp.concatenate([vecs[0, leaf], vecs[1, leaf]], axis=0)
            values.append(dot(stacked(invs[leaf, 0], invs[leaf, 1]), vec).astype(BF))
        moved = [dot(stacked(offs[leaf, 0], offs[leaf, 1]), value).astype(BF) for leaf, value in zip(names, values)]
        for leaf, value, shift in zip(names, values, moved):
            fwd[leaf] = value
            dist = owners[leaf] ^ me
            rank = seen[dist]
            seen[dist] = rank + 1
            part[dist, 0, rank] = shift[:blk]
            part[dist, 1, rank] = shift[blk:]
            ids[pl.ds(dist * cap + rank, 1), :] = ancs[pl.ds(leaf, 1), :]
        return carry

    lax.fori_loop(0, leaves // group, some, 0)
    for dist in range(fronts):
        for rank in range(cap):

            @pl.when(seen[dist] <= rank)
            def _(dist=dist, rank=rank):
                part[dist, 0, rank] = jnp.zeros((blk, cols), BF)
                part[dist, 1, rank] = jnp.zeros((blk, cols), BF)

    for dist in range(fronts):
        row = jnp.concatenate([ids[dist * cap + rank : dist * cap + rank + 1, :] for rank in range(cap)], axis=1)
        table = table_of(row, rows)
        out = send if dist % 2 else keep
        for plane in range(2):
            value = dot(table, part[dist, plane].reshape(cap * blk, cols)).astype(BF)
            for q in range(cols // width):
                out[dist // 2, q, plane] = value[:, q * width : (q + 1) * width]


def forward(h, owners, place, leaf_rhs, leaf_inv, leaf_off, ancestors, fronts, rows, part, after):
    _, _, leaves, blk, width = leaf_rhs.shape
    cols = width // HALVES
    cap = -(-leaves // fronts)
    group = 4
    block = shape_of((fronts // 2, cols // part, 2, rows, part))
    return call(
        functools.partial(forward_kernel, h, group, cap),
        "leaf_forward",
        [owners, place, leaf_rhs, leaf_inv, leaf_off, ancestors],
        [SMEM, SMEM, HBM, HBM, HBM, HBM],
        [shape_of((leaves, 2 * blk, cols)), block, block],
        [VMEM, VMEM, VMEM],
        after,
        [
            pltpu.VMEM((2, leaves, blk, cols), BF),
            pltpu.VMEM((leaves, 2, blk, blk), BF),
            pltpu.VMEM((leaves, 2, blk, blk), BF),
            pltpu.VMEM((leaves, blk), jnp.int32),
            pltpu.VMEM((fronts, 2, cap, blk, cols), BF),
            pltpu.VMEM((fronts * cap, blk), jnp.int32),
            pltpu.SMEM((fronts,), jnp.int32),
            pltpu.SemaphoreType.DMA((leaves // group + 1, 3)),
        ],
        room=50,
    )


def fold_kernel(inv, off, anc, out):
    leaves, _, blk, _ = inv.shape[1:]
    rows = out.shape[2] // 2

    def one(leaf, carry):
        mat = jnp.concatenate([inv[0, leaf, 0], inv[0, leaf, 1]], axis=1)
        real, imag = off[0, leaf, 0], off[0, leaf, 1]
        other = jnp.concatenate([jnp.concatenate([real, -imag], axis=1), jnp.concatenate([imag, real], axis=1)], axis=0)
        both = dot(mat, other, ((1,), (1,))).astype(BF)
        table = table_of(anc[0, pl.ds(leaf, 1), :], rows)
        real = dot(both[:, :blk], table, ((1,), (1,))).astype(BF)
        imag = dot(both[:, blk:], table, ((1,), (1,))).astype(BF)
        out[leaf, :blk, :rows] = real
        out[leaf, :blk, rows:] = -imag
        out[leaf, blk:, :rows] = imag
        out[leaf, blk:, rows:] = real
        return carry

    lax.fori_loop(0, leaves, one, 0, unroll=2)


def fold(leaf_inv, leaf_off, ancestors, rows, after):
    _, leaves, _, blk, _ = leaf_inv.shape
    return call(
        fold_kernel, "leaf_fold", [leaf_inv, leaf_off, ancestors], [VMEM] * 3,
        shape_of((leaves, 2 * blk, 2 * rows)), VMEM, after,
    )


def pack_kernel(place, inv, cpl, same, other):
    blocks, blk = inv.shape[1], inv.shape[3]
    for kind, out in enumerate((same, other)):
        block = (place[0] % blocks) ^ kind
        out[:blk] = inv[0, block, 0].astype(BF)
        out[blk : 2 * blk] = inv[0, block, 1].astype(BF)
        rest = jnp.broadcast_to(cpl[0, pl.ds(block, 1), :], (16, blk))
        row = lax.broadcasted_iota(jnp.int32, (16, blk), 0)
        value = jnp.zeros((16, blk), F32)
        for term in range(3):
            piece = rest.astype(BF).astype(F32)
            value = jnp.where(row == term, piece, value)
            rest = rest - piece
        out[2 * blk :] = value.astype(BF)


def pack(place, root_inv, coupling, after):
    _, blocks, _, blk, _ = root_inv.shape
    shape = shape_of((2 * blk + 16, blk))
    return call(
        pack_kernel, "solve_pack", [place, root_inv, coupling.reshape(1, blocks, blk)], [SMEM, VMEM, VMEM],
        [shape, shape], [VMEM, VMEM], after,
    )


def join_kernel(*refs):
    *parts, out = refs
    at = 0
    for ref in parts:
        out[at : at + ref.shape[0]] = ref[...]
        at += ref.shape[0]


def join(parts, after):
    rows = sum(part.shape[0] for part in parts)
    return call(
        join_kernel, "solve_join", parts, [VMEM] * len(parts), shape_of((rows,) + parts[0].shape[1:]), VMEM, after
    )


def first_kernel(names, keep, near, *outs):
    for (j, first, last), out in zip(names, outs):
        out[...] = (keep[j, first:last].astype(F32) + near[j, first:last].astype(F32)).astype(BF)


def first_sums(names, keep, near, after):
    return call(
        functools.partial(first_kernel, names), "interface_first", [keep, near], [VMEM, VMEM],
        [shape_of((last - first,) + keep.shape[2:]) for _, first, last in names], [VMEM] * len(names), after,
    )


def second_kernel(half, keep, near, by_x, by_y, out_x, out_y):
    parts = keep.shape[1]
    for j, out, extra, first, last in ((1, out_x, by_y, half, parts), (2, out_y, by_x, 0, half)):
        for q in range(parts):
            value = keep[j, q].astype(F32) + near[j, q].astype(F32)
            if first <= q < last:
                value = value + extra[q - first].astype(F32)
            out[q] = value.astype(BF)


def second_sums(half, keep, near, by_x, by_y, after):
    shape = shape_of(keep.shape[1:])
    return call(
        functools.partial(second_kernel, half), "interface_second", [keep, near, by_x, by_y], [VMEM] * 4,
        [shape, shape], [VMEM] * 2, after,
    )


def piece_of(index, blk, blocks):
    low = (index % blocks) * blk
    return index // blocks, slice(low, low + blk)


def reduce_kernel(h, slabs, blk, terms, place, rhs, keep, near, *refs):
    _, parts, _, rows, part = keep.shape
    outs = refs[terms:]
    for index in range(slabs):
        q, span = piece_of(index, blk, rows // blk)
        left = h * parts * part + q * part
        field = []
        for plane in range(2):
            value = keep[0, q, plane, span].astype(F32) + near[0, q, plane, span].astype(F32)
            for ref in refs[:terms]:
                value = value + ref[q, plane, span].astype(F32)
            field.append((rhs[0, plane, span, left : left + part].astype(F32) - value).astype(BF))
        for mask, out in enumerate(outs):

            @pl.when(place[0] ^ mask == index)
            def _(field=field, out=out):
                out[0] = field[0]
                out[1] = field[1]


def reduce(h, place, root_rhs, keep, near, far, slabs, blk, after):
    part = keep.shape[4]
    return call(
        functools.partial(reduce_kernel, h, slabs, blk, len(far)), "interface_reduce",
        [place, root_rhs, keep, near, *far], [SMEM] + [VMEM] * (3 + len(far)),
        [shape_of((2, blk, part))] * slabs, [VMEM] * slabs, after,
    )


def chain_kernel(slabs, count, place, *refs):
    pieces, mats, outs = refs[:slabs], refs[slabs : slabs + count], refs[slabs + count : 2 * slabs + count]
    held, solver = refs[2 * slabs + count :]
    me = place[0]
    for mask in range(slabs):
        held[mask] = pieces[mask][...]
    _, _, blk, part = held.shape
    tall = solver.shape[1]
    at = 0
    for mat in mats:
        for k in range(mat.shape[0] // tall):
            solver[at] = mat[k * tall : (k + 1) * tall]
            at += 1
    state = None
    for slab in range(slabs):
        at = me ^ slab
        field = held[at].reshape(2 * blk, part).astype(F32)
        packed = solver[at]
        if state is not None:
            terms = packed[2 * blk :].astype(F32)
            row = terms[0:1] + terms[1:2] + terms[2:3]
            scale = jnp.broadcast_to(row, (blk, blk)).T[:, :1]
            field = field - jnp.concatenate([scale, scale], axis=0) * state
        mat = stacked(packed[:blk], packed[blk : 2 * blk])
        high = field.astype(BF)
        state = dot(mat, high)
        if slab:
            state = state + dot(mat, (field - high.astype(F32)).astype(BF))
        half = state.astype(BF)
        for mask, out in enumerate(outs):

            @pl.when(at == mask)
            def _(half=half, out=out):
                out[0] = half[:blk]
                out[1] = half[blk:]


def chain(place, pieces, mats, after):
    slabs = len(pieces)
    tall = mats[0].shape
    return call(
        functools.partial(chain_kernel, slabs, len(mats)), "sweep_chain", [place, *pieces, *mats],
        [SMEM] + [VMEM] * (slabs + len(mats)),
        [shape_of(pieces[0].shape)] * slabs, [VMEM] * slabs, after,
        [pltpu.VMEM((slabs,) + pieces[0].shape, BF), pltpu.VMEM((slabs,) + tall, BF)],
    )


def collect_kernel(h, slabs, aliased, place, *refs):
    pieces = refs[:slabs]
    own, root, full, sem = refs[slabs + aliased :]
    _, blk, part = pieces[0].shape
    parts, _, rows, _ = own.shape
    cols = parts * part
    for mask, piece in enumerate(pieces):
        for index in range(slabs):
            q, span = piece_of(index, blk, rows // blk)

            @pl.when(place[0] ^ mask == index)
            def _(piece=piece, q=q, span=span):
                for plane in range(2):
                    own[q, plane, span] = piece[plane]
                    full[plane, span, q * part : (q + 1) * part] = piece[plane].astype(F32)

    copy = pltpu.make_async_copy(full, root.at[0, :, :, pl.ds(h * cols, cols)], sem)
    copy.start()
    copy.wait()


def collect(h, place, pieces, before, rows, width, after):
    slabs = len(pieces)
    cols = width // HALVES
    part = pieces[0].shape[2]
    aliased = [] if before is None else [before]
    return call(
        functools.partial(collect_kernel, h, slabs, len(aliased)), "interface_collect",
        [place, *pieces, *aliased], [SMEM] + [VMEM] * slabs + [HBM] * len(aliased),
        [shape_of((cols // part, 2, rows, part)), shape_of((1, 2, rows, width), F32)], [VMEM, HBM], after,
        [pltpu.VMEM((2, rows, cols), F32), pltpu.SemaphoreType.DMA],
        {1 + slabs: 1} if aliased else None,
    )


def backward_kernel(h, counts, cap, aliased, owners, place, fwd, mats, *refs):
    fronts = len(counts)
    fields = refs[: sum(counts)]
    out, held, slots, sems = refs[sum(counts) + aliased :]
    leaves, wide, cols = fwd.shape
    blk = wide // 2
    tall = mats.shape[2]
    for dist in range(fronts):
        for rank in range(cap):
            slots[dist * cap + rank] = -1
    for leaf in range(leaves):
        first = (owners[leaf] ^ place[1]) * cap
        spot = first
        for rank in range(cap - 1):
            spot = jnp.where(slots[first + rank] >= 0, first + rank + 1, spot)
        slots[spot] = leaf

    def copy_of(leaf):
        return pltpu.make_async_copy(held.at[leaf], out.at[0, :, leaf, :, pl.ds(h * cols, cols)], sems.at[leaf])

    for dist in range(fronts):
        mine, fields = fields[: counts[dist]], fields[counts[dist] :]
        columns = [ref[q].reshape(tall, ref.shape[3]) for ref in mine for q in range(ref.shape[0])]
        field = jnp.concatenate(columns, axis=1)
        for rank in range(cap):
            name = slots[dist * cap + rank]

            @pl.when(name >= 0)
            def _(name=name, field=field):
                result = fwd[name].astype(F32) - dot(mats[name], field)
                held[name, 0] = result[:blk].astype(BF)
                held[name, 1] = result[blk:].astype(BF)
                copy_of(name).start()

    for leaf in range(leaves):
        copy_of(leaf).wait()


def backward(h, owners, place, fwd, mats, fields, before, width, after):
    leaves, wide, cols = fwd.shape
    blk, fronts = wide // 2, len(fields)
    cap = -(-leaves // fronts)
    counts = [len(field) for field in fields]
    flat = [part for field in fields for part in field]
    aliased = [] if before is None else [before]
    return call(
        functools.partial(backward_kernel, h, counts, cap, len(aliased)), "leaf_backward",
        [owners, place, fwd, mats, *flat, *aliased], [SMEM, SMEM] + [VMEM] * (2 + len(flat)) + [HBM] * len(aliased),
        shape_of((1, 2, leaves, blk, width)), HBM, after,
        [
            pltpu.VMEM((leaves, 2, blk, cols), BF),
            pltpu.SMEM((fronts * cap,), jnp.int32),
            pltpu.SemaphoreType.DMA((leaves,)),
        ],
        {4 + len(flat): 0} if aliased else None,
    )


def body(leaf_rhs, leaf_inv, leaf_off, parent, ancestors, root_rhs, root_inv, coupling):
    fronts, slabs = lax.axis_size("front"), lax.axis_size("slab")
    rows, width = root_rhs.shape[2], root_rhs.shape[3]
    blk = leaf_rhs.shape[3]
    owners = parent.reshape(-1)
    place = jnp.stack([lax.axis_index("slab"), lax.axis_index("front")]).astype(jnp.int32)
    pairs = fronts // 2
    parts = slabs // (rows // blk)
    part = width // HALVES // parts
    square = pairs == 4

    def start_forward(h, after):
        fwd, keep, send = forward(
            h, owners, place, leaf_rhs, leaf_inv, leaf_off, ancestors, fronts, rows, part, after
        )
        return fwd, keep, crossed(send, "front", 1)

    def send_first(keep, near, after):
        if not square:
            sums = first_sums([(j, 0, parts) for j in range(1, pairs)], keep, near, after)
            return sums[0], [crossed(value, "front", 2 * (j + 1)) for j, value in enumerate(sums)]
        to_x, to_y = first_sums([(3, 0, parts // 2), (3, parts // 2, parts)], keep, near, after)
        return to_x, [crossed(to_x, "front", 2), crossed(to_y, "front", 4)]

    def send_second(keep, near, got, after):
        if not square:
            return got[0], got
        to_x, to_y = second_sums(parts // 2, keep, near, *got, after)
        return to_x, [crossed(to_x, "front", 2), crossed(to_y, "front", 4)]

    def over_slabs(values):
        return [values[0]] + [crossed(values[mask], "slab", mask) for mask in range(1, slabs)]

    def share(own):
        if square:
            by_x, by_y = crossed(own, "front", 2), crossed(own, "front", 4)
            far = [crossed(by_x[: parts // 2], "front", 4), crossed(by_y[parts // 2 :], "front", 2)]
            mine = [[own], [by_x], [by_y], far]
        else:
            mine = [[own]] + [[crossed(own, "front", 2 * j)] for j in range(1, pairs)]
        return [field for group in mine for field in (group, [crossed(value, "front", 1) for value in group])]

    fwd0, keep0, near0 = start_forward(0, ())
    same, other = pack(place, root_inv, coupling, [fwd0])
    have = [same, crossed(other, "slab", 1)]
    token, got0 = send_first(keep0, near0, [same])
    fwd1, keep1, near1 = start_forward(1, [token])
    token, far0 = send_second(keep0, near0, got0, [fwd1])
    step = 2
    while step < slabs:
        joined = join(have, [token])
        have = have + [crossed(joined, "slab", step)]
        step *= 2
        token = joined
    token, got1 = send_first(keep1, near1, [token])
    folded = fold(leaf_inv, leaf_off, ancestors, rows, [token])
    pieces0 = reduce(0, place, root_rhs, keep0, near0, far0, slabs, blk, [folded])
    token, far1 = send_second(keep1, near1, got1, [pieces0[0]])
    solved0 = chain(place, over_slabs(pieces0), have, [token])
    pieces1 = reduce(1, place, root_rhs, keep1, near1, far1, slabs, blk, [solved0[0]])
    own0, root_sol = collect(0, place, over_slabs(solved0), None, rows, width, [pieces1[0]])
    solved1 = chain(place, over_slabs(pieces1), have, [own0])
    fields0 = share(own0)
    own1, root_sol = collect(1, place, over_slabs(solved1), root_sol, rows, width, ())
    fields1 = share(own1)
    leaf_sol = backward(0, owners, place, fwd0, folded, fields0, None, width, [own1])
    leaf_sol = backward(1, owners, place, fwd1, folded, fields1, leaf_sol, width, ())
    return leaf_sol, root_sol


def solution(mesh):
    in_specs = (
        P("slab", None, "front", None, None),
        P("slab", "front", None, None, None),
        P("slab", "front", None, None, None),
        P("slab", "front", None),
        P("slab", "front", None),
        P("slab", None, "front", None),
        P("slab", "front", None, None, None),
        P("slab", "front"),
    )
    out_specs = (P("slab", None, "front", None, None), P("slab", None, "front", None))
    return jax.shard_map(body, mesh=mesh, in_specs=in_specs, out_specs=out_specs, check_vma=False)
```

```python
import functools

import jax
import jax.numpy as jnp
from jax import lax
from jax.experimental import pallas as pl
from jax.experimental.pallas import tpu as pltpu
from jax.sharding import PartitionSpec as P

HALVES = 2
FORWARD_ROOM = (52, 24)
BF = jnp.bfloat16
F32 = jnp.float32
VMEM = pl.BlockSpec(memory_space=pltpu.VMEM)
SMEM = pl.BlockSpec(memory_space=pltpu.SMEM)
HBM = pl.BlockSpec(memory_space=pltpu.HBM)
ANY = pl.BlockSpec(memory_space=pl.ANY)


def shape_of(shape, dtype=BF):
    return jax.ShapeDtypeStruct(shape, dtype)


def call(kernel, name, ins, in_specs, outs, out_specs, after=(), scratch=(), aliases=None, room=24):
    count, extra = len(ins), len(after)

    def wrapped(*refs):
        kernel(*refs[:count], *refs[count + extra :])

    return pl.pallas_call(
        wrapped,
        in_specs=list(in_specs) + [ANY] * extra,
        out_specs=out_specs,
        out_shape=outs,
        scratch_shapes=list(scratch),
        input_output_aliases=aliases or {},
        compiler_params=pltpu.CompilerParams(vmem_limit_bytes=room * 1024 * 1024),
        cost_estimate=pl.CostEstimate(flops=10**10, bytes_accessed=1, transcendentals=0),
        name=name,
    )(*ins, *after)


def crossed(x, axis, mask):
    return lax.ppermute(x, axis, [(i, i ^ mask) for i in range(lax.axis_size(axis))])


def stacked(real, imag):
    return jnp.concatenate(
        [jnp.concatenate([real, -imag], axis=1), jnp.concatenate([imag, real], axis=1)], axis=0
    )


def dot(a, b, dims=((1,), (0,)), precision=None):
    return lax.dot_general(a, b, (dims, ((), ())), precision=precision, preferred_element_type=F32)


def table_of(anc_row, rows):
    ids = lax.broadcasted_iota(jnp.int32, (rows, anc_row.shape[1]), 0)
    return (ids == anc_row).astype(F32).astype(BF)


def forward_kernel(h, group, cap, owners, place, rhs, inv, off, anc, fwd, keep, send,
                   vecs, invs, offs, ancs, part, ids, seen, sems):
    leaves, blk, cols = vecs.shape[1], vecs.shape[2], vecs.shape[3]
    fronts, rows, width = part.shape[0], keep.shape[3], keep.shape[4]
    me = place[1]
    small = pltpu.make_async_copy(anc.at[0], ancs, sems.at[leaves // group, 0])

    def copies(at):
        span = pl.ds(at * group, group)
        return (
            pltpu.make_async_copy(inv.at[0, span], invs.at[span], sems.at[at, 0]),
            pltpu.make_async_copy(rhs.at[0, :, span, :, pl.ds(h * cols, cols)], vecs.at[:, span], sems.at[at, 1]),
            pltpu.make_async_copy(off.at[0, span], offs.at[span], sems.at[at, 2]),
        )

    for at in range(leaves // group):
        for copy in copies(at):
            copy.start()
    small.start()
    ids[...] = jnp.full(ids.shape, -1, jnp.int32)
    for dist in range(fronts):
        seen[dist] = 0
    small.wait()

    for at in range(leaves // group):
        for copy in copies(at):
            copy.wait()
        names = [at * group + j for j in range(group)]
        values = []
        for leaf in names:
            vec = jnp.concatenate([vecs[0, leaf], vecs[1, leaf]], axis=0)
            values.append(dot(stacked(invs[leaf, 0], invs[leaf, 1]), vec).astype(BF))
        moved = [dot(stacked(offs[leaf, 0], offs[leaf, 1]), value).astype(BF) for leaf, value in zip(names, values)]
        for leaf, value, shift in zip(names, values, moved):
            fwd[leaf] = value
            dist = owners[leaf] ^ me
            rank = seen[dist]
            seen[dist] = rank + 1
            part[dist, 0, rank] = shift[:blk]
            part[dist, 1, rank] = shift[blk:]
            ids[pl.ds(dist * cap + rank, 1), :] = ancs[pl.ds(leaf, 1), :]

    for dist in range(fronts if fronts * cap > leaves else 0):
        for rank in range(cap):

            @pl.when(seen[dist] <= rank)
            def _(dist=dist, rank=rank):
                part[dist, 0, rank] = jnp.zeros((blk, cols), BF)
                part[dist, 1, rank] = jnp.zeros((blk, cols), BF)

    for dist in range(fronts):
        row = jnp.concatenate([ids[dist * cap + rank : dist * cap + rank + 1, :] for rank in range(cap)], axis=1)
        table = table_of(row, rows)
        out = send if dist % 2 else keep
        for plane in range(2):
            value = dot(table, part[dist, plane].reshape(cap * blk, cols)).astype(BF)
            for q in range(cols // width):
                out[dist // 2, q, plane] = value[:, q * width : (q + 1) * width]


def forward(h, owners, place, leaf_rhs, leaf_inv, leaf_off, ancestors, fronts, rows, part, after):
    _, _, leaves, blk, width = leaf_rhs.shape
    cols = width // HALVES
    cap = -(-leaves // fronts)
    group = 4
    block = shape_of((fronts // 2, cols // part, 2, rows, part))
    return call(
        functools.partial(forward_kernel, h, group, cap),
        "leaf_forward",
        [owners, place, leaf_rhs, leaf_inv, leaf_off, ancestors],
        [SMEM, SMEM, HBM, HBM, HBM, HBM],
        [shape_of((leaves, 2 * blk, cols)), block, block],
        [VMEM, VMEM, VMEM],
        after,
        [
            pltpu.VMEM((2, leaves, blk, cols), BF),
            pltpu.VMEM((leaves, 2, blk, blk), BF),
            pltpu.VMEM((leaves, 2, blk, blk), BF),
            pltpu.VMEM((leaves, blk), jnp.int32),
            pltpu.VMEM((fronts, 2, cap, blk, cols), BF),
            pltpu.VMEM((fronts * cap, blk), jnp.int32),
            pltpu.SMEM((fronts,), jnp.int32),
            pltpu.SemaphoreType.DMA((leaves // group + 1, 3)),
        ],
        room=FORWARD_ROOM[h],
    )


def fold_kernel(inv, off, anc, out):
    leaves, _, blk, _ = inv.shape[1:]
    rows = out.shape[2] // 2

    def one(leaf, carry):
        mat = jnp.concatenate([inv[0, leaf, 0], inv[0, leaf, 1]], axis=1)
        real, imag = off[0, leaf, 0], off[0, leaf, 1]
        other = jnp.concatenate([jnp.concatenate([real, -imag], axis=1), jnp.concatenate([imag, real], axis=1)], axis=0)
        both = dot(mat, other, ((1,), (1,))).astype(BF)
        table = table_of(anc[0, pl.ds(leaf, 1), :], rows)
        real = dot(both[:, :blk], table, ((1,), (1,))).astype(BF)
        imag = dot(both[:, blk:], table, ((1,), (1,))).astype(BF)
        out[leaf, :blk, :rows] = real
        out[leaf, :blk, rows:] = -imag
        out[leaf, blk:, :rows] = imag
        out[leaf, blk:, rows:] = real
        return carry

    lax.fori_loop(0, leaves, one, 0, unroll=2)


def fold(leaf_inv, leaf_off, ancestors, rows, after):
    _, leaves, _, blk, _ = leaf_inv.shape
    return call(
        fold_kernel, "leaf_fold", [leaf_inv, leaf_off, ancestors], [VMEM] * 3,
        shape_of((leaves, 2 * blk, 2 * rows)), VMEM, after,
    )


def pack_kernel(place, inv, cpl, same, other):
    blocks, blk = inv.shape[1], inv.shape[3]
    for kind, out in enumerate((same, other)):
        block = (place[0] % blocks) ^ kind
        out[:blk] = inv[0, block, 0].astype(BF)
        out[blk : 2 * blk] = inv[0, block, 1].astype(BF)
        rest = jnp.broadcast_to(cpl[0, pl.ds(block, 1), :], (16, blk))
        row = lax.broadcasted_iota(jnp.int32, (16, blk), 0)
        value = jnp.zeros((16, blk), F32)
        for term in range(3):
            piece = rest.astype(BF).astype(F32)
            value = jnp.where(row == term, piece, value)
            rest = rest - piece
        out[2 * blk :] = value.astype(BF)


def pack(place, root_inv, coupling, after):
    _, blocks, _, blk, _ = root_inv.shape
    shape = shape_of((2 * blk + 16, blk))
    return call(
        pack_kernel, "solve_pack", [place, root_inv, coupling.reshape(1, blocks, blk)], [SMEM, VMEM, VMEM],
        [shape, shape], [VMEM, VMEM], after,
    )


def join_kernel(*refs):
    *parts, out = refs
    at = 0
    for ref in parts:
        out[at : at + ref.shape[0]] = ref[...]
        at += ref.shape[0]


def join(parts, after):
    rows = sum(part.shape[0] for part in parts)
    return call(
        join_kernel, "solve_join", parts, [VMEM] * len(parts), shape_of((rows,) + parts[0].shape[1:]), VMEM, after
    )


def first_kernel(names, keep, near, *outs):
    for (j, first, last), out in zip(names, outs):
        out[...] = (keep[j, first:last].astype(F32) + near[j, first:last].astype(F32)).astype(BF)


def first_sums(names, keep, near, after):
    return call(
        functools.partial(first_kernel, names), "interface_first", [keep, near], [VMEM, VMEM],
        [shape_of((last - first,) + keep.shape[2:]) for _, first, last in names], [VMEM] * len(names), after,
    )


def second_kernel(half, keep, near, by_x, by_y, out_x, out_y):
    parts = keep.shape[1]
    for j, out, extra, first, last in ((1, out_x, by_y, half, parts), (2, out_y, by_x, 0, half)):
        for q in range(parts):
            value = keep[j, q].astype(F32) + near[j, q].astype(F32)
            if first <= q < last:
                value = value + extra[q - first].astype(F32)
            out[q] = value.astype(BF)


def second_sums(half, keep, near, by_x, by_y, after):
    shape = shape_of(keep.shape[1:])
    return call(
        functools.partial(second_kernel, half), "interface_second", [keep, near, by_x, by_y], [VMEM] * 4,
        [shape, shape], [VMEM] * 2, after,
    )


def piece_of(index, blk, blocks):
    low = (index % blocks) * blk
    return index // blocks, slice(low, low + blk)


def reduce_kernel(h, slabs, blk, terms, place, rhs, keep, near, *refs):
    _, parts, _, rows, part = keep.shape
    outs, held = refs[terms:-1], refs[-1]
    for index in range(slabs):
        q, span = piece_of(index, blk, rows // blk)
        left = h * parts * part + q * part
        for plane in range(2):
            value = keep[0, q, plane, span].astype(F32) + near[0, q, plane, span].astype(F32)
            for ref in refs[:terms]:
                value = value + ref[q, plane, span].astype(F32)
            held[index, plane] = (rhs[0, plane, span, left : left + part].astype(F32) - value).astype(BF)
    for mask, out in enumerate(outs):
        out[...] = held[place[0] ^ mask]


def reduce(h, place, root_rhs, keep, near, far, slabs, blk, after):
    part = keep.shape[4]
    return call(
        functools.partial(reduce_kernel, h, slabs, blk, len(far)), "interface_reduce",
        [place, root_rhs, keep, near, *far], [SMEM] + [VMEM] * (3 + len(far)),
        [shape_of((2, blk, part))] * slabs, [VMEM] * slabs, after, [pltpu.VMEM((slabs, 2, blk, part), BF)],
    )


def chain_kernel(slabs, count, place, *refs):
    pieces, mats, outs = refs[:slabs], refs[slabs : slabs + count], refs[slabs + count : 2 * slabs + count]
    held, solver = refs[2 * slabs + count :]
    me = place[0]
    for mask in range(slabs):
        held[mask] = pieces[mask][...]
    _, _, blk, part = held.shape
    tall = solver.shape[1]
    at = 0
    for mat in mats:
        for k in range(mat.shape[0] // tall):
            solver[at] = mat[k * tall : (k + 1) * tall]
            at += 1
    state = None
    for slab in range(slabs):
        at = me ^ slab
        field = held[at].reshape(2 * blk, part).astype(F32)
        packed = solver[at]
        if state is not None:
            terms = packed[2 * blk :].astype(F32)
            row = terms[0:1] + terms[1:2] + terms[2:3]
            scale = jnp.broadcast_to(row, (blk, blk)).T[:, :1]
            field = field - jnp.concatenate([scale, scale], axis=0) * state
        mat = stacked(packed[:blk], packed[blk : 2 * blk])
        high = field.astype(BF)
        if slab:
            low = (field - high.astype(F32)).astype(BF)
            both = dot(mat, jnp.concatenate([high, low], axis=1))
            state = both[:, :part] + both[:, part:]
        else:
            state = dot(mat, high)
        held[at] = state.astype(BF).reshape(2, blk, part)
    for mask, out in enumerate(outs):
        out[...] = held[mask]


def chain(place, pieces, mats, after):
    slabs = len(pieces)
    tall = mats[0].shape
    return call(
        functools.partial(chain_kernel, slabs, len(mats)), "sweep_chain", [place, *pieces, *mats],
        [SMEM] + [VMEM] * (slabs + len(mats)),
        [shape_of(pieces[0].shape)] * slabs, [VMEM] * slabs, after,
        [pltpu.VMEM((slabs,) + pieces[0].shape, BF), pltpu.VMEM((slabs,) + tall, BF)],
    )


def collect_kernel(slabs, place, *refs):
    pieces = refs[:slabs]
    own, held = refs[slabs:]
    _, blk, _ = pieces[0].shape
    rows = own.shape[2]
    for mask, piece in enumerate(pieces):
        held[mask] = piece[...]
    for index in range(slabs):
        q, span = piece_of(index, blk, rows // blk)
        piece = held[place[0] ^ index]
        own[q, 0, span] = piece[0]
        own[q, 1, span] = piece[1]


def collect(place, pieces, rows, after):
    slabs = len(pieces)
    _, blk, part = pieces[0].shape
    return call(
        functools.partial(collect_kernel, slabs), "interface_collect", [place, *pieces], [SMEM] + [VMEM] * slabs,
        shape_of((slabs // (rows // blk), 2, rows, part)), VMEM, after, [pltpu.VMEM((slabs, 2, blk, part), BF)],
    )


def relay_kernel(half, own, by_x, by_y, to_y, to_x, near):
    to_y[...] = by_x[:half]
    to_x[...] = by_y[half:]
    for at, ref in enumerate((own, by_x, by_y)):
        near[at] = ref[...]


def relay(own, by_x, by_y, after):
    parts = own.shape[0]
    half = parts // 2
    return call(
        functools.partial(relay_kernel, half), "interface_relay", [own, by_x, by_y], [VMEM] * 3,
        [shape_of((half,) + own.shape[1:]), shape_of((parts - half,) + own.shape[1:]), shape_of((3,) + own.shape)],
        [VMEM] * 3, after,
    )


def backward_kernel(h, named, count, cap, owns, aliased, owners, place, fwd, mats, *refs):
    fronts = len(named)
    fields, refs = refs[:count], refs[count:]
    roots, refs = refs[:owns], refs[owns + aliased :]
    out, refs = refs[0], refs[1:]
    held, slots, sems = refs[-3:]
    leaves, wide, cols = fwd.shape
    blk = wide // 2
    tall = mats.shape[2]
    full = fronts * cap == leaves
    copies = []
    if owns:
        root, token, wider, root_sem = refs[:4]
        token[...] = jnp.zeros(token.shape, F32)
        parts, _, _, part = roots[0].shape
        for at, ref in enumerate(roots):
            for q in range(parts):
                left = (at * parts + q) * part
                for plane in range(2):
                    wider[plane, :, left : left + part] = ref[q, plane].astype(F32)
        copies.append(pltpu.make_async_copy(wider, root.at[0], root_sem))
        copies[0].start()
    for slot in range(fronts * cap):
        slots[slot] = -1
    for leaf in range(leaves):
        first = (owners[leaf] ^ place[1]) * cap
        spot = first
        for rank in range(cap - 1):
            spot = jnp.where(slots[first + rank] >= 0, first + rank + 1, spot)
        slots[spot] = leaf

    def copy_of(leaf):
        return pltpu.make_async_copy(held.at[leaf], out.at[0, :, leaf, :, pl.ds(h * cols, cols)], sems.at[leaf])

    def solve(name, field):
        result = fwd[name].astype(F32) - dot(mats[name], field)
        held[name, 0] = result[:blk].astype(BF)
        held[name, 1] = result[blk:].astype(BF)
        copy_of(name).start()

    for dist in range(fronts):
        mine = [fields[at] if lead is None else fields[at].at[lead] for at, lead in named[dist]]
        columns = [ref[q].reshape(tall, ref.shape[3]) for ref in mine for q in range(ref.shape[0])]
        field = jnp.concatenate(columns, axis=1)
        for rank in range(cap):
            name = slots[dist * cap + rank]
            if full:
                solve(name, field)
            else:
                pl.when(name >= 0)(functools.partial(solve, name, field))

    for leaf in range(leaves):
        copies.append(copy_of(leaf))
    for copy in copies:
        copy.wait()


def backward(h, owners, place, fwd, mats, fields, roots, before, width, after):
    leaves, wide, cols = fwd.shape
    blk, fronts = wide // 2, len(fields)
    cap = -(-leaves // fronts)
    flat, named = [], []
    for field in fields:
        named.append([])
        for value in field:
            value, lead = value if isinstance(value, tuple) else (value, None)
            known = [at for at, other in enumerate(flat) if other is value]
            if not known:
                flat.append(value)
            named[-1].append((known[0] if known else len(flat) - 1, lead))
    count = len(flat)
    flat = flat + roots
    aliased = [] if before is None else [before]
    outs, specs, scratch = [shape_of((1, 2, leaves, blk, width))], [HBM], []
    if roots:
        rows = roots[0].shape[2]
        outs, specs = outs + [shape_of((1, 2, rows, width), F32), shape_of((8, 128), F32)], [HBM, HBM, VMEM]
        scratch = [pltpu.VMEM((2, rows, width), F32), pltpu.SemaphoreType.DMA]
    return call(
        functools.partial(backward_kernel, h, named, count, cap, len(roots), len(aliased)), "leaf_backward",
        [owners, place, fwd, mats, *flat, *aliased], [SMEM, SMEM] + [VMEM] * (2 + len(flat)) + [HBM] * len(aliased),
        outs, specs, after,
        scratch
        + [
            pltpu.VMEM((leaves, 2, blk, cols), BF),
            pltpu.SMEM((fronts * cap,), jnp.int32),
            pltpu.SemaphoreType.DMA((leaves,)),
        ],
        {4 + len(flat): 0} if aliased else None,
    )


def body(leaf_rhs, leaf_inv, leaf_off, parent, ancestors, root_rhs, root_inv, coupling):
    fronts, slabs = lax.axis_size("front"), lax.axis_size("slab")
    rows, width = root_rhs.shape[2], root_rhs.shape[3]
    blk = leaf_rhs.shape[3]
    owners = parent.reshape(-1)
    place = jnp.stack([lax.axis_index("slab"), lax.axis_index("front")]).astype(jnp.int32)
    pairs = fronts // 2
    parts = slabs // (rows // blk)
    part = width // HALVES // parts
    square = pairs == 4

    def start_forward(h, after):
        fwd, keep, send = forward(
            h, owners, place, leaf_rhs, leaf_inv, leaf_off, ancestors, fronts, rows, part, after
        )
        return fwd, keep, crossed(send, "front", 1)

    def send_first(keep, near, after):
        if not square:
            sums = first_sums([(j, 0, parts) for j in range(1, pairs)], keep, near, after)
            return sums[0], [crossed(value, "front", 2 * (j + 1)) for j, value in enumerate(sums)]
        to_x, to_y = first_sums([(3, 0, parts // 2), (3, parts // 2, parts)], keep, near, after)
        return to_x, [crossed(to_x, "front", 2), crossed(to_y, "front", 4)]

    def send_second(keep, near, got, after):
        if not square:
            return got[0], got
        to_x, to_y = second_sums(parts // 2, keep, near, *got, after)
        return to_x, [crossed(to_x, "front", 2), crossed(to_y, "front", 4)]

    def over_slabs(values):
        return [values[0]] + [crossed(values[mask], "slab", mask) for mask in range(1, slabs)]

    def near_of(values):
        return [crossed(value, "front", 1) for value in values]

    def share_first(own):
        return [crossed(own, "front", mask) for mask in ((2, 4) if square else range(2, fronts, 2))]

    def share_second(own, got, after):
        if not square:
            mine = [own] + got
            return [[value] for pair in zip(mine, near_of(mine)) for value in pair], got[0]
        to_y, to_x, held = relay(own, *got, after)
        far = [crossed(to_y, "front", 4), crossed(to_x, "front", 2)]
        there = crossed(held, "front", 1)
        fields = []
        for at, value in enumerate([own] + got):
            fields += [[value], [(there, at)]]
        return fields + [far, near_of(far)], to_y

    fwd0, keep0, near0 = start_forward(0, ())
    token, got0 = send_first(keep0, near0, ())
    fwd1, keep1, near1 = start_forward(1, [token])
    token, far0 = send_second(keep0, near0, got0, [fwd1])
    same, other = pack(place, root_inv, coupling, [token])
    have = [same, crossed(other, "slab", 1)]
    token, got1 = send_first(keep1, near1, [same])
    step = 2
    while step < slabs:
        token = join(have, [token])
        have = have + [crossed(token, "slab", step)]
        step *= 2
    folded = fold(leaf_inv, leaf_off, ancestors, rows, [token])
    pieces0 = reduce(0, place, root_rhs, keep0, near0, far0, slabs, blk, [folded])
    token, far1 = send_second(keep1, near1, got1, [pieces0[0]])
    solved0 = chain(place, over_slabs(pieces0), have, [token])
    pieces1 = reduce(1, place, root_rhs, keep1, near1, far1, slabs, blk, [solved0[0]])
    own0 = collect(place, over_slabs(solved0), rows, [pieces1[0]])
    got0 = share_first(own0)
    solved1 = chain(place, over_slabs(pieces1), have, [own0])
    fields0, token = share_second(own0, got0, [solved1[0]])
    own1 = collect(place, over_slabs(solved1), rows, [token])
    got1 = share_first(own1)
    leaf_sol, root_sol, token = backward(0, owners, place, fwd0, folded, fields0, [own0, own1], None, width, ())
    fields1, _ = share_second(own1, got1, [token])
    (leaf_sol,) = backward(1, owners, place, fwd1, folded, fields1, [], leaf_sol, width, ())
    return leaf_sol, root_sol


def solution(mesh):
    in_specs = (
        P("slab", None, "front", None, None),
        P("slab", "front", None, None, None),
        P("slab", "front", None, None, None),
        P("slab", "front", None),
        P("slab", "front", None),
        P("slab", None, "front", None),
        P("slab", "front", None, None, None),
        P("slab", "front"),
    )
    out_specs = (P("slab", None, "front", None, None), P("slab", None, "front", None))
    return jax.shard_map(body, mesh=mesh, in_specs=in_specs, out_specs=out_specs, check_vma=False)
```

```python
import functools

import jax
import jax.numpy as jnp
from jax import lax
from jax.experimental import pallas as pl
from jax.experimental.pallas import tpu as pltpu
from jax.sharding import PartitionSpec as P

HALVES = 2
FIRST_ROOM = 52
BRIEF = ("solve_join", "interface_first", "interface_relay", "interface_join")
BF = jnp.bfloat16
F32 = jnp.float32
VMEM = pl.BlockSpec(memory_space=pltpu.VMEM)
SMEM = pl.BlockSpec(memory_space=pltpu.SMEM)
HBM = pl.BlockSpec(memory_space=pltpu.HBM)
ANY = pl.BlockSpec(memory_space=pl.ANY)


def shape_of(shape, dtype=BF):
    return jax.ShapeDtypeStruct(shape, dtype)


def call(kernel, name, ins, in_specs, outs, out_specs, after=(), scratch=(), aliases=None, room=24):
    count, extra = len(ins), len(after)

    def wrapped(*refs):
        kernel(*refs[:count], *refs[count + extra :])

    return pl.pallas_call(
        wrapped,
        in_specs=list(in_specs) + [ANY] * extra,
        out_specs=out_specs,
        out_shape=outs,
        scratch_shapes=list(scratch),
        input_output_aliases=aliases or {},
        compiler_params=pltpu.CompilerParams(vmem_limit_bytes=room * 1024 * 1024),
        cost_estimate=pl.CostEstimate(flops=1 if name in BRIEF else 10**10, bytes_accessed=1, transcendentals=0),
        name=name,
    )(*ins, *after)


def crossed(x, axis, mask):
    return lax.ppermute(x, axis, [(i, i ^ mask) for i in range(lax.axis_size(axis))])


def stacked(real, imag):
    return jnp.concatenate(
        [jnp.concatenate([real, -imag], axis=1), jnp.concatenate([imag, real], axis=1)], axis=0
    )


def dot(a, b, dims=((1,), (0,)), precision=None):
    return lax.dot_general(a, b, (dims, ((), ())), precision=precision, preferred_element_type=F32)


def table_of(anc_row, rows):
    ids = lax.broadcasted_iota(jnp.int32, (rows, anc_row.shape[1]), 0)
    return (ids == anc_row).astype(F32).astype(BF)


def forward_kernel(h, group, cap, owners, place, rhs, inv, off, anc, fwd, keep, send, part, ids, seen, *rest):
    leaves, blk, cols = rhs.shape[2], rhs.shape[3], part.shape[4]
    fronts, rows, width = part.shape[0], keep.shape[3], keep.shape[4]
    me = place[1]
    if rest:
        vecs, invs, offs, ancs, sems = rest
        small = pltpu.make_async_copy(anc.at[0], ancs, sems.at[leaves // group, 0])

        def copies(at):
            span = pl.ds(at * group, group)
            return (
                pltpu.make_async_copy(inv.at[0, span], invs.at[span], sems.at[at, 0]),
                pltpu.make_async_copy(rhs.at[0, :, span, :, pl.ds(h * cols, cols)], vecs.at[:, span], sems.at[at, 1]),
                pltpu.make_async_copy(off.at[0, span], offs.at[span], sems.at[at, 2]),
            )

        for at in range(leaves // group):
            for copy in copies(at):
                copy.start()
        small.start()
    else:
        vecs, invs, offs, ancs = rhs.at[0, :, :, :, pl.ds(h * cols, cols)], inv.at[0], off.at[0], anc.at[0]
    ids[...] = jnp.full(ids.shape, -1, jnp.int32)
    for dist in range(fronts):
        seen[dist] = 0
    if rest:
        small.wait()

    for at in range(leaves // group):
        for copy in copies(at) if rest else ():
            copy.wait()
        names = [at * group + j for j in range(group)]
        values = []
        for leaf in names:
            vec = jnp.concatenate([vecs[0, leaf], vecs[1, leaf]], axis=0)
            values.append(dot(stacked(invs[leaf, 0], invs[leaf, 1]), vec).astype(BF))
        moved = [dot(stacked(offs[leaf, 0], offs[leaf, 1]), value).astype(BF) for leaf, value in zip(names, values)]
        for leaf, value, shift in zip(names, values, moved):
            fwd[leaf] = value
            dist = owners[leaf] ^ me
            rank = seen[dist]
            seen[dist] = rank + 1
            part[dist, 0, rank] = shift[:blk]
            part[dist, 1, rank] = shift[blk:]
            ids[pl.ds(dist * cap + rank, 1), :] = ancs[pl.ds(leaf, 1), :]

    for dist in range(fronts if fronts * cap > leaves else 0):
        for rank in range(cap):

            @pl.when(seen[dist] <= rank)
            def _(dist=dist, rank=rank):
                part[dist, 0, rank] = jnp.zeros((blk, cols), BF)
                part[dist, 1, rank] = jnp.zeros((blk, cols), BF)

    for dist in range(fronts):
        row = jnp.concatenate([ids[dist * cap + rank : dist * cap + rank + 1, :] for rank in range(cap)], axis=1)
        table = table_of(row, rows)
        out = send if dist % 2 else keep
        for plane in range(2):
            value = dot(table, part[dist, plane].reshape(cap * blk, cols)).astype(BF)
            for q in range(cols // width):
                out[dist // 2, q, plane] = value[:, q * width : (q + 1) * width]


def forward(h, owners, place, leaf_rhs, leaf_inv, leaf_off, ancestors, fronts, rows, part, after):
    _, _, leaves, blk, width = leaf_rhs.shape
    cols = width // HALVES
    cap = -(-leaves // fronts)
    group = 8
    block = shape_of((fronts // 2, cols // part, 2, rows, part))
    scratch = [
        pltpu.VMEM((fronts, 2, cap, blk, cols), BF),
        pltpu.VMEM((fronts * cap, blk), jnp.int32),
        pltpu.SMEM((fronts,), jnp.int32),
    ]
    if h == 0:
        scratch += [
            pltpu.VMEM((2, leaves, blk, cols), BF),
            pltpu.VMEM((leaves, 2, blk, blk), BF),
            pltpu.VMEM((leaves, 2, blk, blk), BF),
            pltpu.VMEM((leaves, blk), jnp.int32),
            pltpu.SemaphoreType.DMA((leaves // group + 1, 3)),
        ]
    return call(
        functools.partial(forward_kernel, h, group, cap),
        "leaf_forward",
        [owners, place, leaf_rhs, leaf_inv, leaf_off, ancestors],
        [SMEM, SMEM] + [VMEM if h else HBM] * 4,
        [shape_of((leaves, 2 * blk, cols)), block, block],
        [VMEM, VMEM, VMEM],
        after,
        scratch,
        room=24 if h else FIRST_ROOM,
    )


def fold_kernel(inv, off, anc, out):
    leaves, _, blk, _ = inv.shape[1:]
    rows = out.shape[2] // 2

    def one(leaf, carry):
        mat = jnp.concatenate([inv[0, leaf, 0], inv[0, leaf, 1]], axis=1)
        real, imag = off[0, leaf, 0], off[0, leaf, 1]
        other = jnp.concatenate([jnp.concatenate([real, -imag], axis=1), jnp.concatenate([imag, real], axis=1)], axis=0)
        both = dot(mat, other, ((1,), (1,))).astype(BF)
        table = table_of(anc[0, pl.ds(leaf, 1), :], rows)
        real = dot(both[:, :blk], table, ((1,), (1,))).astype(BF)
        imag = dot(both[:, blk:], table, ((1,), (1,))).astype(BF)
        out[leaf, :blk, :rows] = real
        out[leaf, :blk, rows:] = -imag
        out[leaf, blk:, :rows] = imag
        out[leaf, blk:, rows:] = real
        return carry

    lax.fori_loop(0, leaves, one, 0, unroll=leaves)


def fold(leaf_inv, leaf_off, ancestors, rows, after):
    _, leaves, _, blk, _ = leaf_inv.shape
    return call(
        fold_kernel, "leaf_fold", [leaf_inv, leaf_off, ancestors], [VMEM] * 3,
        shape_of((leaves, 2 * blk, 2 * rows)), VMEM, after,
    )


def pack_kernel(place, inv, cpl, same, other):
    blocks, blk = inv.shape[1], inv.shape[3]
    for kind, out in enumerate((same, other)):
        block = (place[0] % blocks) ^ kind
        out[:blk] = inv[0, block, 0].astype(BF)
        out[blk : 2 * blk] = inv[0, block, 1].astype(BF)
        rest = jnp.broadcast_to(cpl[0, pl.ds(block, 1), :], (16, blk))
        row = lax.broadcasted_iota(jnp.int32, (16, blk), 0)
        value = jnp.zeros((16, blk), F32)
        for term in range(3):
            piece = rest.astype(BF).astype(F32)
            value = jnp.where(row == term, piece, value)
            rest = rest - piece
        out[2 * blk :] = value.astype(BF)


def pack(place, root_inv, coupling, after):
    _, blocks, _, blk, _ = root_inv.shape
    shape = shape_of((2 * blk + 16, blk))
    return call(
        pack_kernel, "solve_pack", [place, root_inv, coupling.reshape(1, blocks, blk)], [SMEM, VMEM, VMEM],
        [shape, shape], [VMEM, VMEM], after,
    )


def join_kernel(*refs):
    *parts, out = refs
    at = 0
    for ref in parts:
        out[at : at + ref.shape[0]] = ref[...]
        at += ref.shape[0]


def join(parts, after, name="solve_join"):
    rows = sum(part.shape[0] for part in parts)
    return call(
        join_kernel, name, parts, [VMEM] * len(parts), shape_of((rows,) + parts[0].shape[1:]), VMEM, after
    )


def first_kernel(names, keep, near, *outs):
    for (j, first, last), out in zip(names, outs):
        out[...] = (keep[j, first:last].astype(F32) + near[j, first:last].astype(F32)).astype(BF)


def first_sums(names, keep, near, after):
    return call(
        functools.partial(first_kernel, names), "interface_first", [keep, near], [VMEM, VMEM],
        [shape_of((last - first,) + keep.shape[2:]) for _, first, last in names], [VMEM] * len(names), after,
    )


def second_kernel(half, keep, near, by_x, by_y, out_x, out_y):
    parts = keep.shape[1]
    for j, out, extra, first, last in ((1, out_x, by_y, half, parts), (2, out_y, by_x, 0, half)):
        for q in range(parts):
            value = keep[j, q].astype(F32) + near[j, q].astype(F32)
            if first <= q < last:
                value = value + extra[q - first].astype(F32)
            out[q] = value.astype(BF)


def second_sums(half, keep, near, by_x, by_y, after):
    shape = shape_of(keep.shape[1:])
    return call(
        functools.partial(second_kernel, half), "interface_second", [keep, near, by_x, by_y], [VMEM] * 4,
        [shape, shape], [VMEM] * 2, after,
    )


def piece_of(index, blk, blocks):
    low = (index % blocks) * blk
    return index // blocks, slice(low, low + blk)


def reduce_kernel(h, slabs, blk, terms, place, rhs, keep, near, *refs):
    _, parts, _, rows, part = keep.shape
    outs, held = refs[terms:-1], refs[-1]
    for index in range(slabs):
        q, span = piece_of(index, blk, rows // blk)
        left = h * parts * part + q * part
        for plane in range(2):
            value = keep[0, q, plane, span].astype(F32) + near[0, q, plane, span].astype(F32)
            for ref in refs[:terms]:
                value = value + ref[q, plane, span].astype(F32)
            held[index, plane] = (rhs[0, plane, span, left : left + part].astype(F32) - value).astype(BF)
    for mask, out in enumerate(outs):
        out[...] = held[place[0] ^ mask]


def reduce(h, place, root_rhs, keep, near, far, slabs, blk, after):
    part = keep.shape[4]
    return call(
        functools.partial(reduce_kernel, h, slabs, blk, len(far)), "interface_reduce",
        [place, root_rhs, keep, near, *far], [SMEM] + [VMEM] * (3 + len(far)),
        [shape_of((2, blk, part))] * slabs, [VMEM] * slabs, after, [pltpu.VMEM((slabs, 2, blk, part), BF)],
    )


def chain_kernel(slabs, count, place, *refs):
    pieces, mats, outs = refs[:slabs], refs[slabs : slabs + count], refs[slabs + count : 2 * slabs + count]
    held, solver = refs[2 * slabs + count :]
    me = place[0]
    for mask in range(slabs):
        held[mask] = pieces[mask][...]
    _, _, blk, part = held.shape
    tall = solver.shape[1]
    at = 0
    for mat in mats:
        for k in range(mat.shape[0] // tall):
            solver[at] = mat[k * tall : (k + 1) * tall]
            at += 1
    state = None
    for slab in range(slabs):
        at = me ^ slab
        field = held[at].reshape(2 * blk, part).astype(F32)
        packed = solver[at]
        if state is not None:
            terms = packed[2 * blk :].astype(F32)
            row = terms[0:1] + terms[1:2] + terms[2:3]
            scale = jnp.broadcast_to(row, (blk, blk)).T[:, :1]
            field = field - jnp.concatenate([scale, scale], axis=0) * state
        mat = stacked(packed[:blk], packed[blk : 2 * blk])
        high = field.astype(BF)
        if slab:
            low = (field - high.astype(F32)).astype(BF)
            both = dot(mat, jnp.concatenate([high, low], axis=1))
            state = both[:, :part] + both[:, part:]
        else:
            state = dot(mat, high)
        held[at] = state.astype(BF).reshape(2, blk, part)
    for mask, out in enumerate(outs):
        out[...] = held[mask]


def chain(place, pieces, mats, after):
    slabs = len(pieces)
    tall = mats[0].shape
    return call(
        functools.partial(chain_kernel, slabs, len(mats)), "sweep_chain", [place, *pieces, *mats],
        [SMEM] + [VMEM] * (slabs + len(mats)),
        [shape_of(pieces[0].shape)] * slabs, [VMEM] * slabs, after,
        [pltpu.VMEM((slabs,) + pieces[0].shape, BF), pltpu.VMEM((slabs,) + tall, BF)],
    )


def collect_kernel(slabs, place, *refs):
    pieces = refs[:slabs]
    own, held = refs[slabs:]
    _, blk, _ = pieces[0].shape
    rows = own.shape[2]
    for mask, piece in enumerate(pieces):
        held[mask] = piece[...]
    for index in range(slabs):
        q, span = piece_of(index, blk, rows // blk)
        piece = held[place[0] ^ index]
        own[q, 0, span] = piece[0]
        own[q, 1, span] = piece[1]


def collect(place, pieces, rows, after):
    slabs = len(pieces)
    _, blk, part = pieces[0].shape
    return call(
        functools.partial(collect_kernel, slabs), "interface_collect", [place, *pieces], [SMEM] + [VMEM] * slabs,
        shape_of((slabs // (rows // blk), 2, rows, part)), VMEM, after, [pltpu.VMEM((slabs, 2, blk, part), BF)],
    )


def relay_kernel(half, own, by_x, by_y, to_y, to_x, near):
    to_y[...] = by_x[:half]
    to_x[...] = by_y[half:]
    for at, ref in enumerate((own, by_x, by_y)):
        near[at] = ref[...]


def relay(own, by_x, by_y, after):
    parts = own.shape[0]
    half = parts // 2
    return call(
        functools.partial(relay_kernel, half), "interface_relay", [own, by_x, by_y], [VMEM] * 3,
        [shape_of((half,) + own.shape[1:]), shape_of((parts - half,) + own.shape[1:]), shape_of((3,) + own.shape)],
        [VMEM] * 3, after,
    )


def backward_kernel(h, named, count, cap, owns, aliased, owners, place, fwd, mats, *refs):
    fronts = len(named)
    fields, refs = refs[:count], refs[count:]
    roots, refs = refs[:owns], refs[owns + aliased :]
    out, refs = refs[0], refs[1:]
    held, slots, sems = refs[-3:]
    leaves, wide, cols = fwd.shape
    blk = wide // 2
    tall = mats.shape[2]
    full = fronts * cap == leaves
    copies = []
    if owns:
        root, token, wider, root_sem = refs[:4]
        token[...] = jnp.zeros(token.shape, F32)
        parts, _, _, part = roots[0].shape
        for at, ref in enumerate(roots):
            for q in range(parts):
                left = (at * parts + q) * part
                for plane in range(2):
                    wider[plane, :, left : left + part] = ref[q, plane].astype(F32)
        copies.append(pltpu.make_async_copy(wider, root.at[0], root_sem))
        copies[0].start()
    for slot in range(fronts * cap):
        slots[slot] = -1
    for leaf in range(leaves):
        first = (owners[leaf] ^ place[1]) * cap
        spot = first
        for rank in range(cap - 1):
            spot = jnp.where(slots[first + rank] >= 0, first + rank + 1, spot)
        slots[spot] = leaf

    def copy_of(leaf):
        return pltpu.make_async_copy(held.at[leaf], out.at[0, :, leaf, :, pl.ds(h * cols, cols)], sems.at[leaf])

    def solve(name, field):
        result = fwd[name].astype(F32) - dot(mats[name], field)
        held[name, 0] = result[:blk].astype(BF)
        held[name, 1] = result[blk:].astype(BF)

    batch = 4
    for low in range(0, fronts, batch):
        names = []
        for dist in range(low, min(fronts, low + batch)):
            mine = [fields[at] if lead is None else fields[at].at[lead] for at, lead in named[dist]]
            columns = [ref[q].reshape(tall, ref.shape[3]) for ref in mine for q in range(ref.shape[0])]
            field = jnp.concatenate(columns, axis=1)
            for rank in range(cap):
                names.append(slots[dist * cap + rank])
                if full:
                    solve(names[-1], field)
                else:
                    pl.when(names[-1] >= 0)(functools.partial(solve, names[-1], field))
        for name in names:
            if full:
                copy_of(name).start()
            else:
                pl.when(name >= 0)(copy_of(name).start)

    for leaf in range(leaves):
        copies.append(copy_of(leaf))
    for copy in copies:
        copy.wait()


def backward(h, owners, place, fwd, mats, fields, roots, before, width, after):
    leaves, wide, cols = fwd.shape
    blk, fronts = wide // 2, len(fields)
    cap = -(-leaves // fronts)
    flat, named = [], []
    for field in fields:
        named.append([])
        for value in field:
            value, lead = value if isinstance(value, tuple) else (value, None)
            known = [at for at, other in enumerate(flat) if other is value]
            if not known:
                flat.append(value)
            named[-1].append((known[0] if known else len(flat) - 1, lead))
    count = len(flat)
    flat = flat + roots
    aliased = [] if before is None else [before]
    outs, specs, scratch = [shape_of((1, 2, leaves, blk, width))], [HBM], []
    if roots:
        rows = roots[0].shape[2]
        outs, specs = outs + [shape_of((1, 2, rows, width), F32), shape_of((8, 128), F32)], [HBM, HBM, VMEM]
        scratch = [pltpu.VMEM((2, rows, width), F32), pltpu.SemaphoreType.DMA]
    return call(
        functools.partial(backward_kernel, h, named, count, cap, len(roots), len(aliased)), "leaf_backward",
        [owners, place, fwd, mats, *flat, *aliased], [SMEM, SMEM] + [VMEM] * (2 + len(flat)) + [HBM] * len(aliased),
        outs, specs, after,
        scratch
        + [
            pltpu.VMEM((leaves, 2, blk, cols), BF),
            pltpu.SMEM((fronts * cap,), jnp.int32),
            pltpu.SemaphoreType.DMA((leaves,)),
        ],
        {4 + len(flat): 0} if aliased else None,
    )


def body(leaf_rhs, leaf_inv, leaf_off, parent, ancestors, root_rhs, root_inv, coupling):
    fronts, slabs = lax.axis_size("front"), lax.axis_size("slab")
    rows, width = root_rhs.shape[2], root_rhs.shape[3]
    blk = leaf_rhs.shape[3]
    owners = parent.reshape(-1)
    place = jnp.stack([lax.axis_index("slab"), lax.axis_index("front")]).astype(jnp.int32)
    pairs = fronts // 2
    parts = slabs // (rows // blk)
    part = width // HALVES // parts
    square = pairs == 4

    def start_forward(h, after):
        fwd, keep, send = forward(
            h, owners, place, leaf_rhs, leaf_inv, leaf_off, ancestors, fronts, rows, part, after
        )
        return fwd, keep, crossed(send, "front", 1)

    def send_first(keep, near, after):
        if not square:
            sums = first_sums([(j, 0, parts) for j in range(1, pairs)], keep, near, after)
            return sums[0], [crossed(value, "front", 2 * (j + 1)) for j, value in enumerate(sums)]
        to_x, to_y = first_sums([(3, 0, parts // 2), (3, parts // 2, parts)], keep, near, after)
        return to_x, [crossed(to_x, "front", 2), crossed(to_y, "front", 4)]

    def send_second(keep, near, got, after):
        if not square:
            return got[0], got
        to_x, to_y = second_sums(parts // 2, keep, near, *got, after)
        return to_x, [crossed(to_x, "front", 2), crossed(to_y, "front", 4)]

    def over_slabs(values):
        return [values[0]] + [crossed(values[mask], "slab", mask) for mask in range(1, slabs)]

    def share_first(own):
        return [crossed(own, "front", mask) for mask in ((2, 4) if square else range(2, fronts, 2))]

    def share_second(own, got, after):
        if not square:
            return got[0], []
        to_y, to_x, held = relay(own, *got, after)
        return to_y, [crossed(to_y, "front", 4), crossed(to_x, "front", 2), crossed(held, "front", 1)]

    def share_third(own, got, more, after):
        if not square:
            mine = [own] + got
            return [[value] for field in mine for value in (field, crossed(field, "front", 1))]
        far = join(more[:2], after, "interface_join")
        fields = []
        for at, value in enumerate([own] + got):
            fields += [[value], [(more[2], at)]]
        return fields + [[far], [crossed(far, "front", 1)]]

    fwd0, keep0, near0 = start_forward(0, ())
    same, other = pack(place, root_inv, coupling, [fwd0])
    have = [same, crossed(other, "slab", 1)]
    token, got0 = send_first(keep0, near0, [same])
    fwd1, keep1, near1 = start_forward(1, [token, have[1]])
    token, far0 = send_second(keep0, near0, got0, [fwd1])
    token, got1 = send_first(keep1, near1, [token])
    step = 2
    while step < slabs:
        token = join(have, [token])
        have = have + [crossed(token, "slab", step)]
        step *= 2
    pieces0 = reduce(0, place, root_rhs, keep0, near0, far0, slabs, blk, [token])
    token, far1 = send_second(keep1, near1, got1, [pieces0[0]])
    solved0 = chain(place, over_slabs(pieces0), have, [token])
    pieces1 = reduce(1, place, root_rhs, keep1, near1, far1, slabs, blk, [solved0[0]])
    own0 = collect(place, over_slabs(solved0), rows, [pieces1[0]])
    got0 = share_first(own0)
    solved1 = chain(place, over_slabs(pieces1), have, [own0])
    folded = fold(leaf_inv, leaf_off, ancestors, rows, [solved1[0]])
    own1 = collect(place, over_slabs(solved1), rows, [folded])
    got1 = share_first(own1)
    token, more0 = share_second(own0, got0, [own1])
    token, more1 = share_second(own1, got1, [token])
    fields0 = share_third(own0, got0, more0, [token])
    leaf_sol, root_sol, token = backward(0, owners, place, fwd0, folded, fields0, [own0, own1], None, width, [token])
    fields1 = share_third(own1, got1, more1, [token])
    (leaf_sol,) = backward(1, owners, place, fwd1, folded, fields1, [], leaf_sol, width, ())
    return leaf_sol, root_sol


def solution(mesh):
    in_specs = (
        P("slab", None, "front", None, None),
        P("slab", "front", None, None, None),
        P("slab", "front", None, None, None),
        P("slab", "front", None),
        P("slab", "front", None),
        P("slab", None, "front", None),
        P("slab", "front", None, None, None),
        P("slab", "front"),
    )
    out_specs = (P("slab", None, "front", None, None), P("slab", None, "front", None))
    return jax.shard_map(body, mesh=mesh, in_specs=in_specs, out_specs=out_specs, check_vma=False)
```

```python
import functools

import jax
import jax.numpy as jnp
from jax import lax
from jax.experimental import pallas as pl
from jax.experimental.pallas import tpu as pltpu
from jax.sharding import PartitionSpec as P

HALVES = 2
FIRST_ROOM = 52
BRIEF = ("solve_join", "interface_first", "interface_join", "interface_second_1", "interface_relay_0")
BF = jnp.bfloat16
F32 = jnp.float32
VMEM = pl.BlockSpec(memory_space=pltpu.VMEM)
SMEM = pl.BlockSpec(memory_space=pltpu.SMEM)
HBM = pl.BlockSpec(memory_space=pltpu.HBM)
ANY = pl.BlockSpec(memory_space=pl.ANY)


def shape_of(shape, dtype=BF):
    return jax.ShapeDtypeStruct(shape, dtype)


def call(kernel, name, ins, in_specs, outs, out_specs, after=(), scratch=(), aliases=None, room=24):
    count, extra = len(ins), len(after)

    def wrapped(*refs):
        kernel(*refs[:count], *refs[count + extra :])

    return pl.pallas_call(
        wrapped,
        in_specs=list(in_specs) + [ANY] * extra,
        out_specs=out_specs,
        out_shape=outs,
        scratch_shapes=list(scratch),
        input_output_aliases=aliases or {},
        compiler_params=pltpu.CompilerParams(vmem_limit_bytes=room * 1024 * 1024),
        cost_estimate=pl.CostEstimate(flops=1 if name in BRIEF else 10**10, bytes_accessed=1, transcendentals=0),
        name=name,
    )(*ins, *after)


def crossed(x, axis, mask):
    return lax.ppermute(x, axis, [(i, i ^ mask) for i in range(lax.axis_size(axis))])


def stacked(real, imag):
    return jnp.concatenate(
        [jnp.concatenate([real, -imag], axis=1), jnp.concatenate([imag, real], axis=1)], axis=0
    )


def dot(a, b, dims=((1,), (0,)), precision=None):
    return lax.dot_general(a, b, (dims, ((), ())), precision=precision, preferred_element_type=F32)


def table_of(anc_row, rows):
    ids = lax.broadcasted_iota(jnp.int32, (rows, anc_row.shape[1]), 0)
    return (ids == anc_row).astype(F32).astype(BF)


def forward_kernel(h, group, cap, owners, place, rhs, inv, off, anc, keep, send, part, ids, seen, *rest):
    leaves, blk, cols = rhs.shape[2], rhs.shape[3], part.shape[4]
    fronts, rows, width = part.shape[0], keep.shape[3], keep.shape[4]
    me = place[1]
    if rest:
        vecs, invs, offs, ancs, sems = rest
        small = pltpu.make_async_copy(anc.at[0], ancs, sems.at[leaves // group, 0])

        def copies(at):
            span = pl.ds(at * group, group)
            return (
                pltpu.make_async_copy(inv.at[0, span], invs.at[span], sems.at[at, 0]),
                pltpu.make_async_copy(rhs.at[0, :, span, :, pl.ds(h * cols, cols)], vecs.at[:, span], sems.at[at, 1]),
                pltpu.make_async_copy(off.at[0, span], offs.at[span], sems.at[at, 2]),
            )

        for at in range(leaves // group):
            for copy in copies(at):
                copy.start()
        small.start()
    else:
        vecs, invs, offs, ancs = rhs.at[0, :, :, :, pl.ds(h * cols, cols)], inv.at[0], off.at[0], anc.at[0]
    ids[...] = jnp.full(ids.shape, -1, jnp.int32)
    for dist in range(fronts):
        seen[dist] = 0
    if rest:
        small.wait()

    for at in range(leaves // group):
        for copy in copies(at) if rest else ():
            copy.wait()
        names = [at * group + j for j in range(group)]
        values = []
        for leaf in names:
            vec = jnp.concatenate([vecs[0, leaf], vecs[1, leaf]], axis=0)
            values.append(dot(stacked(invs[leaf, 0], invs[leaf, 1]), vec).astype(BF))
        moved = [dot(stacked(offs[leaf, 0], offs[leaf, 1]), value).astype(BF) for leaf, value in zip(names, values)]
        for leaf, shift in zip(names, moved):
            dist = owners[leaf] ^ me
            rank = seen[dist]
            seen[dist] = rank + 1
            part[dist, 0, rank] = shift[:blk]
            part[dist, 1, rank] = shift[blk:]
            ids[pl.ds(dist * cap + rank, 1), :] = ancs[pl.ds(leaf, 1), :]

    for dist in range(fronts if fronts * cap > leaves else 0):
        for rank in range(cap):

            @pl.when(seen[dist] <= rank)
            def _(dist=dist, rank=rank):
                part[dist, 0, rank] = jnp.zeros((blk, cols), BF)
                part[dist, 1, rank] = jnp.zeros((blk, cols), BF)

    for dist in range(fronts):
        row = jnp.concatenate([ids[dist * cap + rank : dist * cap + rank + 1, :] for rank in range(cap)], axis=1)
        table = table_of(row, rows)
        out = send if dist % 2 else keep
        for plane in range(2):
            value = dot(table, part[dist, plane].reshape(cap * blk, cols)).astype(BF)
            for q in range(cols // width):
                out[dist // 2, q, plane] = value[:, q * width : (q + 1) * width]


def forward(h, owners, place, leaf_rhs, leaf_inv, leaf_off, ancestors, fronts, rows, part, after):
    _, _, leaves, blk, width = leaf_rhs.shape
    cols = width // HALVES
    cap = -(-leaves // fronts)
    group = 8
    block = shape_of((fronts // 2, cols // part, 2, rows, part))
    scratch = [
        pltpu.VMEM((fronts, 2, cap, blk, cols), BF),
        pltpu.VMEM((fronts * cap, blk), jnp.int32),
        pltpu.SMEM((fronts,), jnp.int32),
    ]
    if h == 0:
        scratch += [
            pltpu.VMEM((2, leaves, blk, cols), BF),
            pltpu.VMEM((leaves, 2, blk, blk), BF),
            pltpu.VMEM((leaves, 2, blk, blk), BF),
            pltpu.VMEM((leaves, blk), jnp.int32),
            pltpu.SemaphoreType.DMA((leaves // group + 1, 3)),
        ]
    return call(
        functools.partial(forward_kernel, h, group, cap),
        "leaf_forward",
        [owners, place, leaf_rhs, leaf_inv, leaf_off, ancestors],
        [SMEM, SMEM] + [VMEM if h else HBM] * 4,
        [block, block],
        [VMEM, VMEM],
        after,
        scratch,
        room=24 if h else FIRST_ROOM,
    )


def fold_kernel(inv, off, anc, out):
    leaves, _, blk, _ = inv.shape[1:]
    wide = 2 * blk
    rows = (out.shape[2] - wide) // 2

    def one(leaf, carry):
        mat = jnp.concatenate([inv[0, leaf, 0], inv[0, leaf, 1]], axis=1)
        real, imag = off[0, leaf, 0], off[0, leaf, 1]
        other = jnp.concatenate([jnp.concatenate([real, -imag], axis=1), jnp.concatenate([imag, real], axis=1)], axis=0)
        both = dot(mat, other, ((1,), (1,))).astype(BF)
        table = table_of(anc[0, pl.ds(leaf, 1), :], rows)
        real = dot(both[:, :blk], table, ((1,), (1,))).astype(BF)
        imag = dot(both[:, blk:], table, ((1,), (1,))).astype(BF)
        out[leaf, :, :wide] = stacked(inv[0, leaf, 0], inv[0, leaf, 1])
        out[leaf, :blk, wide : wide + rows] = -real
        out[leaf, :blk, wide + rows :] = imag
        out[leaf, blk:, wide : wide + rows] = -imag
        out[leaf, blk:, wide + rows :] = -real
        return carry

    lax.fori_loop(0, leaves, one, 0, unroll=leaves)


def fold(leaf_inv, leaf_off, ancestors, rows, after):
    _, leaves, _, blk, _ = leaf_inv.shape
    return call(
        fold_kernel, "leaf_fold", [leaf_inv, leaf_off, ancestors], [VMEM] * 3,
        shape_of((leaves, 2 * blk, 2 * blk + 2 * rows)), VMEM, after,
    )


def pack_kernel(place, inv, cpl, same, other):
    blocks, blk = inv.shape[1], inv.shape[3]
    for kind, out in enumerate((same, other)):
        block = (place[0] % blocks) ^ kind
        out[:blk] = inv[0, block, 0].astype(BF)
        out[blk : 2 * blk] = inv[0, block, 1].astype(BF)
        rest = jnp.broadcast_to(cpl[0, pl.ds(block, 1), :], (16, blk))
        row = lax.broadcasted_iota(jnp.int32, (16, blk), 0)
        value = jnp.zeros((16, blk), F32)
        for term in range(3):
            piece = rest.astype(BF).astype(F32)
            value = jnp.where(row == term, piece, value)
            rest = rest - piece
        out[2 * blk :] = value.astype(BF)


def pack(place, root_inv, coupling, after):
    _, blocks, _, blk, _ = root_inv.shape
    shape = shape_of((2 * blk + 16, blk))
    return call(
        pack_kernel, "solve_pack", [place, root_inv, coupling.reshape(1, blocks, blk)], [SMEM, VMEM, VMEM],
        [shape, shape], [VMEM, VMEM], after,
    )


def join_kernel(*refs):
    *parts, out = refs
    at = 0
    for ref in parts:
        out[at : at + ref.shape[0]] = ref[...]
        at += ref.shape[0]


def join(parts, after, name="solve_join"):
    rows = sum(part.shape[0] for part in parts)
    return call(
        join_kernel, name, parts, [VMEM] * len(parts), shape_of((rows,) + parts[0].shape[1:]), VMEM, after
    )


def first_kernel(names, keep, near, *outs):
    for (j, first, last), out in zip(names, outs):
        out[...] = (keep[j, first:last].astype(F32) + near[j, first:last].astype(F32)).astype(BF)


def first_sums(names, keep, near, after):
    return call(
        functools.partial(first_kernel, names), "interface_first", [keep, near], [VMEM, VMEM],
        [shape_of((last - first,) + keep.shape[2:]) for _, first, last in names], [VMEM] * len(names), after,
    )


def second_kernel(half, keep, near, by_x, by_y, out_x, out_y):
    parts = keep.shape[1]
    for j, out, extra, first, last in ((1, out_x, by_y, half, parts), (2, out_y, by_x, 0, half)):
        for q in range(parts):
            value = keep[j, q].astype(F32) + near[j, q].astype(F32)
            if first <= q < last:
                value = value + extra[q - first].astype(F32)
            out[q] = value.astype(BF)


def second_sums(h, half, keep, near, by_x, by_y, after):
    shape = shape_of(keep.shape[1:])
    return call(
        functools.partial(second_kernel, half), f"interface_second_{h}", [keep, near, by_x, by_y], [VMEM] * 4,
        [shape, shape], [VMEM] * 2, after,
    )


def piece_of(index, blk, blocks):
    low = (index % blocks) * blk
    return index // blocks, slice(low, low + blk)


def reduce_kernel(h, slabs, blk, terms, place, rhs, keep, near, *refs):
    _, parts, _, rows, part = keep.shape
    outs, held = refs[terms:-1], refs[-1]
    for index in range(slabs):
        q, span = piece_of(index, blk, rows // blk)
        left = h * parts * part + q * part
        for plane in range(2):
            value = keep[0, q, plane, span].astype(F32) + near[0, q, plane, span].astype(F32)
            for ref in refs[:terms]:
                value = value + ref[q, plane, span].astype(F32)
            held[index, plane] = (rhs[0, plane, span, left : left + part].astype(F32) - value).astype(BF)
    for mask, out in enumerate(outs):
        out[...] = held[place[0] ^ mask]


def reduce(h, place, root_rhs, keep, near, far, slabs, blk, after):
    part = keep.shape[4]
    return call(
        functools.partial(reduce_kernel, h, slabs, blk, len(far)), "interface_reduce",
        [place, root_rhs, keep, near, *far], [SMEM] + [VMEM] * (3 + len(far)),
        [shape_of((2, blk, part))] * slabs, [VMEM] * slabs, after, [pltpu.VMEM((slabs, 2, blk, part), BF)],
    )


def chain_kernel(slabs, count, place, *refs):
    pieces, mats, outs = refs[:slabs], refs[slabs : slabs + count], refs[slabs + count : 2 * slabs + count]
    held, solver = refs[2 * slabs + count :]
    me = place[0]
    for mask in range(slabs):
        held[mask] = pieces[mask][...]
    _, _, blk, part = held.shape
    tall = solver.shape[1]
    at = 0
    for mat in mats:
        for k in range(mat.shape[0] // tall):
            solver[at] = mat[k * tall : (k + 1) * tall]
            at += 1
    state = None
    for slab in range(slabs):
        at = me ^ slab
        field = held[at].reshape(2 * blk, part).astype(F32)
        packed = solver[at]
        if state is not None:
            terms = packed[2 * blk :].astype(F32)
            row = terms[0:1] + terms[1:2] + terms[2:3]
            scale = jnp.broadcast_to(row, (blk, blk)).T[:, :1]
            field = field - jnp.concatenate([scale, scale], axis=0) * state
        mat = stacked(packed[:blk], packed[blk : 2 * blk])
        high = field.astype(BF)
        if slab:
            low = (field - high.astype(F32)).astype(BF)
            both = dot(mat, jnp.concatenate([high, low], axis=1))
            state = both[:, :part] + both[:, part:]
        else:
            state = dot(mat, high)
        held[at] = state.astype(BF).reshape(2, blk, part)
    for mask, out in enumerate(outs):
        out[...] = held[mask]


def chain(place, pieces, mats, after):
    slabs = len(pieces)
    tall = mats[0].shape
    return call(
        functools.partial(chain_kernel, slabs, len(mats)), "sweep_chain", [place, *pieces, *mats],
        [SMEM] + [VMEM] * (slabs + len(mats)),
        [shape_of(pieces[0].shape)] * slabs, [VMEM] * slabs, after,
        [pltpu.VMEM((slabs,) + pieces[0].shape, BF), pltpu.VMEM((slabs,) + tall, BF)],
    )


def collect_kernel(slabs, place, *refs):
    pieces = refs[:slabs]
    own, held = refs[slabs:]
    _, blk, _ = pieces[0].shape
    rows = own.shape[2]
    for mask, piece in enumerate(pieces):
        held[mask] = piece[...]
    for index in range(slabs):
        q, span = piece_of(index, blk, rows // blk)
        piece = held[place[0] ^ index]
        own[q, 0, span] = piece[0]
        own[q, 1, span] = piece[1]


def collect(place, pieces, rows, after):
    slabs = len(pieces)
    _, blk, part = pieces[0].shape
    return call(
        functools.partial(collect_kernel, slabs), "interface_collect", [place, *pieces], [SMEM] + [VMEM] * slabs,
        shape_of((slabs // (rows // blk), 2, rows, part)), VMEM, after, [pltpu.VMEM((slabs, 2, blk, part), BF)],
    )


def relay_kernel(half, own, by_x, by_y, to_y, to_x, near):
    to_y[...] = by_x[:half]
    to_x[...] = by_y[half:]
    for at, ref in enumerate((own, by_x, by_y)):
        near[at] = ref[...]


def relay(h, own, by_x, by_y, after):
    parts = own.shape[0]
    half = parts // 2
    return call(
        functools.partial(relay_kernel, half), f"interface_relay_{h}", [own, by_x, by_y], [VMEM] * 3,
        [shape_of((half,) + own.shape[1:]), shape_of((parts - half,) + own.shape[1:]), shape_of((3,) + own.shape)],
        [VMEM] * 3, after,
    )


def backward_kernel(h, named, count, cap, owns, aliased, owners, place, rhs, mats, *refs):
    fronts = len(named)
    fields, refs = refs[:count], refs[count:]
    roots, refs = refs[:owns], refs[owns + aliased :]
    out, refs = refs[0], refs[1:]
    held, slots, sems = refs[-3:]
    leaves, wide, tall = mats.shape
    blk, cols = wide // 2, rhs.shape[4] // HALVES
    tall = tall - wide
    full = fronts * cap == leaves
    copies = []
    if owns:
        root, token, wider, root_sem = refs[:4]
        token[...] = jnp.zeros(token.shape, F32)
        parts, _, _, part = roots[0].shape
        for at, ref in enumerate(roots):
            for q in range(parts):
                left = (at * parts + q) * part
                for plane in range(2):
                    wider[plane, :, left : left + part] = ref[q, plane].astype(F32)
        copies.append(pltpu.make_async_copy(wider, root.at[0], root_sem))
        copies[0].start()
    for slot in range(fronts * cap):
        slots[slot] = -1
    for leaf in range(leaves):
        first = (owners[leaf] ^ place[1]) * cap
        spot = first
        for rank in range(cap - 1):
            spot = jnp.where(slots[first + rank] >= 0, first + rank + 1, spot)
        slots[spot] = leaf

    def copy_of(leaf):
        return pltpu.make_async_copy(held.at[leaf], out.at[0, :, leaf, :, pl.ds(h * cols, cols)], sems.at[leaf])

    def solve(name, field):
        here = pl.ds(h * cols, cols)
        vec = jnp.concatenate([rhs[0, 0, name, :, here], rhs[0, 1, name, :, here]], axis=0)
        result = dot(mats[name, :, :wide], vec) + dot(mats[name, :, wide:], field)
        held[name, 0] = result[:blk].astype(BF)
        held[name, 1] = result[blk:].astype(BF)

    batch = 4
    for low in range(0, fronts, batch):
        names = []
        for dist in range(low, min(fronts, low + batch)):
            mine = [fields[at] if lead is None else fields[at].at[lead] for at, lead in named[dist]]
            columns = [ref[q].reshape(tall, ref.shape[3]) for ref in mine for q in range(ref.shape[0])]
            field = jnp.concatenate(columns, axis=1)
            for rank in range(cap):
                names.append(slots[dist * cap + rank])
                if full:
                    solve(names[-1], field)
                else:
                    pl.when(names[-1] >= 0)(functools.partial(solve, names[-1], field))
        for name in names:
            if full:
                copy_of(name).start()
            else:
                pl.when(name >= 0)(copy_of(name).start)

    for leaf in range(leaves):
        copies.append(copy_of(leaf))
    for copy in copies:
        copy.wait()


def backward(h, owners, place, leaf_rhs, mats, fields, roots, before, width, after):
    leaves, wide, _ = mats.shape
    blk, fronts, cols = wide // 2, len(fields), width // HALVES
    cap = -(-leaves // fronts)
    flat, named = [], []
    for field in fields:
        named.append([])
        for value in field:
            value, lead = value if isinstance(value, tuple) else (value, None)
            known = [at for at, other in enumerate(flat) if other is value]
            if not known:
                flat.append(value)
            named[-1].append((known[0] if known else len(flat) - 1, lead))
    count = len(flat)
    flat = flat + roots
    aliased = [] if before is None else [before]
    outs, specs, scratch = [shape_of((1, 2, leaves, blk, width))], [HBM], []
    if roots:
        rows = roots[0].shape[2]
        outs, specs = outs + [shape_of((1, 2, rows, width), F32), shape_of((8, 128), F32)], [HBM, HBM, VMEM]
        scratch = [pltpu.VMEM((2, rows, width), F32), pltpu.SemaphoreType.DMA]
    return call(
        functools.partial(backward_kernel, h, named, count, cap, len(roots), len(aliased)), "leaf_backward",
        [owners, place, leaf_rhs, mats, *flat, *aliased], [SMEM, SMEM] + [VMEM] * (2 + len(flat)) + [HBM] * len(aliased),
        outs, specs, after,
        scratch
        + [
            pltpu.VMEM((leaves, 2, blk, cols), BF),
            pltpu.SMEM((fronts * cap,), jnp.int32),
            pltpu.SemaphoreType.DMA((leaves,)),
        ],
        {4 + len(flat): 0} if aliased else None,
    )


def body(leaf_rhs, leaf_inv, leaf_off, parent, ancestors, root_rhs, root_inv, coupling):
    fronts, slabs = lax.axis_size("front"), lax.axis_size("slab")
    rows, width = root_rhs.shape[2], root_rhs.shape[3]
    blk = leaf_rhs.shape[3]
    owners = parent.reshape(-1)
    place = jnp.stack([lax.axis_index("slab"), lax.axis_index("front")]).astype(jnp.int32)
    pairs = fronts // 2
    parts = slabs // (rows // blk)
    part = width // HALVES // parts
    square = pairs == 4

    def start_forward(h, after):
        keep, send = forward(
            h, owners, place, leaf_rhs, leaf_inv, leaf_off, ancestors, fronts, rows, part, after
        )
        return keep, crossed(send, "front", 1)

    def send_first(keep, near, after):
        if not square:
            sums = first_sums([(j, 0, parts) for j in range(1, pairs)], keep, near, after)
            return sums[0], [crossed(value, "front", 2 * (j + 1)) for j, value in enumerate(sums)]
        to_x, to_y = first_sums([(3, 0, parts // 2), (3, parts // 2, parts)], keep, near, after)
        return to_x, [crossed(to_x, "front", 2), crossed(to_y, "front", 4)]

    def send_second(h, keep, near, got, after):
        if not square:
            return got[0], got
        to_x, to_y = second_sums(h, parts // 2, keep, near, *got, after)
        return to_x, [crossed(to_x, "front", 2), crossed(to_y, "front", 4)]

    def over_slabs(values):
        return [values[0]] + [crossed(values[mask], "slab", mask) for mask in range(1, slabs)]

    def share_first(own):
        return [crossed(own, "front", mask) for mask in ((2, 4) if square else range(2, fronts, 2))]

    def share_second(h, own, got, after):
        if not square:
            return got[0], []
        to_y, to_x, held = relay(h, own, *got, after)
        return to_y, [crossed(to_y, "front", 4), crossed(to_x, "front", 2), crossed(held, "front", 1)]

    def share_third(own, got, more, after):
        if not square:
            mine = [own] + got
            return [[value] for field in mine for value in (field, crossed(field, "front", 1))]
        far = join(more[:2], after, "interface_join")
        fields = []
        for at, value in enumerate([own] + got):
            fields += [[value], [(more[2], at)]]
        return fields + [[far], [crossed(far, "front", 1)]]

    keep0, near0 = start_forward(0, ())
    same, other = pack(place, root_inv, coupling, [keep0])
    have = [same, crossed(other, "slab", 1)]
    token, got0 = send_first(keep0, near0, [same])
    keep1, near1 = start_forward(1, [token, have[1]])
    token, far0 = send_second(0, keep0, near0, got0, [keep1])
    token, got1 = send_first(keep1, near1, [token])
    step = 2
    while step < slabs:
        token = join(have, [token])
        have = have + [crossed(token, "slab", step)]
        step *= 2
    token, far1 = send_second(1, keep1, near1, got1, [token])
    pieces0 = reduce(0, place, root_rhs, keep0, near0, far0, slabs, blk, [token])
    pieces1 = reduce(1, place, root_rhs, keep1, near1, far1, slabs, blk, [pieces0[0]])
    solved0 = chain(place, over_slabs(pieces0), have, [pieces1[0]])
    solved1 = chain(place, over_slabs(pieces1), have, [solved0[0]])
    own0 = collect(place, over_slabs(solved0), rows, [solved1[0]])
    got0 = share_first(own0)
    own1 = collect(place, over_slabs(solved1), rows, [own0])
    got1 = share_first(own1)
    folded = fold(leaf_inv, leaf_off, ancestors, rows, [own1])
    token, more0 = share_second(0, own0, got0, [folded])
    token, more1 = share_second(1, own1, got1, [token])
    fields0 = share_third(own0, got0, more0, [token])
    leaf_sol, root_sol, token = backward(
        0, owners, place, leaf_rhs, folded, fields0, [own0, own1], None, width, [token]
    )
    fields1 = share_third(own1, got1, more1, [token])
    (leaf_sol,) = backward(1, owners, place, leaf_rhs, folded, fields1, [], leaf_sol, width, ())
    return leaf_sol, root_sol


def solution(mesh):
    in_specs = (
        P("slab", None, "front", None, None),
        P("slab", "front", None, None, None),
        P("slab", "front", None, None, None),
        P("slab", "front", None),
        P("slab", "front", None),
        P("slab", None, "front", None),
        P("slab", "front", None, None, None),
        P("slab", "front"),
    )
    out_specs = (P("slab", None, "front", None, None), P("slab", None, "front", None))
    return jax.shard_map(body, mesh=mesh, in_specs=in_specs, out_specs=out_specs, check_vma=False)
```

```python
import functools

import jax
import jax.numpy as jnp
from jax import lax
from jax.experimental import pallas as pl
from jax.experimental.pallas import tpu as pltpu
from jax.sharding import PartitionSpec as P

HALVES = 2
FIRST_ROOM = 52
BRIEF = ("solve_join", "interface_first", "interface_join", "interface_second_1", "interface_relay_0")
BF = jnp.bfloat16
F32 = jnp.float32
VMEM = pl.BlockSpec(memory_space=pltpu.VMEM)
SMEM = pl.BlockSpec(memory_space=pltpu.SMEM)
HBM = pl.BlockSpec(memory_space=pltpu.HBM)
ANY = pl.BlockSpec(memory_space=pl.ANY)


def shape_of(shape, dtype=BF):
    return jax.ShapeDtypeStruct(shape, dtype)


def call(kernel, name, ins, in_specs, outs, out_specs, after=(), scratch=(), aliases=None, room=24):
    count, extra = len(ins), len(after)

    def wrapped(*refs):
        kernel(*refs[:count], *refs[count + extra :])

    return pl.pallas_call(
        wrapped,
        in_specs=list(in_specs) + [ANY] * extra,
        out_specs=out_specs,
        out_shape=outs,
        scratch_shapes=list(scratch),
        input_output_aliases=aliases or {},
        compiler_params=pltpu.CompilerParams(vmem_limit_bytes=room * 1024 * 1024),
        cost_estimate=pl.CostEstimate(flops=1 if name in BRIEF else 10**10, bytes_accessed=1, transcendentals=0),
        name=name,
    )(*ins, *after)


def crossed(x, axis, mask):
    return lax.ppermute(x, axis, [(i, i ^ mask) for i in range(lax.axis_size(axis))])


def stacked(real, imag):
    return jnp.concatenate(
        [jnp.concatenate([real, -imag], axis=1), jnp.concatenate([imag, real], axis=1)], axis=0
    )


def dot(a, b, dims=((1,), (0,)), precision=None):
    return lax.dot_general(a, b, (dims, ((), ())), precision=precision, preferred_element_type=F32)


def table_of(anc_row, rows):
    ids = lax.broadcasted_iota(jnp.int32, (rows, anc_row.shape[1]), 0)
    return (ids == anc_row).astype(F32).astype(BF)


def forward_kernel(h, group, cap, owners, place, rhs, inv, off, anc, keep, send, part, ids, seen, *rest):
    leaves, blk, cols = rhs.shape[2], rhs.shape[3], part.shape[4]
    fronts, rows, width = part.shape[0], keep.shape[3], keep.shape[4]
    me = place[1]
    if rest:
        vecs, invs, offs, ancs, sems = rest
        small = pltpu.make_async_copy(anc.at[0], ancs, sems.at[leaves // group, 0])

        def copies(at):
            span = pl.ds(at * group, group)
            return (
                pltpu.make_async_copy(inv.at[0, span], invs.at[span], sems.at[at, 0]),
                pltpu.make_async_copy(rhs.at[0, :, span, :, pl.ds(h * cols, cols)], vecs.at[:, span], sems.at[at, 1]),
                pltpu.make_async_copy(off.at[0, span], offs.at[span], sems.at[at, 2]),
            )

        for at in range(leaves // group):
            for copy in copies(at):
                copy.start()
        small.start()
    else:
        vecs, invs, offs, ancs = rhs.at[0, :, :, :, pl.ds(h * cols, cols)], inv.at[0], off.at[0], anc.at[0]
    ids[...] = jnp.full(ids.shape, -1, jnp.int32)
    for dist in range(fronts):
        seen[dist] = 0
    if rest:
        small.wait()

    for at in range(leaves // group):
        for copy in copies(at) if rest else ():
            copy.wait()
        names = [at * group + j for j in range(group)]
        values = []
        for leaf in names:
            vec = jnp.concatenate([vecs[0, leaf], vecs[1, leaf]], axis=0)
            values.append(dot(stacked(invs[leaf, 0], invs[leaf, 1]), vec).astype(BF))
        moved = [dot(stacked(offs[leaf, 0], offs[leaf, 1]), value).astype(BF) for leaf, value in zip(names, values)]
        for leaf, shift in zip(names, moved):
            dist = owners[leaf] ^ me
            rank = seen[dist]
            seen[dist] = rank + 1
            part[dist, 0, rank] = shift[:blk]
            part[dist, 1, rank] = shift[blk:]
            ids[pl.ds(dist * cap + rank, 1), :] = ancs[pl.ds(leaf, 1), :]

    for dist in range(fronts if fronts * cap > leaves else 0):
        for rank in range(cap):

            @pl.when(seen[dist] <= rank)
            def _(dist=dist, rank=rank):
                part[dist, 0, rank] = jnp.zeros((blk, cols), BF)
                part[dist, 1, rank] = jnp.zeros((blk, cols), BF)

    for dist in range(fronts):
        row = jnp.concatenate([ids[dist * cap + rank : dist * cap + rank + 1, :] for rank in range(cap)], axis=1)
        table = table_of(row, rows)
        out = send if dist % 2 else keep
        for plane in range(2):
            value = dot(table, part[dist, plane].reshape(cap * blk, cols)).astype(BF)
            for q in range(cols // width):
                out[dist // 2, q, plane] = value[:, q * width : (q + 1) * width]


def forward(h, owners, place, leaf_rhs, leaf_inv, leaf_off, ancestors, fronts, rows, part, after):
    _, _, leaves, blk, width = leaf_rhs.shape
    cols = width // HALVES
    cap = -(-leaves // fronts)
    group = 8
    block = shape_of((fronts // 2, cols // part, 2, rows, part))
    scratch = [
        pltpu.VMEM((fronts, 2, cap, blk, cols), BF),
        pltpu.VMEM((fronts * cap, blk), jnp.int32),
        pltpu.SMEM((fronts,), jnp.int32),
    ]
    if h == 0:
        scratch += [
            pltpu.VMEM((2, leaves, blk, cols), BF),
            pltpu.VMEM((leaves, 2, blk, blk), BF),
            pltpu.VMEM((leaves, 2, blk, blk), BF),
            pltpu.VMEM((leaves, blk), jnp.int32),
            pltpu.SemaphoreType.DMA((leaves // group + 1, 3)),
        ]
    return call(
        functools.partial(forward_kernel, h, group, cap),
        "leaf_forward",
        [owners, place, leaf_rhs, leaf_inv, leaf_off, ancestors],
        [SMEM, SMEM] + [VMEM if h else HBM] * 4,
        [block, block],
        [VMEM, VMEM],
        after,
        scratch,
        room=24 if h else FIRST_ROOM,
    )


def fold_kernel(inv, off, anc, out):
    leaves, _, blk, _ = inv.shape[1:]
    wide = 2 * blk
    rows = (out.shape[2] - wide) // 2

    def one(leaf, carry):
        mat = jnp.concatenate([inv[0, leaf, 0], inv[0, leaf, 1]], axis=1)
        real, imag = off[0, leaf, 0], off[0, leaf, 1]
        other = jnp.concatenate([jnp.concatenate([real, -imag], axis=1), jnp.concatenate([imag, real], axis=1)], axis=0)
        both = dot(mat, other, ((1,), (1,))).astype(BF)
        table = table_of(anc[0, pl.ds(leaf, 1), :], rows)
        real = dot(both[:, :blk], table, ((1,), (1,))).astype(BF)
        imag = dot(both[:, blk:], table, ((1,), (1,))).astype(BF)
        out[leaf, :, :wide] = stacked(inv[0, leaf, 0], inv[0, leaf, 1])
        out[leaf, :blk, wide : wide + rows] = -real
        out[leaf, :blk, wide + rows :] = imag
        out[leaf, blk:, wide : wide + rows] = -imag
        out[leaf, blk:, wide + rows :] = -real
        return carry

    lax.fori_loop(0, leaves, one, 0, unroll=leaves)


def fold(leaf_inv, leaf_off, ancestors, rows, after):
    _, leaves, _, blk, _ = leaf_inv.shape
    return call(
        fold_kernel, "leaf_fold", [leaf_inv, leaf_off, ancestors], [VMEM] * 3,
        shape_of((leaves, 2 * blk, 2 * blk + 2 * rows)), VMEM, after,
    )


def pack_kernel(place, inv, cpl, same, other):
    blocks, blk = inv.shape[1], inv.shape[3]
    for kind, out in enumerate((same, other)):
        block = (place[0] % blocks) ^ kind
        out[:blk] = inv[0, block, 0].astype(BF)
        out[blk : 2 * blk] = inv[0, block, 1].astype(BF)
        rest = jnp.broadcast_to(cpl[0, pl.ds(block, 1), :], (16, blk))
        row = lax.broadcasted_iota(jnp.int32, (16, blk), 0)
        value = jnp.zeros((16, blk), F32)
        for term in range(3):
            piece = rest.astype(BF).astype(F32)
            value = jnp.where(row == term, piece, value)
            rest = rest - piece
        out[2 * blk :] = value.astype(BF)


def pack(place, root_inv, coupling, after):
    _, blocks, _, blk, _ = root_inv.shape
    shape = shape_of((2 * blk + 16, blk))
    return call(
        pack_kernel, "solve_pack", [place, root_inv, coupling.reshape(1, blocks, blk)], [SMEM, VMEM, VMEM],
        [shape, shape], [VMEM, VMEM], after,
    )


def join_kernel(*refs):
    *parts, out = refs
    at = 0
    for ref in parts:
        out[at : at + ref.shape[0]] = ref[...]
        at += ref.shape[0]


def join(parts, after, name="solve_join"):
    rows = sum(part.shape[0] for part in parts)
    return call(
        join_kernel, name, parts, [VMEM] * len(parts), shape_of((rows,) + parts[0].shape[1:]), VMEM, after
    )


def first_kernel(names, keep, near, *outs):
    for (j, first, last), out in zip(names, outs):
        out[...] = (keep[j, first:last].astype(F32) + near[j, first:last].astype(F32)).astype(BF)


def first_sums(names, keep, near, after):
    return call(
        functools.partial(first_kernel, names), "interface_first", [keep, near], [VMEM, VMEM],
        [shape_of((last - first,) + keep.shape[2:]) for _, first, last in names], [VMEM] * len(names), after,
    )


def second_kernel(half, keep, near, by_x, by_y, out_x, out_y):
    parts = keep.shape[1]
    for j, out, extra, first, last in ((1, out_x, by_y, half, parts), (2, out_y, by_x, 0, half)):
        for q in range(parts):
            value = keep[j, q].astype(F32) + near[j, q].astype(F32)
            if first <= q < last:
                value = value + extra[q - first].astype(F32)
            out[q] = value.astype(BF)


def second_sums(h, half, keep, near, by_x, by_y, after):
    shape = shape_of(keep.shape[1:])
    return call(
        functools.partial(second_kernel, half), f"interface_second_{h}", [keep, near, by_x, by_y], [VMEM] * 4,
        [shape, shape], [VMEM] * 2, after,
    )


def piece_of(index, blk, blocks):
    low = (index % blocks) * blk
    return index // blocks, slice(low, low + blk)


def reduce_kernel(h, slabs, blk, terms, place, rhs, keep, near, *refs):
    _, parts, _, rows, part = keep.shape
    outs, held = refs[terms:-1], refs[-1]
    for index in range(slabs):
        q, span = piece_of(index, blk, rows // blk)
        left = h * parts * part + q * part
        for plane in range(2):
            value = keep[0, q, plane, span].astype(F32) + near[0, q, plane, span].astype(F32)
            for ref in refs[:terms]:
                value = value + ref[q, plane, span].astype(F32)
            held[index, plane] = (rhs[0, plane, span, left : left + part].astype(F32) - value).astype(BF)
    for mask, out in enumerate(outs):
        out[...] = held[place[0] ^ mask]


def reduce(h, place, root_rhs, keep, near, far, slabs, blk, after):
    part = keep.shape[4]
    return call(
        functools.partial(reduce_kernel, h, slabs, blk, len(far)), "interface_reduce",
        [place, root_rhs, keep, near, *far], [SMEM] + [VMEM] * (3 + len(far)),
        [shape_of((2, blk, part))] * slabs, [VMEM] * slabs, after, [pltpu.VMEM((slabs, 2, blk, part), BF)],
    )


def chain_kernel(slabs, count, place, *refs):
    pieces, mats, outs = refs[:slabs], refs[slabs : slabs + count], refs[slabs + count : 2 * slabs + count]
    held, solver = refs[2 * slabs + count :]
    me = place[0]
    for mask in range(slabs):
        held[mask] = pieces[mask][...]
    _, _, blk, part = held.shape
    tall = solver.shape[1]
    at = 0
    for mat in mats:
        for k in range(mat.shape[0] // tall):
            solver[at] = mat[k * tall : (k + 1) * tall]
            at += 1
    state = None
    for slab in range(slabs):
        at = me ^ slab
        field = held[at].reshape(2 * blk, part).astype(F32)
        packed = solver[at]
        if state is not None:
            terms = packed[2 * blk :].astype(F32)
            row = terms[0:1] + terms[1:2] + terms[2:3]
            scale = jnp.broadcast_to(row, (blk, blk)).T[:, :1]
            field = field - jnp.concatenate([scale, scale], axis=0) * state
        mat = stacked(packed[:blk], packed[blk : 2 * blk])
        high = field.astype(BF)
        if slab:
            low = (field - high.astype(F32)).astype(BF)
            both = dot(mat, jnp.concatenate([high, low], axis=1))
            state = both[:, :part] + both[:, part:]
        else:
            state = dot(mat, high)
        held[at] = state.astype(BF).reshape(2, blk, part)
    for mask, out in enumerate(outs):
        out[...] = held[mask]


def chain(place, pieces, mats, after):
    slabs = len(pieces)
    tall = mats[0].shape
    return call(
        functools.partial(chain_kernel, slabs, len(mats)), "sweep_chain", [place, *pieces, *mats],
        [SMEM] + [VMEM] * (slabs + len(mats)),
        [shape_of(pieces[0].shape)] * slabs, [VMEM] * slabs, after,
        [pltpu.VMEM((slabs,) + pieces[0].shape, BF), pltpu.VMEM((slabs,) + tall, BF)],
    )


def collect_kernel(slabs, place, *refs):
    pieces = refs[:slabs]
    own, held = refs[slabs:]
    _, blk, _ = pieces[0].shape
    rows = own.shape[2]
    for mask, piece in enumerate(pieces):
        held[mask] = piece[...]
    for index in range(slabs):
        q, span = piece_of(index, blk, rows // blk)
        piece = held[place[0] ^ index]
        own[q, 0, span] = piece[0]
        own[q, 1, span] = piece[1]


def collect(place, pieces, rows, after):
    slabs = len(pieces)
    _, blk, part = pieces[0].shape
    return call(
        functools.partial(collect_kernel, slabs), "interface_collect", [place, *pieces], [SMEM] + [VMEM] * slabs,
        shape_of((slabs // (rows // blk), 2, rows, part)), VMEM, after, [pltpu.VMEM((slabs, 2, blk, part), BF)],
    )


def relay_kernel(half, own, by_x, by_y, to_y, to_x, near):
    to_y[...] = by_x[:half]
    to_x[...] = by_y[half:]
    for at, ref in enumerate((own, by_x, by_y)):
        near[at] = ref[...]


def relay(h, own, by_x, by_y, after):
    parts = own.shape[0]
    half = parts // 2
    return call(
        functools.partial(relay_kernel, half), f"interface_relay_{h}", [own, by_x, by_y], [VMEM] * 3,
        [shape_of((half,) + own.shape[1:]), shape_of((parts - half,) + own.shape[1:]), shape_of((3,) + own.shape)],
        [VMEM] * 3, after,
    )


def backward_kernel(h, named, count, cap, owns, aliased, owners, place, rhs, mats, *refs):
    fronts = len(named)
    fields, refs = refs[:count], refs[count:]
    roots, refs = refs[:owns], refs[owns + aliased :]
    out, refs = refs[0], refs[1:]
    held, slots, sems = refs[-3:]
    leaves, wide, tall = mats.shape
    blk, cols = wide // 2, rhs.shape[4] // HALVES
    tall = tall - wide
    full = fronts * cap == leaves
    copies = []
    if owns:
        root, wider, root_sem = refs[:3]
        parts, _, _, part = roots[0].shape
        for at, ref in enumerate(roots):
            for q in range(parts):
                left = (at * parts + q) * part
                for plane in range(2):
                    wider[plane, :, left : left + part] = ref[q, plane].astype(F32)
        copies.append(pltpu.make_async_copy(wider, root.at[0], root_sem))
        copies[0].start()
    for slot in range(fronts * cap):
        slots[slot] = -1
    for leaf in range(leaves):
        first = (owners[leaf] ^ place[1]) * cap
        spot = first
        for rank in range(cap - 1):
            spot = jnp.where(slots[first + rank] >= 0, first + rank + 1, spot)
        slots[spot] = leaf

    def copy_of(leaf):
        return pltpu.make_async_copy(held.at[leaf], out.at[0, :, leaf, :, pl.ds(h * cols, cols)], sems.at[leaf])

    def solve(name, field):
        here = pl.ds(h * cols, cols)
        vec = jnp.concatenate([rhs[0, 0, name, :, here], rhs[0, 1, name, :, here]], axis=0)
        result = dot(mats[name, :, :wide], vec) + dot(mats[name, :, wide:], field)
        held[name, 0] = result[:blk].astype(BF)
        held[name, 1] = result[blk:].astype(BF)

    batch = 4
    for low in range(0, fronts, batch):
        names = []
        for dist in range(low, min(fronts, low + batch)):
            mine = [fields[at] if lead is None else fields[at].at[lead] for at, lead in named[dist]]
            columns = [ref[q].reshape(tall, ref.shape[3]) for ref in mine for q in range(ref.shape[0])]
            field = jnp.concatenate(columns, axis=1)
            for rank in range(cap):
                names.append(slots[dist * cap + rank])
                if full:
                    solve(names[-1], field)
                else:
                    pl.when(names[-1] >= 0)(functools.partial(solve, names[-1], field))
        for name in names:
            if full:
                copy_of(name).start()
            else:
                pl.when(name >= 0)(copy_of(name).start)

    for leaf in range(leaves):
        copies.append(copy_of(leaf))
    for copy in copies:
        copy.wait()


def backward(h, owners, place, leaf_rhs, mats, fields, roots, before, width, after):
    leaves, wide, _ = mats.shape
    blk, fronts, cols = wide // 2, len(fields), width // HALVES
    cap = -(-leaves // fronts)
    flat, named = [], []
    for field in fields:
        named.append([])
        for value in field:
            value, lead = value if isinstance(value, tuple) else (value, None)
            known = [at for at, other in enumerate(flat) if other is value]
            if not known:
                flat.append(value)
            named[-1].append((known[0] if known else len(flat) - 1, lead))
    count = len(flat)
    flat = flat + roots
    aliased = [] if before is None else [before]
    outs, specs, scratch = [shape_of((1, 2, leaves, blk, width))], [HBM], []
    if roots:
        rows = roots[0].shape[2]
        outs, specs = outs + [shape_of((1, 2, rows, width), F32)], [HBM, HBM]
        scratch = [pltpu.VMEM((2, rows, width), F32), pltpu.SemaphoreType.DMA]
    return call(
        functools.partial(backward_kernel, h, named, count, cap, len(roots), len(aliased)), "leaf_backward",
        [owners, place, leaf_rhs, mats, *flat, *aliased], [SMEM, SMEM] + [VMEM] * (2 + len(flat)) + [HBM] * len(aliased),
        outs, specs, after,
        scratch
        + [
            pltpu.VMEM((leaves, 2, blk, cols), BF),
            pltpu.SMEM((fronts * cap,), jnp.int32),
            pltpu.SemaphoreType.DMA((leaves,)),
        ],
        {4 + len(flat): 0} if aliased else None,
    )


def body(leaf_rhs, leaf_inv, leaf_off, parent, ancestors, root_rhs, root_inv, coupling):
    fronts, slabs = lax.axis_size("front"), lax.axis_size("slab")
    rows, width = root_rhs.shape[2], root_rhs.shape[3]
    blk = leaf_rhs.shape[3]
    owners = parent.reshape(-1)
    place = jnp.stack([lax.axis_index("slab"), lax.axis_index("front")]).astype(jnp.int32)
    pairs = fronts // 2
    parts = slabs // (rows // blk)
    part = width // HALVES // parts
    square = pairs == 4

    def start_forward(h, after):
        keep, send = forward(
            h, owners, place, leaf_rhs, leaf_inv, leaf_off, ancestors, fronts, rows, part, after
        )
        return keep, crossed(send, "front", 1)

    def send_first(keep, near, after):
        if not square:
            sums = first_sums([(j, 0, parts) for j in range(1, pairs)], keep, near, after)
            return sums[0], [crossed(value, "front", 2 * (j + 1)) for j, value in enumerate(sums)]
        to_x, to_y = first_sums([(3, 0, parts // 2), (3, parts // 2, parts)], keep, near, after)
        return to_x, [crossed(to_x, "front", 2), crossed(to_y, "front", 4)]

    def send_second(h, keep, near, got, after):
        if not square:
            return got[0], got
        to_x, to_y = second_sums(h, parts // 2, keep, near, *got, after)
        return to_x, [crossed(to_x, "front", 2), crossed(to_y, "front", 4)]

    def over_slabs(values):
        return [values[0]] + [crossed(values[mask], "slab", mask) for mask in range(1, slabs)]

    def share_first(own):
        return [crossed(own, "front", mask) for mask in ((2, 4) if square else range(2, fronts, 2))]

    def share_second(h, own, got, after):
        if not square:
            return got[0], []
        to_y, to_x, held = relay(h, own, *got, after)
        return to_y, [crossed(to_y, "front", 4), crossed(to_x, "front", 2), crossed(held, "front", 1)]

    def share_third(owns, gots, mores):
        if not square:
            whole = [[own] + got for own, got in zip(owns, gots)]
            return [[[value] for field in mine for value in (field, crossed(field, "front", 1))] for mine in whole]
        far = join([value for more in mores for value in more[:2]], (), "interface_join")
        there = crossed(far, "front", 1)
        fields = []
        for h, (own, got, more) in enumerate(zip(owns, gots, mores)):
            span = pl.ds(h * parts, parts)
            near = [field for at, value in enumerate([own] + got) for field in ([value], [(more[2], at)])]
            fields.append(near + [[(far, span)], [(there, span)]])
        return fields

    keep0, near0 = start_forward(0, ())
    token, got0 = send_first(keep0, near0, ())
    keep1, near1 = start_forward(1, [token])
    token, far0 = send_second(0, keep0, near0, got0, [keep1])
    token, got1 = send_first(keep1, near1, [token])
    same, other = pack(place, root_inv, coupling, [token])
    have, step = [same, crossed(other, "slab", 1)], 2
    while step < slabs:
        token = join(have, [token])
        have = have + [crossed(token, "slab", step)]
        step *= 2
    token, far1 = send_second(1, keep1, near1, got1, [token])
    pieces0 = reduce(0, place, root_rhs, keep0, near0, far0, slabs, blk, [token])
    pieces1 = reduce(1, place, root_rhs, keep1, near1, far1, slabs, blk, [pieces0[0]])
    solved0 = chain(place, over_slabs(pieces0), have, [pieces1[0]])
    solved1 = chain(place, over_slabs(pieces1), have, [solved0[0]])
    own0 = collect(place, over_slabs(solved0), rows, [solved1[0]])
    got0 = share_first(own0)
    own1 = collect(place, over_slabs(solved1), rows, [own0])
    got1 = share_first(own1)
    folded = fold(leaf_inv, leaf_off, ancestors, rows, [own1])
    token, more0 = share_second(0, own0, got0, [folded])
    _, more1 = share_second(1, own1, got1, [token])
    fields0, fields1 = share_third((own0, own1), (got0, got1), (more0, more1))
    leaf_sol, root_sol = backward(
        0, owners, place, leaf_rhs, folded, fields0, [own0, own1], None, width, ()
    )
    (leaf_sol,) = backward(1, owners, place, leaf_rhs, folded, fields1, [], leaf_sol, width, ())
    return leaf_sol, root_sol


def solution(mesh):
    in_specs = (
        P("slab", None, "front", None, None),
        P("slab", "front", None, None, None),
        P("slab", "front", None, None, None),
        P("slab", "front", None),
        P("slab", "front", None),
        P("slab", None, "front", None),
        P("slab", "front", None, None, None),
        P("slab", "front"),
    )
    out_specs = (P("slab", None, "front", None, None), P("slab", None, "front", None))
    return jax.shard_map(body, mesh=mesh, in_specs=in_specs, out_specs=out_specs, check_vma=False)
```

```python
import functools

import jax
import jax.numpy as jnp
from jax import lax
from jax.experimental import pallas as pl
from jax.experimental.pallas import tpu as pltpu
from jax.sharding import PartitionSpec as P

HALVES = 2
FIRST_ROOM = 52
BRIEF = ("solve_join", "interface_first", "interface_join", "interface_second_1", "interface_relay_0")
BF = jnp.bfloat16
F32 = jnp.float32
VMEM = pl.BlockSpec(memory_space=pltpu.VMEM)
SMEM = pl.BlockSpec(memory_space=pltpu.SMEM)
HBM = pl.BlockSpec(memory_space=pltpu.HBM)
ANY = pl.BlockSpec(memory_space=pl.ANY)


def shape_of(shape, dtype=BF):
    return jax.ShapeDtypeStruct(shape, dtype)


def call(kernel, name, ins, in_specs, outs, out_specs, after=(), scratch=(), aliases=None, room=24):
    count, extra = len(ins), len(after)

    def wrapped(*refs):
        kernel(*refs[:count], *refs[count + extra :])

    return pl.pallas_call(
        wrapped,
        in_specs=list(in_specs) + [ANY] * extra,
        out_specs=out_specs,
        out_shape=outs,
        scratch_shapes=list(scratch),
        input_output_aliases=aliases or {},
        compiler_params=pltpu.CompilerParams(vmem_limit_bytes=room * 1024 * 1024),
        cost_estimate=pl.CostEstimate(flops=1 if name in BRIEF else 10**10, bytes_accessed=1, transcendentals=0),
        name=name,
    )(*ins, *after)


def crossed(x, axis, mask):
    return lax.ppermute(x, axis, [(i, i ^ mask) for i in range(lax.axis_size(axis))])


def stacked(real, imag):
    return jnp.concatenate(
        [jnp.concatenate([real, -imag], axis=1), jnp.concatenate([imag, real], axis=1)], axis=0
    )


def dot(a, b, dims=((1,), (0,)), precision=None):
    return lax.dot_general(a, b, (dims, ((), ())), precision=precision, preferred_element_type=F32)


def table_of(anc_row, rows):
    ids = lax.broadcasted_iota(jnp.int32, (rows, anc_row.shape[1]), 0)
    return (ids == anc_row).astype(F32).astype(BF)


def forward_kernel(h, group, cap, owners, place, rhs, inv, off, anc, keep, send, part, ids, seen, *rest):
    leaves, blk, cols = rhs.shape[2], rhs.shape[3], part.shape[4]
    fronts, rows, width = part.shape[0], keep.shape[3], keep.shape[4]
    me = place[1]
    if rest:
        vecs, invs, offs, ancs, sems = rest
        small = pltpu.make_async_copy(anc.at[0], ancs, sems.at[leaves // group, 0])

        def copies(at):
            span = pl.ds(at * group, group)
            return (
                pltpu.make_async_copy(inv.at[0, span], invs.at[span], sems.at[at, 0]),
                pltpu.make_async_copy(rhs.at[0, :, span, :, pl.ds(h * cols, cols)], vecs.at[:, span], sems.at[at, 1]),
                pltpu.make_async_copy(off.at[0, span], offs.at[span], sems.at[at, 2]),
            )

        for at in range(leaves // group):
            for copy in copies(at):
                copy.start()
        small.start()
    else:
        vecs, invs, offs, ancs = rhs.at[0, :, :, :, pl.ds(h * cols, cols)], inv.at[0], off.at[0], anc.at[0]
    ids[...] = jnp.full(ids.shape, -1, jnp.int32)
    for dist in range(fronts):
        seen[dist] = 0
    if rest:
        small.wait()

    for at in range(leaves // group):
        for copy in copies(at) if rest else ():
            copy.wait()
        names = [at * group + j for j in range(group)]
        values = []
        for leaf in names:
            vec = jnp.concatenate([vecs[0, leaf], vecs[1, leaf]], axis=0)
            values.append(dot(stacked(invs[leaf, 0], invs[leaf, 1]), vec).astype(BF))
        moved = [dot(stacked(offs[leaf, 0], offs[leaf, 1]), value).astype(BF) for leaf, value in zip(names, values)]
        for leaf, shift in zip(names, moved):
            dist = owners[leaf] ^ me
            rank = seen[dist]
            seen[dist] = rank + 1
            part[dist, 0, rank] = shift[:blk]
            part[dist, 1, rank] = shift[blk:]
            ids[pl.ds(dist * cap + rank, 1), :] = ancs[pl.ds(leaf, 1), :]

    for dist in range(fronts if fronts * cap > leaves else 0):
        for rank in range(cap):

            @pl.when(seen[dist] <= rank)
            def _(dist=dist, rank=rank):
                part[dist, 0, rank] = jnp.zeros((blk, cols), BF)
                part[dist, 1, rank] = jnp.zeros((blk, cols), BF)

    for dist in range(fronts):
        row = jnp.concatenate([ids[dist * cap + rank : dist * cap + rank + 1, :] for rank in range(cap)], axis=1)
        table = table_of(row, rows)
        out = send if dist % 2 else keep
        for plane in range(2):
            value = dot(table, part[dist, plane].reshape(cap * blk, cols)).astype(BF)
            for q in range(cols // width):
                out[dist // 2, q, plane] = value[:, q * width : (q + 1) * width]


def forward(h, owners, place, leaf_rhs, leaf_inv, leaf_off, ancestors, fronts, rows, part, after):
    _, _, leaves, blk, width = leaf_rhs.shape
    cols = width // HALVES
    cap = -(-leaves // fronts)
    group = 8
    block = shape_of((fronts // 2, cols // part, 2, rows, part))
    scratch = [
        pltpu.VMEM((fronts, 2, cap, blk, cols), BF),
        pltpu.VMEM((fronts * cap, blk), jnp.int32),
        pltpu.SMEM((fronts,), jnp.int32),
    ]
    if h == 0:
        scratch += [
            pltpu.VMEM((2, leaves, blk, cols), BF),
            pltpu.VMEM((leaves, 2, blk, blk), BF),
            pltpu.VMEM((leaves, 2, blk, blk), BF),
            pltpu.VMEM((leaves, blk), jnp.int32),
            pltpu.SemaphoreType.DMA((leaves // group + 1, 3)),
        ]
    return call(
        functools.partial(forward_kernel, h, group, cap),
        "leaf_forward",
        [owners, place, leaf_rhs, leaf_inv, leaf_off, ancestors],
        [SMEM, SMEM] + [VMEM if h else HBM] * 4,
        [block, block],
        [VMEM, VMEM],
        after,
        scratch,
        room=24 if h else FIRST_ROOM,
    )


def fold_kernel(inv, off, anc, out):
    leaves, _, blk, _ = inv.shape[1:]
    wide = 2 * blk
    rows = (out.shape[2] - wide) // 2

    def one(leaf, carry):
        mat = jnp.concatenate([inv[0, leaf, 0], inv[0, leaf, 1]], axis=1)
        real, imag = off[0, leaf, 0], off[0, leaf, 1]
        other = jnp.concatenate([jnp.concatenate([real, -imag], axis=1), jnp.concatenate([imag, real], axis=1)], axis=0)
        both = dot(mat, other, ((1,), (1,))).astype(BF)
        table = table_of(anc[0, pl.ds(leaf, 1), :], rows)
        real = dot(both[:, :blk], table, ((1,), (1,))).astype(BF)
        imag = dot(both[:, blk:], table, ((1,), (1,))).astype(BF)
        out[leaf, :, :wide] = stacked(inv[0, leaf, 0], inv[0, leaf, 1])
        out[leaf, :blk, wide : wide + rows] = -real
        out[leaf, :blk, wide + rows :] = imag
        out[leaf, blk:, wide : wide + rows] = -imag
        out[leaf, blk:, wide + rows :] = -real
        return carry

    lax.fori_loop(0, leaves, one, 0, unroll=leaves)


def fold(leaf_inv, leaf_off, ancestors, rows, after):
    _, leaves, _, blk, _ = leaf_inv.shape
    return call(
        fold_kernel, "leaf_fold", [leaf_inv, leaf_off, ancestors], [VMEM] * 3,
        shape_of((leaves, 2 * blk, 2 * blk + 2 * rows)), VMEM, after,
    )


def pack_kernel(place, inv, cpl, same, other):
    blocks, blk = inv.shape[1], inv.shape[3]
    for kind, out in enumerate((same, other)):
        block = (place[0] % blocks) ^ kind
        out[:blk] = inv[0, block, 0].astype(BF)
        out[blk : 2 * blk] = inv[0, block, 1].astype(BF)
        rest = jnp.broadcast_to(cpl[0, pl.ds(block, 1), :], (16, blk))
        row = lax.broadcasted_iota(jnp.int32, (16, blk), 0)
        value = jnp.zeros((16, blk), F32)
        for term in range(3):
            piece = rest.astype(BF).astype(F32)
            value = jnp.where(row == term, piece, value)
            rest = rest - piece
        out[2 * blk :] = value.astype(BF)


def pack(place, root_inv, coupling, after):
    _, blocks, _, blk, _ = root_inv.shape
    shape = shape_of((2 * blk + 16, blk))
    return call(
        pack_kernel, "solve_pack", [place, root_inv, coupling.reshape(1, blocks, blk)], [SMEM, VMEM, VMEM],
        [shape, shape], [VMEM, VMEM], after,
    )


def join_kernel(*refs):
    *parts, out = refs
    at = 0
    for ref in parts:
        out[at : at + ref.shape[0]] = ref[...]
        at += ref.shape[0]


def join(parts, after, name="solve_join"):
    rows = sum(part.shape[0] for part in parts)
    return call(
        join_kernel, name, parts, [VMEM] * len(parts), shape_of((rows,) + parts[0].shape[1:]), VMEM, after
    )


def first_kernel(names, keep, near, *outs):
    for (j, first, last), out in zip(names, outs):
        out[...] = (keep[j, first:last].astype(F32) + near[j, first:last].astype(F32)).astype(BF)


def first_sums(names, keep, near, after):
    return call(
        functools.partial(first_kernel, names), "interface_first", [keep, near], [VMEM, VMEM],
        [shape_of((last - first,) + keep.shape[2:]) for _, first, last in names], [VMEM] * len(names), after,
    )


def second_kernel(half, keep, near, by_x, by_y, out_x, out_y):
    parts = keep.shape[1]
    for j, out, extra, first, last in ((1, out_x, by_y, half, parts), (2, out_y, by_x, 0, half)):
        for q in range(parts):
            value = keep[j, q].astype(F32) + near[j, q].astype(F32)
            if first <= q < last:
                value = value + extra[q - first].astype(F32)
            out[q] = value.astype(BF)


def second_sums(h, half, keep, near, by_x, by_y, after):
    shape = shape_of(keep.shape[1:])
    return call(
        functools.partial(second_kernel, half), f"interface_second_{h}", [keep, near, by_x, by_y], [VMEM] * 4,
        [shape, shape], [VMEM] * 2, after,
    )


def piece_of(index, blk, blocks):
    low = (index % blocks) * blk
    return index // blocks, slice(low, low + blk)


def reduce_kernel(h, slabs, blk, terms, place, rhs, keep, near, *refs):
    _, parts, _, rows, part = keep.shape
    outs, held = refs[terms:-1], refs[-1]
    for index in range(slabs):
        q, span = piece_of(index, blk, rows // blk)
        left = h * parts * part + q * part
        for plane in range(2):
            value = keep[0, q, plane, span].astype(F32) + near[0, q, plane, span].astype(F32)
            for ref in refs[:terms]:
                value = value + ref[q, plane, span].astype(F32)
            held[index, plane] = (rhs[0, plane, span, left : left + part].astype(F32) - value).astype(BF)
    for mask, out in enumerate(outs):
        out[...] = held[place[0] ^ mask]


def reduce(h, place, root_rhs, keep, near, far, slabs, blk, after):
    part = keep.shape[4]
    return call(
        functools.partial(reduce_kernel, h, slabs, blk, len(far)), "interface_reduce",
        [place, root_rhs, keep, near, *far], [SMEM] + [VMEM] * (3 + len(far)),
        [shape_of((2, blk, part))] * slabs, [VMEM] * slabs, after, [pltpu.VMEM((slabs, 2, blk, part), BF)],
    )


def chain_kernel(slabs, count, place, *refs):
    pieces, mats, outs = refs[:slabs], refs[slabs : slabs + count], refs[slabs + count : 2 * slabs + count]
    held, solver = refs[2 * slabs + count :]
    me = place[0]
    for mask in range(slabs):
        held[mask] = pieces[mask][...]
    _, _, blk, part = held.shape
    tall = solver.shape[1]
    at = 0
    for mat in mats:
        for k in range(mat.shape[0] // tall):
            solver[at] = mat[k * tall : (k + 1) * tall]
            at += 1
    state = None
    for slab in range(slabs):
        at = me ^ slab
        field = held[at].reshape(2 * blk, part).astype(F32)
        packed = solver[at]
        if state is not None:
            terms = packed[2 * blk :].astype(F32)
            row = terms[0:1] + terms[1:2] + terms[2:3]
            scale = jnp.broadcast_to(row, (blk, blk)).T[:, :1]
            field = field - jnp.concatenate([scale, scale], axis=0) * state
        mat = stacked(packed[:blk], packed[blk : 2 * blk])
        high = field.astype(BF)
        if slab:
            low = (field - high.astype(F32)).astype(BF)
            both = dot(mat, jnp.concatenate([high, low], axis=1))
            state = both[:, :part] + both[:, part:]
        else:
            state = dot(mat, high)
        held[at] = state.astype(BF).reshape(2, blk, part)
    for mask, out in enumerate(outs):
        out[...] = held[mask]


def chain(place, pieces, mats, after):
    slabs = len(pieces)
    tall = mats[0].shape
    return call(
        functools.partial(chain_kernel, slabs, len(mats)), "sweep_chain", [place, *pieces, *mats],
        [SMEM] + [VMEM] * (slabs + len(mats)),
        [shape_of(pieces[0].shape)] * slabs, [VMEM] * slabs, after,
        [pltpu.VMEM((slabs,) + pieces[0].shape, BF), pltpu.VMEM((slabs,) + tall, BF)],
    )


def collect_kernel(slabs, place, *refs):
    pieces = refs[:slabs]
    own, held = refs[slabs:]
    _, blk, _ = pieces[0].shape
    rows = own.shape[2]
    for mask, piece in enumerate(pieces):
        held[mask] = piece[...]
    for index in range(slabs):
        q, span = piece_of(index, blk, rows // blk)
        piece = held[place[0] ^ index]
        own[q, 0, span] = piece[0]
        own[q, 1, span] = piece[1]


def collect(place, pieces, rows, after):
    slabs = len(pieces)
    _, blk, part = pieces[0].shape
    return call(
        functools.partial(collect_kernel, slabs), "interface_collect", [place, *pieces], [SMEM] + [VMEM] * slabs,
        shape_of((slabs // (rows // blk), 2, rows, part)), VMEM, after, [pltpu.VMEM((slabs, 2, blk, part), BF)],
    )


def relay_kernel(half, own, by_x, by_y, to_y, to_x, near):
    to_y[...] = by_x[:half]
    to_x[...] = by_y[half:]
    for at, ref in enumerate((own, by_x, by_y)):
        near[at] = ref[...]


def relay(h, own, by_x, by_y, after):
    parts = own.shape[0]
    half = parts // 2
    return call(
        functools.partial(relay_kernel, half), f"interface_relay_{h}", [own, by_x, by_y], [VMEM] * 3,
        [shape_of((half,) + own.shape[1:]), shape_of((parts - half,) + own.shape[1:]), shape_of((3,) + own.shape)],
        [VMEM] * 3, after,
    )


def backward_kernel(jobs, count, cap, fronts, owns, aliased, owners, place, rhs, mats, *refs):
    fields, refs = refs[:count], refs[count:]
    roots, refs = refs[:owns], refs[owns + aliased :]
    out, refs = refs[0], refs[1:]
    held, slots, sems = refs[-3:]
    leaves, wide, tall = mats.shape
    blk, cols = wide // 2, rhs.shape[4] // HALVES
    tall = tall - wide
    full = fronts * cap == leaves
    copies = []
    if owns:
        root, token, wider, root_sem = refs[:4]
        token[...] = jnp.zeros(token.shape, F32)
        parts, _, _, part = roots[0].shape
        for at, ref in enumerate(roots):
            for q in range(parts):
                left = (at * parts + q) * part
                for plane in range(2):
                    wider[plane, :, left : left + part] = ref[q, plane].astype(F32)
        copies.append((True, pltpu.make_async_copy(wider, root.at[0], root_sem)))
        copies[0][1].start()
    for slot in range(fronts * cap):
        slots[slot] = -1
    for leaf in range(leaves):
        first = (owners[leaf] ^ place[1]) * cap
        spot = first
        for rank in range(cap - 1):
            spot = jnp.where(slots[first + rank] >= 0, first + rank + 1, spot)
        slots[spot] = leaf

    def solve(at, h, name, field):
        here = pl.ds(h * cols, cols)
        vec = jnp.concatenate([rhs[0, 0, name, :, here], rhs[0, 1, name, :, here]], axis=0)
        result = dot(mats[name, :, :wide], vec) + dot(mats[name, :, wide:], field)
        held[at, 0] = result[:blk].astype(BF)
        held[at, 1] = result[blk:].astype(BF)

    batch = 4
    for low in range(0, len(jobs), batch):
        ready = len(copies)
        for job in range(low, min(len(jobs), low + batch)):
            h, dist, sources = jobs[job]
            mine = [fields[at] if lead is None else fields[at].at[lead] for at, lead in sources]
            columns = [ref[q].reshape(tall, ref.shape[3]) for ref in mine for q in range(ref.shape[0])]
            field = jnp.concatenate(columns, axis=1)
            for rank in range(cap):
                at, name = job * cap + rank, slots[dist * cap + rank]
                copy = pltpu.make_async_copy(
                    held.at[at], out.at[0, :, jnp.maximum(name, 0), :, pl.ds(h * cols, cols)], sems.at[at]
                )
                copies.append((name >= 0, copy))
                if full:
                    solve(at, h, name, field)
                else:
                    pl.when(name >= 0)(functools.partial(solve, at, h, name, field))
        for there, copy in copies[ready:]:
            if full:
                copy.start()
            else:
                pl.when(there)(copy.start)

    for at, (there, copy) in enumerate(copies):
        if full or (owns and at == 0):
            copy.wait()
        else:
            pl.when(there)(copy.wait)


def backward(name, owners, place, leaf_rhs, mats, jobs, fronts, roots, before, after):
    _, _, leaves, blk, width = leaf_rhs.shape
    cap, cols = -(-leaves // fronts), width // HALVES
    flat, named = [], []
    for h, dist, field in jobs:
        sources = []
        for value in field:
            value, lead = value if isinstance(value, tuple) else (value, None)
            known = [at for at, other in enumerate(flat) if other is value]
            if not known:
                flat.append(value)
            sources.append((known[0] if known else len(flat) - 1, lead))
        named.append((h, dist, sources))
    count = len(flat)
    flat = flat + roots
    aliased = [] if before is None else [before]
    outs, specs, scratch = [shape_of((1, 2, leaves, blk, width))], [HBM], []
    if roots:
        rows = roots[0].shape[2]
        outs, specs = outs + [shape_of((1, 2, rows, width), F32), shape_of((8, 128), F32)], [HBM, HBM, VMEM]
        scratch = [pltpu.VMEM((2, rows, width), F32), pltpu.SemaphoreType.DMA]
    return call(
        functools.partial(backward_kernel, named, count, cap, fronts, len(roots), len(aliased)), name,
        [owners, place, leaf_rhs, mats, *flat, *aliased], [SMEM, SMEM] + [VMEM] * (2 + len(flat)) + [HBM] * len(aliased),
        outs, specs, after,
        scratch
        + [
            pltpu.VMEM((len(jobs) * cap, 2, blk, cols), BF),
            pltpu.SMEM((fronts * cap,), jnp.int32),
            pltpu.SemaphoreType.DMA((len(jobs) * cap,)),
        ],
        {4 + len(flat): 0} if aliased else None,
    )


def body(leaf_rhs, leaf_inv, leaf_off, parent, ancestors, root_rhs, root_inv, coupling):
    fronts, slabs = lax.axis_size("front"), lax.axis_size("slab")
    rows, width = root_rhs.shape[2], root_rhs.shape[3]
    blk = leaf_rhs.shape[3]
    owners = parent.reshape(-1)
    place = jnp.stack([lax.axis_index("slab"), lax.axis_index("front")]).astype(jnp.int32)
    pairs = fronts // 2
    parts = slabs // (rows // blk)
    part = width // HALVES // parts
    square = pairs == 4

    def start_forward(h, after):
        keep, send = forward(
            h, owners, place, leaf_rhs, leaf_inv, leaf_off, ancestors, fronts, rows, part, after
        )
        return keep, crossed(send, "front", 1)

    def send_first(keep, near, after):
        if not square:
            sums = first_sums([(j, 0, parts) for j in range(1, pairs)], keep, near, after)
            return sums[0], [crossed(value, "front", 2 * (j + 1)) for j, value in enumerate(sums)]
        to_x, to_y = first_sums([(3, 0, parts // 2), (3, parts // 2, parts)], keep, near, after)
        return to_x, [crossed(to_x, "front", 2), crossed(to_y, "front", 4)]

    def send_second(h, keep, near, got, after):
        if not square:
            return got[0], got
        to_x, to_y = second_sums(h, parts // 2, keep, near, *got, after)
        return to_x, [crossed(to_x, "front", 2), crossed(to_y, "front", 4)]

    def over_slabs(values):
        return [values[0]] + [crossed(values[mask], "slab", mask) for mask in range(1, slabs)]

    def share_first(own):
        return [crossed(own, "front", mask) for mask in ((2, 4) if square else range(2, fronts, 2))]

    def share_second(h, own, got, after):
        if not square:
            return got[0], []
        to_y, to_x, held = relay(h, own, *got, after)
        return to_y, [crossed(to_y, "front", 4), crossed(to_x, "front", 2), crossed(held, "front", 1)]

    def near_jobs(h, own, got, more):
        mine = [own] + got
        if square:
            fields = [field for at, value in enumerate(mine) for field in ([value], [(more[2], at)])]
        else:
            fields = [[field] for value in mine for field in (value, crossed(value, "front", 1))]
        return [(h, dist, field) for dist, field in enumerate(fields)]

    def far_jobs(mores, after):
        far = join([value for more in mores for value in more[:2]], after, "interface_join")
        there = crossed(far, "front", 1)
        jobs = []
        for h in range(len(mores)):
            span = pl.ds(h * parts, parts)
            jobs += [(h, fronts - 2, [(far, span)]), (h, fronts - 1, [(there, span)])]
        return jobs

    keep0, near0 = start_forward(0, ())
    token, got0 = send_first(keep0, near0, ())
    keep1, near1 = start_forward(1, [token])
    token, far0 = send_second(0, keep0, near0, got0, [keep1])
    token, got1 = send_first(keep1, near1, [token])
    same, other = pack(place, root_inv, coupling, [token])
    have, step = [same, crossed(other, "slab", 1)], 2
    while step < slabs:
        token = join(have, [token])
        have = have + [crossed(token, "slab", step)]
        step *= 2
    token, far1 = send_second(1, keep1, near1, got1, [token])
    pieces0 = reduce(0, place, root_rhs, keep0, near0, far0, slabs, blk, [token])
    pieces1 = reduce(1, place, root_rhs, keep1, near1, far1, slabs, blk, [pieces0[0]])
    solved0 = chain(place, over_slabs(pieces0), have, [pieces1[0]])
    solved1 = chain(place, over_slabs(pieces1), have, [solved0[0]])
    own0 = collect(place, over_slabs(solved0), rows, [solved1[0]])
    got0 = share_first(own0)
    own1 = collect(place, over_slabs(solved1), rows, [own0])
    got1 = share_first(own1)
    folded = fold(leaf_inv, leaf_off, ancestors, rows, [own1])
    token, more0 = share_second(0, own0, got0, [folded])
    token, more1 = share_second(1, own1, got1, [token])
    leaf_sol, root_sol, token = backward(
        "leaf_backward", owners, place, leaf_rhs, folded, near_jobs(0, own0, got0, more0), fronts, [own0, own1], None, [token]
    )
    (leaf_sol,) = backward(
        "leaf_backward", owners, place, leaf_rhs, folded, near_jobs(1, own1, got1, more1), fronts, [], leaf_sol, ()
    )
    if square:
        jobs = far_jobs((more0, more1), [token])
        (leaf_sol,) = backward("leaf_backward", owners, place, leaf_rhs, folded, jobs, fronts, [], leaf_sol, ())
    return leaf_sol, root_sol


def solution(mesh):
    in_specs = (
        P("slab", None, "front", None, None),
        P("slab", "front", None, None, None),
        P("slab", "front", None, None, None),
        P("slab", "front", None),
        P("slab", "front", None),
        P("slab", None, "front", None),
        P("slab", "front", None, None, None),
        P("slab", "front"),
    )
    out_specs = (P("slab", None, "front", None, None), P("slab", None, "front", None))
    return jax.shard_map(body, mesh=mesh, in_specs=in_specs, out_specs=out_specs, check_vma=False)
```

```python
import functools

import jax
import jax.numpy as jnp
from jax import lax
from jax.experimental import pallas as pl
from jax.experimental.pallas import tpu as pltpu
from jax.sharding import PartitionSpec as P

HALVES = 2
FIRST_ROOM = 51
BRIEF = ("solve_join", "interface_first", "interface_join", "interface_second_1", "interface_relay_0")
BF = jnp.bfloat16
F32 = jnp.float32
VMEM = pl.BlockSpec(memory_space=pltpu.VMEM)
SMEM = pl.BlockSpec(memory_space=pltpu.SMEM)
HBM = pl.BlockSpec(memory_space=pltpu.HBM)
ANY = pl.BlockSpec(memory_space=pl.ANY)


def shape_of(shape, dtype=BF):
    return jax.ShapeDtypeStruct(shape, dtype)


def call(kernel, name, ins, in_specs, outs, out_specs, after=(), scratch=(), aliases=None, room=24):
    count, extra = len(ins), len(after)

    def wrapped(*refs):
        kernel(*refs[:count], *refs[count + extra :])

    return pl.pallas_call(
        wrapped,
        in_specs=list(in_specs) + [ANY] * extra,
        out_specs=out_specs,
        out_shape=outs,
        scratch_shapes=list(scratch),
        input_output_aliases=aliases or {},
        compiler_params=pltpu.CompilerParams(vmem_limit_bytes=room * 1024 * 1024),
        cost_estimate=pl.CostEstimate(flops=1 if name in BRIEF else 10**10, bytes_accessed=1, transcendentals=0),
        name=name,
    )(*ins, *after)


def crossed(x, axis, mask):
    return lax.ppermute(x, axis, [(i, i ^ mask) for i in range(lax.axis_size(axis))])


def stacked(real, imag):
    return jnp.concatenate(
        [jnp.concatenate([real, -imag], axis=1), jnp.concatenate([imag, real], axis=1)], axis=0
    )


def dot(a, b, dims=((1,), (0,)), precision=None):
    return lax.dot_general(a, b, (dims, ((), ())), precision=precision, preferred_element_type=F32)


def table_of(anc_row, rows):
    ids = lax.broadcasted_iota(jnp.int32, (rows, anc_row.shape[1]), 0)
    return (ids == anc_row).astype(F32).astype(BF)


def forward_kernel(h, group, cap, owners, place, rhs, inv, off, anc, keep, send, last, part, ids, seen, *rest):
    leaves, blk, cols = rhs.shape[2], rhs.shape[3], part.shape[4]
    fronts, rows, width = part.shape[0], keep.shape[3], keep.shape[4]
    me = place[1]
    if rest:
        vecs, invs, offs, ancs, sems = rest
        small = pltpu.make_async_copy(anc.at[0], ancs, sems.at[leaves // group, 0])

        def copies(at):
            span = pl.ds(at * group, group)
            return (
                pltpu.make_async_copy(inv.at[0, span], invs.at[span], sems.at[at, 0]),
                pltpu.make_async_copy(rhs.at[0, :, span, :, pl.ds(h * cols, cols)], vecs.at[:, span], sems.at[at, 1]),
                pltpu.make_async_copy(off.at[0, span], offs.at[span], sems.at[at, 2]),
            )

        for at in range(leaves // group):
            for copy in copies(at):
                copy.start()
        small.start()
    else:
        vecs, invs, offs, ancs = rhs.at[0, :, :, :, pl.ds(h * cols, cols)], inv.at[0], off.at[0], anc.at[0]
    ids[...] = jnp.full(ids.shape, -1, jnp.int32)
    for dist in range(fronts):
        seen[dist] = 0
    if rest:
        small.wait()

    for at in range(leaves // group):
        for copy in copies(at) if rest else ():
            copy.wait()
        names = [at * group + j for j in range(group)]
        values = []
        for leaf in names:
            vec = jnp.concatenate([vecs[0, leaf], vecs[1, leaf]], axis=0)
            values.append(dot(stacked(invs[leaf, 0], invs[leaf, 1]), vec).astype(BF))
        moved = [dot(stacked(offs[leaf, 0], offs[leaf, 1]), value).astype(BF) for leaf, value in zip(names, values)]
        for leaf, shift in zip(names, moved):
            dist = owners[leaf] ^ me
            rank = seen[dist]
            seen[dist] = rank + 1
            part[dist, 0, rank] = shift[:blk]
            part[dist, 1, rank] = shift[blk:]
            ids[pl.ds(dist * cap + rank, 1), :] = ancs[pl.ds(leaf, 1), :]

    for dist in range(fronts if fronts * cap > leaves else 0):
        for rank in range(cap):

            @pl.when(seen[dist] <= rank)
            def _(dist=dist, rank=rank):
                part[dist, 0, rank] = jnp.zeros((blk, cols), BF)
                part[dist, 1, rank] = jnp.zeros((blk, cols), BF)

    for dist in range(fronts):
        row = jnp.concatenate([ids[dist * cap + rank : dist * cap + rank + 1, :] for rank in range(cap)], axis=1)
        table = table_of(row, rows)
        out = keep if dist % 2 == 0 else send if dist < fronts - 1 else last
        spot = 0 if dist == fronts - 1 else dist // 2
        for plane in range(2):
            value = dot(table, part[dist, plane].reshape(cap * blk, cols)).astype(BF)
            for q in range(cols // width):
                out[spot, q, plane] = value[:, q * width : (q + 1) * width]


def forward(h, owners, place, leaf_rhs, leaf_inv, leaf_off, ancestors, fronts, rows, part, after):
    _, _, leaves, blk, width = leaf_rhs.shape
    cols = width // HALVES
    cap = -(-leaves // fronts)
    group = 8
    block = (cols // part, 2, rows, part)
    scratch = [
        pltpu.VMEM((fronts, 2, cap, blk, cols), BF),
        pltpu.VMEM((fronts * cap, blk), jnp.int32),
        pltpu.SMEM((fronts,), jnp.int32),
    ]
    if h == 0:
        scratch += [
            pltpu.VMEM((2, leaves, blk, cols), BF),
            pltpu.VMEM((leaves, 2, blk, blk), BF),
            pltpu.VMEM((leaves, 2, blk, blk), BF),
            pltpu.VMEM((leaves, blk), jnp.int32),
            pltpu.SemaphoreType.DMA((leaves // group + 1, 3)),
        ]
    return call(
        functools.partial(forward_kernel, h, group, cap),
        "leaf_forward",
        [owners, place, leaf_rhs, leaf_inv, leaf_off, ancestors],
        [SMEM, SMEM] + [VMEM if h else HBM] * 4,
        [shape_of((fronts // 2,) + block), shape_of((fronts // 2 - 1,) + block), shape_of((1,) + block)],
        [VMEM, VMEM, VMEM],
        after,
        scratch,
        room=24 if h else FIRST_ROOM,
    )


def fold_kernel(inv, off, anc, out):
    leaves, _, blk, _ = inv.shape[1:]
    wide = 2 * blk
    rows = (out.shape[2] - wide) // 2

    def one(leaf, carry):
        mat = jnp.concatenate([inv[0, leaf, 0], inv[0, leaf, 1]], axis=1)
        real, imag = off[0, leaf, 0], off[0, leaf, 1]
        other = jnp.concatenate([jnp.concatenate([real, -imag], axis=1), jnp.concatenate([imag, real], axis=1)], axis=0)
        both = dot(mat, other, ((1,), (1,))).astype(BF)
        table = table_of(anc[0, pl.ds(leaf, 1), :], rows)
        real = dot(both[:, :blk], table, ((1,), (1,))).astype(BF)
        imag = dot(both[:, blk:], table, ((1,), (1,))).astype(BF)
        out[leaf, :, :wide] = stacked(inv[0, leaf, 0], inv[0, leaf, 1])
        out[leaf, :blk, wide : wide + rows] = -real
        out[leaf, :blk, wide + rows :] = imag
        out[leaf, blk:, wide : wide + rows] = -imag
        out[leaf, blk:, wide + rows :] = -real
        return carry

    lax.fori_loop(0, leaves, one, 0, unroll=leaves)


def fold(leaf_inv, leaf_off, ancestors, rows, after):
    _, leaves, _, blk, _ = leaf_inv.shape
    return call(
        fold_kernel, "leaf_fold", [leaf_inv, leaf_off, ancestors], [VMEM] * 3,
        shape_of((leaves, 2 * blk, 2 * blk + 2 * rows)), VMEM, after,
    )


def pack_kernel(place, inv, cpl, same, other):
    blocks, blk = inv.shape[1], inv.shape[3]
    for kind, out in enumerate((same, other)):
        block = (place[0] % blocks) ^ kind
        out[:blk] = inv[0, block, 0].astype(BF)
        out[blk : 2 * blk] = inv[0, block, 1].astype(BF)
        rest = jnp.broadcast_to(cpl[0, pl.ds(block, 1), :], (16, blk))
        row = lax.broadcasted_iota(jnp.int32, (16, blk), 0)
        value = jnp.zeros((16, blk), F32)
        for term in range(3):
            piece = rest.astype(BF).astype(F32)
            value = jnp.where(row == term, piece, value)
            rest = rest - piece
        out[2 * blk :] = value.astype(BF)


def pack(place, root_inv, coupling, after):
    _, blocks, _, blk, _ = root_inv.shape
    shape = shape_of((2 * blk + 16, blk))
    return call(
        pack_kernel, "solve_pack", [place, root_inv, coupling.reshape(1, blocks, blk)], [SMEM, VMEM, VMEM],
        [shape, shape], [VMEM, VMEM], after,
    )


def join_kernel(*refs):
    *parts, out = refs
    at = 0
    for ref in parts:
        out[at : at + ref.shape[0]] = ref[...]
        at += ref.shape[0]


def join(parts, after, name="solve_join"):
    rows = sum(part.shape[0] for part in parts)
    return call(
        join_kernel, name, parts, [VMEM] * len(parts), shape_of((rows,) + parts[0].shape[1:]), VMEM, after
    )


def first_kernel(names, keep, *refs):
    nears, outs = refs[: -len(names)], refs[-len(names) :]
    for (j, first, last), out in zip(names, outs):
        near, at = (nears[-1], 0) if j == keep.shape[0] - 1 else (nears[0], j)
        out[...] = (keep[j, first:last].astype(F32) + near[at, first:last].astype(F32)).astype(BF)


def first_sums(names, keep, nears, after):
    return call(
        functools.partial(first_kernel, names), "interface_first", [keep, *nears], [VMEM] * (1 + len(nears)),
        [shape_of((last - first,) + keep.shape[2:]) for _, first, last in names], [VMEM] * len(names), after,
    )


def second_kernel(half, keep, near, by_x, by_y, out_x, out_y):
    parts = keep.shape[1]
    for j, out, extra, first, last in ((1, out_x, by_y, half, parts), (2, out_y, by_x, 0, half)):
        for q in range(parts):
            value = keep[j, q].astype(F32) + near[j, q].astype(F32)
            if first <= q < last:
                value = value + extra[q - first].astype(F32)
            out[q] = value.astype(BF)


def second_sums(h, half, keep, near, by_x, by_y, after):
    shape = shape_of(keep.shape[1:])
    return call(
        functools.partial(second_kernel, half), f"interface_second_{h}", [keep, near, by_x, by_y], [VMEM] * 4,
        [shape, shape], [VMEM] * 2, after,
    )


def piece_of(index, blk, blocks):
    low = (index % blocks) * blk
    return index // blocks, slice(low, low + blk)


def reduce_kernel(h, slabs, blk, terms, place, rhs, keep, near, *refs):
    _, parts, _, rows, part = keep.shape
    outs, held = refs[terms:-1], refs[-1]
    for index in range(slabs):
        q, span = piece_of(index, blk, rows // blk)
        left = h * parts * part + q * part
        for plane in range(2):
            value = keep[0, q, plane, span].astype(F32) + near[0, q, plane, span].astype(F32)
            for ref in refs[:terms]:
                value = value + ref[q, plane, span].astype(F32)
            held[index, plane] = (rhs[0, plane, span, left : left + part].astype(F32) - value).astype(BF)
    for mask, out in enumerate(outs):
        out[...] = held[place[0] ^ mask]


def reduce(h, place, root_rhs, keep, near, far, slabs, blk, after):
    part = keep.shape[4]
    return call(
        functools.partial(reduce_kernel, h, slabs, blk, len(far)), "interface_reduce",
        [place, root_rhs, keep, near, *far], [SMEM] + [VMEM] * (3 + len(far)),
        [shape_of((2, blk, part))] * slabs, [VMEM] * slabs, after, [pltpu.VMEM((slabs, 2, blk, part), BF)],
    )


def chain_kernel(slabs, count, place, *refs):
    pieces, mats, outs = refs[:slabs], refs[slabs : slabs + count], refs[slabs + count : 2 * slabs + count]
    held, solver = refs[2 * slabs + count :]
    me = place[0]
    for mask in range(slabs):
        held[mask] = pieces[mask][...]
    _, _, blk, part = held.shape
    tall = solver.shape[1]
    at = 0
    for mat in mats:
        for k in range(mat.shape[0] // tall):
            solver[at] = mat[k * tall : (k + 1) * tall]
            at += 1
    state = None
    for slab in range(slabs):
        at = me ^ slab
        field = held[at].reshape(2 * blk, part).astype(F32)
        packed = solver[at]
        if state is not None:
            terms = packed[2 * blk :].astype(F32)
            row = terms[0:1] + terms[1:2] + terms[2:3]
            scale = jnp.broadcast_to(row, (blk, blk)).T[:, :1]
            field = field - jnp.concatenate([scale, scale], axis=0) * state
        mat = stacked(packed[:blk], packed[blk : 2 * blk])
        high = field.astype(BF)
        if slab:
            low = (field - high.astype(F32)).astype(BF)
            both = dot(mat, jnp.concatenate([high, low], axis=1))
            state = both[:, :part] + both[:, part:]
        else:
            state = dot(mat, high)
        held[at] = state.astype(BF).reshape(2, blk, part)
    for mask, out in enumerate(outs):
        out[...] = held[mask]


def chain(place, pieces, mats, after):
    slabs = len(pieces)
    tall = mats[0].shape
    return call(
        functools.partial(chain_kernel, slabs, len(mats)), "sweep_chain", [place, *pieces, *mats],
        [SMEM] + [VMEM] * (slabs + len(mats)),
        [shape_of(pieces[0].shape)] * slabs, [VMEM] * slabs, after,
        [pltpu.VMEM((slabs,) + pieces[0].shape, BF), pltpu.VMEM((slabs,) + tall, BF)],
    )


def collect_kernel(slabs, place, *refs):
    pieces = refs[:slabs]
    own, held = refs[slabs:]
    _, blk, _ = pieces[0].shape
    rows = own.shape[2]
    for mask, piece in enumerate(pieces):
        held[mask] = piece[...]
    for index in range(slabs):
        q, span = piece_of(index, blk, rows // blk)
        piece = held[place[0] ^ index]
        own[q, 0, span] = piece[0]
        own[q, 1, span] = piece[1]


def collect(place, pieces, rows, after):
    slabs = len(pieces)
    _, blk, part = pieces[0].shape
    return call(
        functools.partial(collect_kernel, slabs), "interface_collect", [place, *pieces], [SMEM] + [VMEM] * slabs,
        shape_of((slabs // (rows // blk), 2, rows, part)), VMEM, after, [pltpu.VMEM((slabs, 2, blk, part), BF)],
    )


def relay_kernel(half, own, by_x, by_y, to_y, to_x, near):
    to_y[...] = by_x[:half]
    to_x[...] = by_y[half:]
    for at, ref in enumerate((own, by_x, by_y)):
        near[at] = ref[...]


def relay(h, own, by_x, by_y, after):
    parts = own.shape[0]
    half = parts // 2
    return call(
        functools.partial(relay_kernel, half), f"interface_relay_{h}", [own, by_x, by_y], [VMEM] * 3,
        [shape_of((half,) + own.shape[1:]), shape_of((parts - half,) + own.shape[1:]), shape_of((3,) + own.shape)],
        [VMEM] * 3, after,
    )


def backward_kernel(jobs, count, cap, fronts, owns, aliased, owners, place, rhs, mats, *refs):
    fields, refs = refs[:count], refs[count:]
    roots, refs = refs[:owns], refs[owns + aliased :]
    out, refs = refs[0], refs[1:]
    held, slots, sems = refs[-3:]
    leaves, wide, tall = mats.shape
    blk, cols = wide // 2, rhs.shape[4] // HALVES
    tall = tall - wide
    full = fronts * cap == leaves
    copies = []
    if owns:
        root, token, wider, root_sem = refs[:4]
        token[...] = jnp.zeros(token.shape, F32)
        parts, _, _, part = roots[0].shape
        for at, ref in enumerate(roots):
            for q in range(parts):
                left = (at * parts + q) * part
                for plane in range(2):
                    wider[plane, :, left : left + part] = ref[q, plane].astype(F32)
        copies.append((True, pltpu.make_async_copy(wider, root.at[0], root_sem)))
        copies[0][1].start()
    for slot in range(fronts * cap):
        slots[slot] = -1
    for leaf in range(leaves):
        first = (owners[leaf] ^ place[1]) * cap
        spot = first
        for rank in range(cap - 1):
            spot = jnp.where(slots[first + rank] >= 0, first + rank + 1, spot)
        slots[spot] = leaf

    def solve(at, h, name, field):
        here = pl.ds(h * cols, cols)
        vec = jnp.concatenate([rhs[0, 0, name, :, here], rhs[0, 1, name, :, here]], axis=0)
        result = dot(mats[name, :, :wide], vec) + dot(mats[name, :, wide:], field)
        held[at, 0] = result[:blk].astype(BF)
        held[at, 1] = result[blk:].astype(BF)

    batch = 4
    for low in range(0, len(jobs), batch):
        ready = len(copies)
        for job in range(low, min(len(jobs), low + batch)):
            h, dist, sources = jobs[job]
            mine = [fields[at] if lead is None else fields[at].at[lead] for at, lead in sources]
            columns = [ref[q].reshape(tall, ref.shape[3]) for ref in mine for q in range(ref.shape[0])]
            field = jnp.concatenate(columns, axis=1)
            for rank in range(cap):
                at, name = job * cap + rank, slots[dist * cap + rank]
                copy = pltpu.make_async_copy(
                    held.at[at], out.at[0, :, jnp.maximum(name, 0), :, pl.ds(h * cols, cols)], sems.at[at]
                )
                copies.append((name >= 0, copy))
                if full:
                    solve(at, h, name, field)
                else:
                    pl.when(name >= 0)(functools.partial(solve, at, h, name, field))
        for there, copy in copies[ready:]:
            if full:
                copy.start()
            else:
                pl.when(there)(copy.start)

    for at, (there, copy) in enumerate(copies):
        if full or (owns and at == 0):
            copy.wait()
        else:
            pl.when(there)(copy.wait)


def backward(name, owners, place, leaf_rhs, mats, jobs, fronts, roots, before, after):
    _, _, leaves, blk, width = leaf_rhs.shape
    cap, cols = -(-leaves // fronts), width // HALVES
    flat, named = [], []
    for h, dist, field in jobs:
        sources = []
        for value in field:
            value, lead = value if isinstance(value, tuple) else (value, None)
            known = [at for at, other in enumerate(flat) if other is value]
            if not known:
                flat.append(value)
            sources.append((known[0] if known else len(flat) - 1, lead))
        named.append((h, dist, sources))
    count = len(flat)
    flat = flat + roots
    aliased = [] if before is None else [before]
    outs, specs, scratch = [shape_of((1, 2, leaves, blk, width))], [HBM], []
    if roots:
        rows = roots[0].shape[2]
        outs, specs = outs + [shape_of((1, 2, rows, width), F32), shape_of((8, 128), F32)], [HBM, HBM, VMEM]
        scratch = [pltpu.VMEM((2, rows, width), F32), pltpu.SemaphoreType.DMA]
    return call(
        functools.partial(backward_kernel, named, count, cap, fronts, len(roots), len(aliased)), name,
        [owners, place, leaf_rhs, mats, *flat, *aliased], [SMEM, SMEM] + [VMEM] * (2 + len(flat)) + [HBM] * len(aliased),
        outs, specs, after,
        scratch
        + [
            pltpu.VMEM((len(jobs) * cap, 2, blk, cols), BF),
            pltpu.SMEM((fronts * cap,), jnp.int32),
            pltpu.SemaphoreType.DMA((len(jobs) * cap,)),
        ],
        {4 + len(flat): 0} if aliased else None,
    )


def body(leaf_rhs, leaf_inv, leaf_off, parent, ancestors, root_rhs, root_inv, coupling):
    fronts, slabs = lax.axis_size("front"), lax.axis_size("slab")
    rows, width = root_rhs.shape[2], root_rhs.shape[3]
    blk = leaf_rhs.shape[3]
    owners = parent.reshape(-1)
    place = jnp.stack([lax.axis_index("slab"), lax.axis_index("front")]).astype(jnp.int32)
    pairs = fronts // 2
    parts = slabs // (rows // blk)
    part = width // HALVES // parts
    square = pairs == 4

    def start_forward(h, after):
        keep, send, last = forward(
            h, owners, place, leaf_rhs, leaf_inv, leaf_off, ancestors, fronts, rows, part, after
        )
        last = crossed(last, "front", 1)
        return keep, (crossed(send, "front", 1), last)

    def send_first(keep, near, after):
        if not square:
            sums = first_sums([(j, 0, parts) for j in range(1, pairs)], keep, near, after)
            return sums[0], [crossed(value, "front", 2 * (j + 1)) for j, value in enumerate(sums)]
        to_x, to_y = first_sums([(3, 0, parts // 2), (3, parts // 2, parts)], keep, near[1:], after)
        return to_x, [crossed(to_x, "front", 2), crossed(to_y, "front", 4)]

    def send_second(h, keep, near, got, after):
        if not square:
            return got[0], got
        to_x, to_y = second_sums(h, parts // 2, keep, near[0], *got, after)
        return to_x, [crossed(to_x, "front", 2), crossed(to_y, "front", 4)]

    def over_slabs(values):
        return [values[0]] + [crossed(values[mask], "slab", mask) for mask in range(1, slabs)]

    def share_first(own):
        return [crossed(own, "front", mask) for mask in ((2, 4) if square else range(2, fronts, 2))]

    def share_second(h, own, got, after):
        if not square:
            return got[0], []
        to_y, to_x, held = relay(h, own, *got, after)
        return to_y, [crossed(to_y, "front", 4), crossed(to_x, "front", 2), crossed(held, "front", 1)]

    def near_jobs(h, own, got, more):
        mine = [own] + got
        if square:
            fields = [field for at, value in enumerate(mine) for field in ([value], [(more[2], at)])]
        else:
            fields = [[field] for value in mine for field in (value, crossed(value, "front", 1))]
        return [(h, dist, field) for dist, field in enumerate(fields)]

    def far_jobs(mores, after):
        far = join([value for more in mores for value in more[:2]], after, "interface_join")
        there = crossed(far, "front", 1)
        jobs = []
        for h in range(len(mores)):
            span = pl.ds(h * parts, parts)
            jobs += [(h, fronts - 2, [(far, span)]), (h, fronts - 1, [(there, span)])]
        return jobs

    keep0, near0 = start_forward(0, ())
    same, other = pack(place, root_inv, coupling, [keep0])
    have, step = [same, crossed(other, "slab", 1)], 2
    token, got0 = send_first(keep0, near0, [same])
    keep1, near1 = start_forward(1, [token, have[1]])
    token, far0 = send_second(0, keep0, near0, got0, [keep1])
    token, got1 = send_first(keep1, near1, [token])
    while step < slabs:
        token = join(have, [token])
        have = have + [crossed(token, "slab", step)]
        step *= 2
    token, far1 = send_second(1, keep1, near1, got1, [token])
    pieces0 = reduce(0, place, root_rhs, keep0, near0[0], far0, slabs, blk, [token])
    pieces1 = reduce(1, place, root_rhs, keep1, near1[0], far1, slabs, blk, [pieces0[0]])
    solved0 = chain(place, over_slabs(pieces0), have, [pieces1[0]])
    solved1 = chain(place, over_slabs(pieces1), have, [solved0[0]])
    own0 = collect(place, over_slabs(solved0), rows, [solved1[0]])
    got0 = share_first(own0)
    own1 = collect(place, over_slabs(solved1), rows, [own0])
    got1 = share_first(own1)
    folded = fold(leaf_inv, leaf_off, ancestors, rows, [own1])
    token, more0 = share_second(0, own0, got0, [folded])
    token, more1 = share_second(1, own1, got1, [token])
    leaf_sol, root_sol, token = backward(
        "leaf_backward", owners, place, leaf_rhs, folded, near_jobs(0, own0, got0, more0), fronts, [own0, own1], None, [token]
    )
    (leaf_sol,) = backward(
        "leaf_backward", owners, place, leaf_rhs, folded, near_jobs(1, own1, got1, more1), fronts, [], leaf_sol, ()
    )
    if square:
        jobs = far_jobs((more0, more1), [token])
        (leaf_sol,) = backward("leaf_backward", owners, place, leaf_rhs, folded, jobs, fronts, [], leaf_sol, ())
    return leaf_sol, root_sol


def solution(mesh):
    in_specs = (
        P("slab", None, "front", None, None),
        P("slab", "front", None, None, None),
        P("slab", "front", None, None, None),
        P("slab", "front", None),
        P("slab", "front", None),
        P("slab", None, "front", None),
        P("slab", "front", None, None, None),
        P("slab", "front"),
    )
    out_specs = (P("slab", None, "front", None, None), P("slab", None, "front", None))
    return jax.shard_map(body, mesh=mesh, in_specs=in_specs, out_specs=out_specs, check_vma=False)
```

```python
import functools

import jax
import jax.numpy as jnp
from jax import lax
from jax.experimental import pallas as pl
from jax.experimental.pallas import tpu as pltpu
from jax.sharding import PartitionSpec as P

HALVES = 2
FIRST_ROOM = 51
BRIEF = ("solve_join", "interface_first", "interface_join", "interface_second_1", "interface_relay_0")
BF = jnp.bfloat16
F32 = jnp.float32
VMEM = pl.BlockSpec(memory_space=pltpu.VMEM)
SMEM = pl.BlockSpec(memory_space=pltpu.SMEM)
HBM = pl.BlockSpec(memory_space=pltpu.HBM)
ANY = pl.BlockSpec(memory_space=pl.ANY)


def shape_of(shape, dtype=BF):
    return jax.ShapeDtypeStruct(shape, dtype)


def call(kernel, name, ins, in_specs, outs, out_specs, after=(), scratch=(), aliases=None, room=24):
    count, extra = len(ins), len(after)

    def wrapped(*refs):
        kernel(*refs[:count], *refs[count + extra :])

    return pl.pallas_call(
        wrapped,
        in_specs=list(in_specs) + [ANY] * extra,
        out_specs=out_specs,
        out_shape=outs,
        scratch_shapes=list(scratch),
        input_output_aliases=aliases or {},
        compiler_params=pltpu.CompilerParams(vmem_limit_bytes=room * 1024 * 1024),
        cost_estimate=pl.CostEstimate(flops=1 if name in BRIEF else 10**10, bytes_accessed=1, transcendentals=0),
        name=name,
    )(*ins, *after)


def crossed(x, axis, mask):
    return lax.ppermute(x, axis, [(i, i ^ mask) for i in range(lax.axis_size(axis))])


def stacked(real, imag):
    return jnp.concatenate(
        [jnp.concatenate([real, -imag], axis=1), jnp.concatenate([imag, real], axis=1)], axis=0
    )


def dot(a, b, dims=((1,), (0,)), precision=None):
    return lax.dot_general(a, b, (dims, ((), ())), precision=precision, preferred_element_type=F32)


def table_of(anc_row, rows):
    ids = lax.broadcasted_iota(jnp.int32, (rows, anc_row.shape[1]), 0)
    return (ids == anc_row).astype(F32).astype(BF)


def forward_kernel(h, group, cap, owners, place, rhs, inv, off, anc, keep, send, last, part, ids, seen, *rest):
    leaves, blk, cols = rhs.shape[2], rhs.shape[3], part.shape[4]
    fronts, rows, width = part.shape[0], keep.shape[3], keep.shape[4]
    me = place[1]
    if rest:
        vecs, invs, offs, ancs, sems = rest
        small = pltpu.make_async_copy(anc.at[0], ancs, sems.at[leaves // group, 0])

        def copies(at):
            span = pl.ds(at * group, group)
            return (
                pltpu.make_async_copy(inv.at[0, span], invs.at[span], sems.at[at, 0]),
                pltpu.make_async_copy(rhs.at[0, :, span, :, pl.ds(h * cols, cols)], vecs.at[:, span], sems.at[at, 1]),
                pltpu.make_async_copy(off.at[0, span], offs.at[span], sems.at[at, 2]),
            )

        for at in range(leaves // group):
            for copy in copies(at):
                copy.start()
        small.start()
    else:
        vecs, invs, offs, ancs = rhs.at[0, :, :, :, pl.ds(h * cols, cols)], inv.at[0], off.at[0], anc.at[0]
    ids[...] = jnp.full(ids.shape, -1, jnp.int32)
    for dist in range(fronts):
        seen[dist] = 0
    if rest:
        small.wait()

    for at in range(leaves // group):
        for copy in copies(at) if rest else ():
            copy.wait()
        names = [at * group + j for j in range(group)]
        values = []
        for leaf in names:
            vec = jnp.concatenate([vecs[0, leaf], vecs[1, leaf]], axis=0)
            values.append(dot(stacked(invs[leaf, 0], invs[leaf, 1]), vec).astype(BF))
        moved = [dot(stacked(offs[leaf, 0], offs[leaf, 1]), value).astype(BF) for leaf, value in zip(names, values)]
        for leaf, shift in zip(names, moved):
            dist = owners[leaf] ^ me
            rank = seen[dist]
            seen[dist] = rank + 1
            part[dist, 0, rank] = shift[:blk]
            part[dist, 1, rank] = shift[blk:]
            ids[pl.ds(dist * cap + rank, 1), :] = ancs[pl.ds(leaf, 1), :]

    for dist in range(fronts if fronts * cap > leaves else 0):
        for rank in range(cap):

            @pl.when(seen[dist] <= rank)
            def _(dist=dist, rank=rank):
                part[dist, 0, rank] = jnp.zeros((blk, cols), BF)
                part[dist, 1, rank] = jnp.zeros((blk, cols), BF)

    for dist in range(fronts):
        row = jnp.concatenate([ids[dist * cap + rank : dist * cap + rank + 1, :] for rank in range(cap)], axis=1)
        table = table_of(row, rows)
        out = keep if dist % 2 == 0 else send if dist < fronts - 1 else last
        spot = 0 if dist == fronts - 1 else dist // 2
        for plane in range(2):
            value = dot(table, part[dist, plane].reshape(cap * blk, cols)).astype(BF)
            for q in range(cols // width):
                out[spot, q, plane] = value[:, q * width : (q + 1) * width]


def forward(h, owners, place, leaf_rhs, leaf_inv, leaf_off, ancestors, fronts, rows, part, after):
    _, _, leaves, blk, width = leaf_rhs.shape
    cols = width // HALVES
    cap = -(-leaves // fronts)
    group = 8
    block = (cols // part, 2, rows, part)
    scratch = [
        pltpu.VMEM((fronts, 2, cap, blk, cols), BF),
        pltpu.VMEM((fronts * cap, blk), jnp.int32),
        pltpu.SMEM((fronts,), jnp.int32),
    ]
    if h == 0:
        scratch += [
            pltpu.VMEM((2, leaves, blk, cols), BF),
            pltpu.VMEM((leaves, 2, blk, blk), BF),
            pltpu.VMEM((leaves, 2, blk, blk), BF),
            pltpu.VMEM((leaves, blk), jnp.int32),
            pltpu.SemaphoreType.DMA((leaves // group + 1, 3)),
        ]
    return call(
        functools.partial(forward_kernel, h, group, cap),
        "leaf_forward",
        [owners, place, leaf_rhs, leaf_inv, leaf_off, ancestors],
        [SMEM, SMEM] + [VMEM if h else HBM] * 4,
        [shape_of((fronts // 2,) + block), shape_of((fronts // 2 - 1,) + block), shape_of((1,) + block)],
        [VMEM, VMEM, VMEM],
        after,
        scratch,
        room=24 if h else FIRST_ROOM,
    )


def fold_kernel(inv, off, anc, out):
    leaves, _, blk, _ = inv.shape[1:]
    wide = 2 * blk
    rows = (out.shape[2] - wide) // 2

    def one(leaf, carry):
        mat = jnp.concatenate([inv[0, leaf, 0], inv[0, leaf, 1]], axis=1)
        real, imag = off[0, leaf, 0], off[0, leaf, 1]
        other = jnp.concatenate([jnp.concatenate([real, -imag], axis=1), jnp.concatenate([imag, real], axis=1)], axis=0)
        both = dot(mat, other, ((1,), (1,))).astype(BF)
        table = table_of(anc[0, pl.ds(leaf, 1), :], rows)
        real = dot(both[:, :blk], table, ((1,), (1,))).astype(BF)
        imag = dot(both[:, blk:], table, ((1,), (1,))).astype(BF)
        out[leaf, :, :wide] = stacked(inv[0, leaf, 0], inv[0, leaf, 1])
        out[leaf, :blk, wide : wide + rows] = -real
        out[leaf, :blk, wide + rows :] = imag
        out[leaf, blk:, wide : wide + rows] = -imag
        out[leaf, blk:, wide + rows :] = -real
        return carry

    lax.fori_loop(0, leaves, one, 0, unroll=leaves)


def fold(leaf_inv, leaf_off, ancestors, rows, after):
    _, leaves, _, blk, _ = leaf_inv.shape
    return call(
        fold_kernel, "leaf_fold", [leaf_inv, leaf_off, ancestors], [VMEM] * 3,
        shape_of((leaves, 2 * blk, 2 * blk + 2 * rows)), VMEM, after,
    )


def pack_kernel(place, inv, cpl, same, other):
    blocks, blk = inv.shape[1], inv.shape[3]
    for kind, out in enumerate((same, other)):
        block = (place[0] % blocks) ^ kind
        out[:blk] = inv[0, block, 0].astype(BF)
        out[blk : 2 * blk] = inv[0, block, 1].astype(BF)
        rest = jnp.broadcast_to(cpl[0, pl.ds(block, 1), :], (16, blk))
        row = lax.broadcasted_iota(jnp.int32, (16, blk), 0)
        value = jnp.zeros((16, blk), F32)
        for term in range(3):
            piece = rest.astype(BF).astype(F32)
            value = jnp.where(row == term, piece, value)
            rest = rest - piece
        out[2 * blk :] = value.astype(BF)


def pack(place, root_inv, coupling, after):
    _, blocks, _, blk, _ = root_inv.shape
    shape = shape_of((2 * blk + 16, blk))
    return call(
        pack_kernel, "solve_pack", [place, root_inv, coupling.reshape(1, blocks, blk)], [SMEM, VMEM, VMEM],
        [shape, shape], [VMEM, VMEM], after,
    )


def join_kernel(*refs):
    *parts, out = refs
    at = 0
    for ref in parts:
        out[at : at + ref.shape[0]] = ref[...]
        at += ref.shape[0]


def join(parts, after, name="solve_join"):
    rows = sum(part.shape[0] for part in parts)
    return call(
        join_kernel, name, parts, [VMEM] * len(parts), shape_of((rows,) + parts[0].shape[1:]), VMEM, after
    )


def first_kernel(names, keep, *refs):
    nears, outs = refs[: -len(names)], refs[-len(names) :]
    for (j, first, last), out in zip(names, outs):
        near, at = (nears[-1], 0) if j == keep.shape[0] - 1 else (nears[0], j)
        out[...] = (keep[j, first:last].astype(F32) + near[at, first:last].astype(F32)).astype(BF)


def first_sums(names, keep, nears, after):
    return call(
        functools.partial(first_kernel, names), "interface_first", [keep, *nears], [VMEM] * (1 + len(nears)),
        [shape_of((last - first,) + keep.shape[2:]) for _, first, last in names], [VMEM] * len(names), after,
    )


def second_kernel(half, keep, near, by_x, by_y, out_x, out_y):
    parts = keep.shape[1]
    for j, out, extra, first, last in ((1, out_x, by_y, half, parts), (2, out_y, by_x, 0, half)):
        for q in range(parts):
            value = keep[j, q].astype(F32) + near[j, q].astype(F32)
            if first <= q < last:
                value = value + extra[q - first].astype(F32)
            out[q] = value.astype(BF)


def second_sums(h, half, keep, near, by_x, by_y, after):
    shape = shape_of(keep.shape[1:])
    return call(
        functools.partial(second_kernel, half), f"interface_second_{h}", [keep, near, by_x, by_y], [VMEM] * 4,
        [shape, shape], [VMEM] * 2, after,
    )


def piece_of(index, blk, blocks):
    low = (index % blocks) * blk
    return index // blocks, slice(low, low + blk)


def reduce_kernel(h, slabs, blk, terms, place, rhs, keep, near, *refs):
    _, parts, _, rows, part = keep.shape
    outs, held = refs[terms:-1], refs[-1]
    for index in range(slabs):
        q, span = piece_of(index, blk, rows // blk)
        left = h * parts * part + q * part
        for plane in range(2):
            value = keep[0, q, plane, span].astype(F32) + near[0, q, plane, span].astype(F32)
            for ref in refs[:terms]:
                value = value + ref[q, plane, span].astype(F32)
            held[index, plane] = (rhs[0, plane, span, left : left + part].astype(F32) - value).astype(BF)
    for mask, out in enumerate(outs):
        out[...] = held[place[0] ^ mask]


def reduce(h, place, root_rhs, keep, near, far, slabs, blk, after):
    part = keep.shape[4]
    return call(
        functools.partial(reduce_kernel, h, slabs, blk, len(far)), "interface_reduce",
        [place, root_rhs, keep, near, *far], [SMEM] + [VMEM] * (3 + len(far)),
        [shape_of((2, blk, part))] * slabs, [VMEM] * slabs, after, [pltpu.VMEM((slabs, 2, blk, part), BF)],
    )


def chain_kernel(slabs, count, place, *refs):
    pieces, mats, outs = refs[:slabs], refs[slabs : slabs + count], refs[slabs + count : 2 * slabs + count]
    held, solver = refs[2 * slabs + count :]
    me = place[0]
    for mask in range(slabs):
        held[mask] = pieces[mask][...]
    _, _, blk, part = held.shape
    tall = solver.shape[1]
    at = 0
    for mat in mats:
        for k in range(mat.shape[0] // tall):
            solver[at] = mat[k * tall : (k + 1) * tall]
            at += 1
    state = None
    for slab in range(slabs):
        at = me ^ slab
        field = held[at].reshape(2 * blk, part).astype(F32)
        packed = solver[at]
        if state is not None:
            terms = packed[2 * blk :].astype(F32)
            row = terms[0:1] + terms[1:2] + terms[2:3]
            scale = jnp.broadcast_to(row, (blk, blk)).T[:, :1]
            field = field - jnp.concatenate([scale, scale], axis=0) * state
        mat = stacked(packed[:blk], packed[blk : 2 * blk])
        high = field.astype(BF)
        if slab:
            low = (field - high.astype(F32)).astype(BF)
            both = dot(mat, jnp.concatenate([high, low], axis=1))
            state = both[:, :part] + both[:, part:]
        else:
            state = dot(mat, high)
        held[at] = state.astype(BF).reshape(2, blk, part)
    for mask, out in enumerate(outs):
        out[...] = held[mask]


def chain(place, pieces, mats, after):
    slabs = len(pieces)
    tall = mats[0].shape
    return call(
        functools.partial(chain_kernel, slabs, len(mats)), "sweep_chain", [place, *pieces, *mats],
        [SMEM] + [VMEM] * (slabs + len(mats)),
        [shape_of(pieces[0].shape)] * slabs, [VMEM] * slabs, after,
        [pltpu.VMEM((slabs,) + pieces[0].shape, BF), pltpu.VMEM((slabs,) + tall, BF)],
    )


def collect_kernel(slabs, place, *refs):
    pieces = refs[:slabs]
    own, held = refs[slabs:]
    _, blk, _ = pieces[0].shape
    rows = own.shape[2]
    for mask, piece in enumerate(pieces):
        held[mask] = piece[...]
    for index in range(slabs):
        q, span = piece_of(index, blk, rows // blk)
        piece = held[place[0] ^ index]
        own[q, 0, span] = piece[0]
        own[q, 1, span] = piece[1]


def collect(place, pieces, rows, after):
    slabs = len(pieces)
    _, blk, part = pieces[0].shape
    return call(
        functools.partial(collect_kernel, slabs), "interface_collect", [place, *pieces], [SMEM] + [VMEM] * slabs,
        shape_of((slabs // (rows // blk), 2, rows, part)), VMEM, after, [pltpu.VMEM((slabs, 2, blk, part), BF)],
    )


def relay_kernel(half, own, by_x, by_y, to_y, to_x, near):
    to_y[...] = by_x[:half]
    to_x[...] = by_y[half:]
    for at, ref in enumerate((own, by_x, by_y)):
        near[at] = ref[...]


def relay(h, own, by_x, by_y, after):
    parts = own.shape[0]
    half = parts // 2
    return call(
        functools.partial(relay_kernel, half), f"interface_relay_{h}", [own, by_x, by_y], [VMEM] * 3,
        [shape_of((half,) + own.shape[1:]), shape_of((parts - half,) + own.shape[1:]), shape_of((3,) + own.shape)],
        [VMEM] * 3, after,
    )


def backward_kernel(jobs, count, cap, fronts, owns, aliased, owners, place, rhs, mats, *refs):
    fields, refs = refs[:count], refs[count:]
    roots, refs = refs[:owns], refs[owns + aliased :]
    out, refs = refs[0], refs[1:]
    held, slots, sems = refs[-3:]
    leaves, wide, tall = mats.shape
    blk, cols = wide // 2, rhs.shape[4] // HALVES
    tall = tall - wide
    full = fronts * cap == leaves
    copies = []
    if owns:
        root, token, wider, root_sem = refs[:4]
        token[...] = jnp.zeros(token.shape, F32)
        parts, _, _, part = roots[0].shape
        for at, ref in enumerate(roots):
            for q in range(parts):
                left = (at * parts + q) * part
                for plane in range(2):
                    wider[plane, :, left : left + part] = ref[q, plane].astype(F32)
        copies.append((True, pltpu.make_async_copy(wider, root.at[0], root_sem)))
        copies[0][1].start()
    for slot in range(fronts * cap):
        slots[slot] = -1
    for leaf in range(leaves):
        first = (owners[leaf] ^ place[1]) * cap
        spot = first
        for rank in range(cap - 1):
            spot = jnp.where(slots[first + rank] >= 0, first + rank + 1, spot)
        slots[spot] = leaf

    def solve(at, h, name, field):
        here = pl.ds(h * cols, cols)
        vec = jnp.concatenate([rhs[0, 0, name, :, here], rhs[0, 1, name, :, here]], axis=0)
        result = dot(mats[name, :, :wide], vec) + dot(mats[name, :, wide:], field)
        held[at, 0] = result[:blk].astype(BF)
        held[at, 1] = result[blk:].astype(BF)

    batch = 4
    for low in range(0, len(jobs), batch):
        ready = len(copies)
        for job in range(low, min(len(jobs), low + batch)):
            h, dist, sources = jobs[job]
            mine = [fields[at] if lead is None else fields[at].at[lead] for at, lead in sources]
            columns = [ref[q].reshape(tall, ref.shape[3]) for ref in mine for q in range(ref.shape[0])]
            field = jnp.concatenate(columns, axis=1)
            for rank in range(cap):
                at, name = job * cap + rank, slots[dist * cap + rank]
                copy = pltpu.make_async_copy(
                    held.at[at], out.at[0, :, jnp.maximum(name, 0), :, pl.ds(h * cols, cols)], sems.at[at]
                )
                copies.append((name >= 0, copy))
                if full:
                    solve(at, h, name, field)
                else:
                    pl.when(name >= 0)(functools.partial(solve, at, h, name, field))
        for there, copy in copies[ready:]:
            if full:
                copy.start()
            else:
                pl.when(there)(copy.start)

    for at, (there, copy) in enumerate(copies):
        if full or (owns and at == 0):
            copy.wait()
        else:
            pl.when(there)(copy.wait)


def backward(name, owners, place, leaf_rhs, mats, jobs, fronts, roots, before, after):
    _, _, leaves, blk, width = leaf_rhs.shape
    cap, cols = -(-leaves // fronts), width // HALVES
    flat, named = [], []
    for h, dist, field in jobs:
        sources = []
        for value in field:
            value, lead = value if isinstance(value, tuple) else (value, None)
            known = [at for at, other in enumerate(flat) if other is value]
            if not known:
                flat.append(value)
            sources.append((known[0] if known else len(flat) - 1, lead))
        named.append((h, dist, sources))
    count = len(flat)
    flat = flat + roots
    aliased = [] if before is None else [before]
    outs, specs, scratch = [shape_of((1, 2, leaves, blk, width))], [HBM], []
    if roots:
        rows = roots[0].shape[2]
        outs, specs = outs + [shape_of((1, 2, rows, width), F32), shape_of((8, 128), F32)], [HBM, HBM, VMEM]
        scratch = [pltpu.VMEM((2, rows, width), F32), pltpu.SemaphoreType.DMA]
    return call(
        functools.partial(backward_kernel, named, count, cap, fronts, len(roots), len(aliased)), name,
        [owners, place, leaf_rhs, mats, *flat, *aliased], [SMEM, SMEM] + [VMEM] * (2 + len(flat)) + [HBM] * len(aliased),
        outs, specs, after,
        scratch
        + [
            pltpu.VMEM((len(jobs) * cap, 2, blk, cols), BF),
            pltpu.SMEM((fronts * cap,), jnp.int32),
            pltpu.SemaphoreType.DMA((len(jobs) * cap,)),
        ],
        {4 + len(flat): 0} if aliased else None,
    )


def body(leaf_rhs, leaf_inv, leaf_off, parent, ancestors, root_rhs, root_inv, coupling):
    fronts, slabs = lax.axis_size("front"), lax.axis_size("slab")
    rows, width = root_rhs.shape[2], root_rhs.shape[3]
    blk = leaf_rhs.shape[3]
    owners = parent.reshape(-1)
    place = jnp.stack([lax.axis_index("slab"), lax.axis_index("front")]).astype(jnp.int32)
    pairs = fronts // 2
    parts = slabs // (rows // blk)
    part = width // HALVES // parts
    square = pairs == 4

    def start_forward(h, after):
        keep, send, last = forward(
            h, owners, place, leaf_rhs, leaf_inv, leaf_off, ancestors, fronts, rows, part, after
        )
        last = crossed(last, "front", 1)
        return keep, (crossed(send, "front", 1), last)

    def send_first(keep, near, after):
        if not square:
            sums = first_sums([(j, 0, parts) for j in range(1, pairs)], keep, near, after)
            return sums[0], [crossed(value, "front", 2 * (j + 1)) for j, value in enumerate(sums)]
        to_x, to_y = first_sums([(3, 0, parts // 2), (3, parts // 2, parts)], keep, near[1:], after)
        return to_x, [crossed(to_x, "front", 2), crossed(to_y, "front", 4)]

    def send_second(h, keep, near, got, after):
        if not square:
            return got[0], got
        to_x, to_y = second_sums(h, parts // 2, keep, near[0], *got, after)
        return to_x, [crossed(to_x, "front", 2), crossed(to_y, "front", 4)]

    def over_slabs(values):
        return [values[0]] + [crossed(values[mask], "slab", mask) for mask in range(1, slabs)]

    def share_first(own):
        return [crossed(own, "front", mask) for mask in ((2, 4) if square else range(2, fronts, 2))]

    def share_second(h, own, got, after):
        if not square:
            return got[0], []
        to_y, to_x, held = relay(h, own, *got, after)
        return to_y, [crossed(to_y, "front", 4), crossed(to_x, "front", 2), crossed(held, "front", 1)]

    def near_jobs(h, own, got, more):
        mine = [own] + got
        if square:
            fields = [field for at, value in enumerate(mine) for field in ([value], [(more[2], at)])]
        else:
            fields = [[field] for value in mine for field in (value, crossed(value, "front", 1))]
        return [(h, dist, field) for dist, field in enumerate(fields)]

    def far_jobs(mores, after):
        far = join([value for more in mores for value in more[:2]], after, "interface_join")
        there = crossed(far, "front", 1)
        jobs = []
        for h in range(len(mores)):
            span = pl.ds(h * parts, parts)
            jobs += [(h, fronts - 2, [(far, span)]), (h, fronts - 1, [(there, span)])]
        return jobs

    keep0, near0 = start_forward(0, ())
    same, other = pack(place, root_inv, coupling, [keep0])
    have, step = [same, crossed(other, "slab", 1)], 2
    token, got0 = send_first(keep0, near0, [same])
    keep1, near1 = start_forward(1, [token, have[1]])
    token, far0 = send_second(0, keep0, near0, got0, [keep1])
    token, got1 = send_first(keep1, near1, [token, near1[0]])
    while step < slabs:
        token = join(have, [token])
        have = have + [crossed(token, "slab", step)]
        step *= 2
    token, far1 = send_second(1, keep1, near1, got1, [token])
    pieces0 = reduce(0, place, root_rhs, keep0, near0[0], far0, slabs, blk, [token])
    pieces1 = reduce(1, place, root_rhs, keep1, near1[0], far1, slabs, blk, [pieces0[0]])
    solved0 = chain(place, over_slabs(pieces0), have, [pieces1[0]])
    solved1 = chain(place, over_slabs(pieces1), have, [solved0[0]])
    own0 = collect(place, over_slabs(solved0), rows, [solved1[0]])
    got0 = share_first(own0)
    own1 = collect(place, over_slabs(solved1), rows, [own0])
    got1 = share_first(own1)
    folded = fold(leaf_inv, leaf_off, ancestors, rows, [own1])
    token, more0 = share_second(0, own0, got0, [folded])
    token, more1 = share_second(1, own1, got1, [token])
    leaf_sol, root_sol, token = backward(
        "leaf_backward", owners, place, leaf_rhs, folded, near_jobs(0, own0, got0, more0), fronts, [own0, own1], None, [token]
    )
    (leaf_sol,) = backward(
        "leaf_backward", owners, place, leaf_rhs, folded, near_jobs(1, own1, got1, more1), fronts, [], leaf_sol, ()
    )
    if square:
        jobs = far_jobs((more0, more1), [token])
        (leaf_sol,) = backward("leaf_backward", owners, place, leaf_rhs, folded, jobs, fronts, [], leaf_sol, ())
    return leaf_sol, root_sol


def solution(mesh):
    in_specs = (
        P("slab", None, "front", None, None),
        P("slab", "front", None, None, None),
        P("slab", "front", None, None, None),
        P("slab", "front", None),
        P("slab", "front", None),
        P("slab", None, "front", None),
        P("slab", "front", None, None, None),
        P("slab", "front"),
    )
    out_specs = (P("slab", None, "front", None, None), P("slab", None, "front", None))
    return jax.shard_map(body, mesh=mesh, in_specs=in_specs, out_specs=out_specs, check_vma=False)
```

```python
import functools

import jax
import jax.numpy as jnp
from jax import lax
from jax.experimental import pallas as pl
from jax.experimental.pallas import tpu as pltpu
from jax.sharding import PartitionSpec as P

HALVES = 2
FIRST_ROOM = 51
BRIEF = ("solve_join", "interface_first", "interface_join", "interface_second_1", "interface_relay_0")
BF = jnp.bfloat16
F32 = jnp.float32
VMEM = pl.BlockSpec(memory_space=pltpu.VMEM)
SMEM = pl.BlockSpec(memory_space=pltpu.SMEM)
HBM = pl.BlockSpec(memory_space=pltpu.HBM)
ANY = pl.BlockSpec(memory_space=pl.ANY)


def shape_of(shape, dtype=BF):
    return jax.ShapeDtypeStruct(shape, dtype)


def call(kernel, name, ins, in_specs, outs, out_specs, after=(), scratch=(), aliases=None, room=24):
    count, extra = len(ins), len(after)

    def wrapped(*refs):
        kernel(*refs[:count], *refs[count + extra :])

    return pl.pallas_call(
        wrapped,
        in_specs=list(in_specs) + [ANY] * extra,
        out_specs=out_specs,
        out_shape=outs,
        scratch_shapes=list(scratch),
        input_output_aliases=aliases or {},
        compiler_params=pltpu.CompilerParams(vmem_limit_bytes=room * 1024 * 1024),
        cost_estimate=pl.CostEstimate(flops=1 if name in BRIEF else 10**10, bytes_accessed=1, transcendentals=0),
        name=name,
    )(*ins, *after)


def crossed(x, axis, mask):
    return lax.ppermute(x, axis, [(i, i ^ mask) for i in range(lax.axis_size(axis))])


def stacked(real, imag):
    return jnp.concatenate(
        [jnp.concatenate([real, -imag], axis=1), jnp.concatenate([imag, real], axis=1)], axis=0
    )


def dot(a, b, dims=((1,), (0,)), precision=None):
    return lax.dot_general(a, b, (dims, ((), ())), precision=precision, preferred_element_type=F32)


def table_of(anc_row, rows):
    ids = lax.broadcasted_iota(jnp.int32, (rows, anc_row.shape[1]), 0)
    return (ids == anc_row).astype(F32).astype(BF)


def forward_kernel(h, group, cap, owners, place, rhs, inv, off, anc, keep, send, last, part, ids, seen, *rest):
    leaves, blk, cols = rhs.shape[2], rhs.shape[3], part.shape[4]
    fronts, rows, width = part.shape[0], keep.shape[3], keep.shape[4]
    me = place[1]
    if rest:
        vecs, invs, offs, ancs, sems = rest
        small = pltpu.make_async_copy(anc.at[0], ancs, sems.at[leaves // group, 0])

        def copies(at):
            span = pl.ds(at * group, group)
            return (
                pltpu.make_async_copy(inv.at[0, span], invs.at[span], sems.at[at, 0]),
                pltpu.make_async_copy(rhs.at[0, :, span, :, pl.ds(h * cols, cols)], vecs.at[:, span], sems.at[at, 1]),
                pltpu.make_async_copy(off.at[0, span], offs.at[span], sems.at[at, 2]),
            )

        for at in range(leaves // group):
            for copy in copies(at):
                copy.start()
        small.start()
    else:
        vecs, invs, offs, ancs = rhs.at[0, :, :, :, pl.ds(h * cols, cols)], inv.at[0], off.at[0], anc.at[0]
    ids[...] = jnp.full(ids.shape, -1, jnp.int32)
    for dist in range(fronts):
        seen[dist] = 0
    if rest:
        small.wait()

    for at in range(leaves // group):
        for copy in copies(at) if rest else ():
            copy.wait()
        names = [at * group + j for j in range(group)]
        values = []
        for leaf in names:
            vec = jnp.concatenate([vecs[0, leaf], vecs[1, leaf]], axis=0)
            values.append(dot(stacked(invs[leaf, 0], invs[leaf, 1]), vec).astype(BF))
        moved = [dot(stacked(offs[leaf, 0], offs[leaf, 1]), value).astype(BF) for leaf, value in zip(names, values)]
        for leaf, shift in zip(names, moved):
            dist = owners[leaf] ^ me
            rank = seen[dist]
            seen[dist] = rank + 1
            part[dist, 0, rank] = shift[:blk]
            part[dist, 1, rank] = shift[blk:]
            ids[pl.ds(dist * cap + rank, 1), :] = ancs[pl.ds(leaf, 1), :]

    for dist in range(fronts if fronts * cap > leaves else 0):
        for rank in range(cap):

            @pl.when(seen[dist] <= rank)
            def _(dist=dist, rank=rank):
                part[dist, 0, rank] = jnp.zeros((blk, cols), BF)
                part[dist, 1, rank] = jnp.zeros((blk, cols), BF)

    for dist in range(fronts):
        row = jnp.concatenate([ids[dist * cap + rank : dist * cap + rank + 1, :] for rank in range(cap)], axis=1)
        table = table_of(row, rows)
        out = keep if dist % 2 == 0 else send if dist < fronts - 1 else last
        spot = 0 if dist == fronts - 1 else dist // 2
        for plane in range(2):
            value = dot(table, part[dist, plane].reshape(cap * blk, cols)).astype(BF)
            for q in range(cols // width):
                out[spot, q, plane] = value[:, q * width : (q + 1) * width]


def forward(h, owners, place, leaf_rhs, leaf_inv, leaf_off, ancestors, fronts, rows, part, after):
    _, _, leaves, blk, width = leaf_rhs.shape
    cols = width // HALVES
    cap = -(-leaves // fronts)
    group = 8
    block = (cols // part, 2, rows, part)
    scratch = [
        pltpu.VMEM((fronts, 2, cap, blk, cols), BF),
        pltpu.VMEM((fronts * cap, blk), jnp.int32),
        pltpu.SMEM((fronts,), jnp.int32),
    ]
    if h == 0:
        scratch += [
            pltpu.VMEM((2, leaves, blk, cols), BF),
            pltpu.VMEM((leaves, 2, blk, blk), BF),
            pltpu.VMEM((leaves, 2, blk, blk), BF),
            pltpu.VMEM((leaves, blk), jnp.int32),
            pltpu.SemaphoreType.DMA((leaves // group + 1, 3)),
        ]
    return call(
        functools.partial(forward_kernel, h, group, cap),
        "leaf_forward",
        [owners, place, leaf_rhs, leaf_inv, leaf_off, ancestors],
        [SMEM, SMEM] + [VMEM if h else HBM] * 4,
        [shape_of((fronts // 2,) + block), shape_of((fronts // 2 - 1,) + block), shape_of((1,) + block)],
        [VMEM, VMEM, VMEM],
        after,
        scratch,
        room=24 if h else FIRST_ROOM,
    )


def fold_kernel(inv, off, anc, out):
    leaves, _, blk, _ = inv.shape[1:]
    wide = 2 * blk
    rows = (out.shape[2] - wide) // 2

    def one(leaf, carry):
        mat = jnp.concatenate([inv[0, leaf, 0], inv[0, leaf, 1]], axis=1)
        real, imag = off[0, leaf, 0], off[0, leaf, 1]
        other = jnp.concatenate([jnp.concatenate([real, -imag], axis=1), jnp.concatenate([imag, real], axis=1)], axis=0)
        both = dot(mat, other, ((1,), (1,))).astype(BF)
        table = table_of(anc[0, pl.ds(leaf, 1), :], rows)
        real = dot(both[:, :blk], table, ((1,), (1,))).astype(BF)
        imag = dot(both[:, blk:], table, ((1,), (1,))).astype(BF)
        out[leaf, :, :wide] = stacked(inv[0, leaf, 0], inv[0, leaf, 1])
        out[leaf, :blk, wide : wide + rows] = -real
        out[leaf, :blk, wide + rows :] = imag
        out[leaf, blk:, wide : wide + rows] = -imag
        out[leaf, blk:, wide + rows :] = -real
        return carry

    lax.fori_loop(0, leaves, one, 0, unroll=leaves)


def fold(leaf_inv, leaf_off, ancestors, rows, after):
    _, leaves, _, blk, _ = leaf_inv.shape
    return call(
        fold_kernel, "leaf_fold", [leaf_inv, leaf_off, ancestors], [VMEM] * 3,
        shape_of((leaves, 2 * blk, 2 * blk + 2 * rows)), VMEM, after,
    )


def pack_kernel(place, inv, cpl, same, other):
    blocks, blk = inv.shape[1], inv.shape[3]
    for kind, out in enumerate((same, other)):
        block = (place[0] % blocks) ^ kind
        out[:blk] = inv[0, block, 0].astype(BF)
        out[blk : 2 * blk] = inv[0, block, 1].astype(BF)
        rest = jnp.broadcast_to(cpl[0, pl.ds(block, 1), :], (16, blk))
        row = lax.broadcasted_iota(jnp.int32, (16, blk), 0)
        value = jnp.zeros((16, blk), F32)
        for term in range(3):
            piece = rest.astype(BF).astype(F32)
            value = jnp.where(row == term, piece, value)
            rest = rest - piece
        out[2 * blk :] = value.astype(BF)


def pack(place, root_inv, coupling, after):
    _, blocks, _, blk, _ = root_inv.shape
    shape = shape_of((2 * blk + 16, blk))
    return call(
        pack_kernel, "solve_pack", [place, root_inv, coupling.reshape(1, blocks, blk)], [SMEM, VMEM, VMEM],
        [shape, shape], [VMEM, VMEM], after,
    )


def join_kernel(*refs):
    *parts, out = refs
    at = 0
    for ref in parts:
        out[at : at + ref.shape[0]] = ref[...]
        at += ref.shape[0]


def join(parts, after, name="solve_join"):
    rows = sum(part.shape[0] for part in parts)
    return call(
        join_kernel, name, parts, [VMEM] * len(parts), shape_of((rows,) + parts[0].shape[1:]), VMEM, after
    )


def first_kernel(names, keep, *refs):
    nears, outs = refs[: -len(names)], refs[-len(names) :]
    for (j, first, last), out in zip(names, outs):
        near, at = (nears[-1], 0) if j == keep.shape[0] - 1 else (nears[0], j)
        out[...] = (keep[j, first:last].astype(F32) + near[at, first:last].astype(F32)).astype(BF)


def first_sums(names, keep, nears, after):
    return call(
        functools.partial(first_kernel, names), "interface_first", [keep, *nears], [VMEM] * (1 + len(nears)),
        [shape_of((last - first,) + keep.shape[2:]) for _, first, last in names], [VMEM] * len(names), after,
    )


def second_kernel(half, keep, near, by_x, by_y, out_x, out_y):
    parts = keep.shape[1]
    for j, out, extra, first, last in ((1, out_x, by_y, half, parts), (2, out_y, by_x, 0, half)):
        for q in range(parts):
            value = keep[j, q].astype(F32) + near[j, q].astype(F32)
            if first <= q < last:
                value = value + extra[q - first].astype(F32)
            out[q] = value.astype(BF)


def second_sums(h, half, keep, near, by_x, by_y, after):
    shape = shape_of(keep.shape[1:])
    return call(
        functools.partial(second_kernel, half), f"interface_second_{h}", [keep, near, by_x, by_y], [VMEM] * 4,
        [shape, shape], [VMEM] * 2, after,
    )


def piece_of(index, blk, blocks):
    low = (index % blocks) * blk
    return index // blocks, slice(low, low + blk)


def reduce_kernel(h, slabs, blk, terms, place, rhs, keep, near, *refs):
    _, parts, _, rows, part = keep.shape
    outs, held = refs[terms:-1], refs[-1]
    for index in range(slabs):
        q, span = piece_of(index, blk, rows // blk)
        left = h * parts * part + q * part
        for plane in range(2):
            value = keep[0, q, plane, span].astype(F32) + near[0, q, plane, span].astype(F32)
            for ref in refs[:terms]:
                value = value + ref[q, plane, span].astype(F32)
            held[index, plane] = (rhs[0, plane, span, left : left + part].astype(F32) - value).astype(BF)
    for mask, out in enumerate(outs):
        out[...] = held[place[0] ^ mask]


def reduce(h, place, root_rhs, keep, near, far, slabs, blk, after):
    part = keep.shape[4]
    return call(
        functools.partial(reduce_kernel, h, slabs, blk, len(far)), "interface_reduce",
        [place, root_rhs, keep, near, *far], [SMEM] + [VMEM] * (3 + len(far)),
        [shape_of((2, blk, part))] * slabs, [VMEM] * slabs, after, [pltpu.VMEM((slabs, 2, blk, part), BF)],
    )


def chain_kernel(slabs, count, place, *refs):
    pieces, mats, outs = refs[:slabs], refs[slabs : slabs + count], refs[slabs + count : 2 * slabs + count]
    held, solver = refs[2 * slabs + count :]
    me = place[0]
    for mask in range(slabs):
        held[mask] = pieces[mask][...]
    _, _, blk, part = held.shape
    tall = solver.shape[1]
    at = 0
    for mat in mats:
        for k in range(mat.shape[0] // tall):
            solver[at] = mat[k * tall : (k + 1) * tall]
            at += 1
    state = None
    for slab in range(slabs):
        at = me ^ slab
        field = held[at].reshape(2 * blk, part).astype(F32)
        packed = solver[at]
        if state is not None:
            terms = packed[2 * blk :].astype(F32)
            row = terms[0:1] + terms[1:2] + terms[2:3]
            scale = jnp.broadcast_to(row, (blk, blk)).T[:, :1]
            field = field - jnp.concatenate([scale, scale], axis=0) * state
        mat = stacked(packed[:blk], packed[blk : 2 * blk])
        high = field.astype(BF)
        if slab:
            low = (field - high.astype(F32)).astype(BF)
            both = dot(mat, jnp.concatenate([high, low], axis=1))
            state = both[:, :part] + both[:, part:]
        else:
            state = dot(mat, high)
        held[at] = state.astype(BF).reshape(2, blk, part)
    for mask, out in enumerate(outs):
        out[...] = held[mask]


def chain(place, pieces, mats, after):
    slabs = len(pieces)
    tall = mats[0].shape
    return call(
        functools.partial(chain_kernel, slabs, len(mats)), "sweep_chain", [place, *pieces, *mats],
        [SMEM] + [VMEM] * (slabs + len(mats)),
        [shape_of(pieces[0].shape)] * slabs, [VMEM] * slabs, after,
        [pltpu.VMEM((slabs,) + pieces[0].shape, BF), pltpu.VMEM((slabs,) + tall, BF)],
    )


def collect_kernel(slabs, place, *refs):
    pieces = refs[:slabs]
    own, held = refs[slabs:]
    _, blk, _ = pieces[0].shape
    rows = own.shape[2]
    for mask, piece in enumerate(pieces):
        held[mask] = piece[...]
    for index in range(slabs):
        q, span = piece_of(index, blk, rows // blk)
        piece = held[place[0] ^ index]
        own[q, 0, span] = piece[0]
        own[q, 1, span] = piece[1]


def collect(place, pieces, rows, after):
    slabs = len(pieces)
    _, blk, part = pieces[0].shape
    return call(
        functools.partial(collect_kernel, slabs), "interface_collect", [place, *pieces], [SMEM] + [VMEM] * slabs,
        shape_of((slabs // (rows // blk), 2, rows, part)), VMEM, after, [pltpu.VMEM((slabs, 2, blk, part), BF)],
    )


def relay_kernel(half, own, by_x, by_y, to_y, to_x, near):
    to_y[...] = by_x[:half]
    to_x[...] = by_y[half:]
    for at, ref in enumerate((own, by_x, by_y)):
        near[at] = ref[...]


def relay(h, own, by_x, by_y, after):
    parts = own.shape[0]
    half = parts // 2
    return call(
        functools.partial(relay_kernel, half), f"interface_relay_{h}", [own, by_x, by_y], [VMEM] * 3,
        [shape_of((half,) + own.shape[1:]), shape_of((parts - half,) + own.shape[1:]), shape_of((3,) + own.shape)],
        [VMEM] * 3, after,
    )


def backward_kernel(jobs, count, cap, fronts, owns, aliased, owners, place, rhs, mats, *refs):
    fields, refs = refs[:count], refs[count:]
    roots, refs = refs[:owns], refs[owns + aliased :]
    out, refs = refs[0], refs[1:]
    held, slots, sems = refs[-3:]
    leaves, wide, tall = mats.shape
    blk, cols = wide // 2, rhs.shape[4] // HALVES
    tall = tall - wide
    full = fronts * cap == leaves
    copies = []
    if owns:
        root, token, wider, root_sem = refs[:4]
        token[...] = jnp.zeros(token.shape, F32)
        parts, _, _, part = roots[0].shape
        for at, ref in enumerate(roots):
            for q in range(parts):
                left = (at * parts + q) * part
                for plane in range(2):
                    wider[plane, :, left : left + part] = ref[q, plane].astype(F32)
        copies.append((True, pltpu.make_async_copy(wider, root.at[0], root_sem)))
        copies[0][1].start()
    for slot in range(fronts * cap):
        slots[slot] = -1
    for leaf in range(leaves):
        first = (owners[leaf] ^ place[1]) * cap
        spot = first
        for rank in range(cap - 1):
            spot = jnp.where(slots[first + rank] >= 0, first + rank + 1, spot)
        slots[spot] = leaf

    def solve(at, h, name, field):
        here = pl.ds(h * cols, cols)
        vec = jnp.concatenate([rhs[0, 0, name, :, here], rhs[0, 1, name, :, here]], axis=0)
        result = dot(mats[name, :, :wide], vec) + dot(mats[name, :, wide:], field)
        held[at, 0] = result[:blk].astype(BF)
        held[at, 1] = result[blk:].astype(BF)

    batch = -(-len(jobs) // 2)
    for low in range(0, len(jobs), batch):
        ready = len(copies)
        for job in range(low, min(len(jobs), low + batch)):
            h, dist, sources = jobs[job]
            mine = [fields[at] if lead is None else fields[at].at[lead] for at, lead in sources]
            columns = [ref[q].reshape(tall, ref.shape[3]) for ref in mine for q in range(ref.shape[0])]
            field = jnp.concatenate(columns, axis=1)
            for rank in range(cap):
                at, name = job * cap + rank, slots[dist * cap + rank]
                copy = pltpu.make_async_copy(
                    held.at[at], out.at[0, :, jnp.maximum(name, 0), :, pl.ds(h * cols, cols)], sems.at[at]
                )
                copies.append((name >= 0, copy))
                if full:
                    solve(at, h, name, field)
                else:
                    pl.when(name >= 0)(functools.partial(solve, at, h, name, field))
        for there, copy in copies[ready:]:
            if full:
                copy.start()
            else:
                pl.when(there)(copy.start)

    for at, (there, copy) in enumerate(copies):
        if full or (owns and at == 0):
            copy.wait()
        else:
            pl.when(there)(copy.wait)


def backward(name, owners, place, leaf_rhs, mats, jobs, fronts, roots, before, after):
    _, _, leaves, blk, width = leaf_rhs.shape
    cap, cols = -(-leaves // fronts), width // HALVES
    flat, named = [], []
    for h, dist, field in jobs:
        sources = []
        for value in field:
            value, lead = value if isinstance(value, tuple) else (value, None)
            known = [at for at, other in enumerate(flat) if other is value]
            if not known:
                flat.append(value)
            sources.append((known[0] if known else len(flat) - 1, lead))
        named.append((h, dist, sources))
    count = len(flat)
    flat = flat + roots
    aliased = [] if before is None else [before]
    outs, specs, scratch = [shape_of((1, 2, leaves, blk, width))], [HBM], []
    if roots:
        rows = roots[0].shape[2]
        outs, specs = outs + [shape_of((1, 2, rows, width), F32), shape_of((8, 128), F32)], [HBM, HBM, VMEM]
        scratch = [pltpu.VMEM((2, rows, width), F32), pltpu.SemaphoreType.DMA]
    return call(
        functools.partial(backward_kernel, named, count, cap, fronts, len(roots), len(aliased)), name,
        [owners, place, leaf_rhs, mats, *flat, *aliased], [SMEM, SMEM] + [VMEM] * (2 + len(flat)) + [HBM] * len(aliased),
        outs, specs, after,
        scratch
        + [
            pltpu.VMEM((len(jobs) * cap, 2, blk, cols), BF),
            pltpu.SMEM((fronts * cap,), jnp.int32),
            pltpu.SemaphoreType.DMA((len(jobs) * cap,)),
        ],
        {4 + len(flat): 0} if aliased else None,
    )


def body(leaf_rhs, leaf_inv, leaf_off, parent, ancestors, root_rhs, root_inv, coupling):
    fronts, slabs = lax.axis_size("front"), lax.axis_size("slab")
    rows, width = root_rhs.shape[2], root_rhs.shape[3]
    blk = leaf_rhs.shape[3]
    owners = parent.reshape(-1)
    place = jnp.stack([lax.axis_index("slab"), lax.axis_index("front")]).astype(jnp.int32)
    pairs = fronts // 2
    parts = slabs // (rows // blk)
    part = width // HALVES // parts
    square = pairs == 4

    def start_forward(h, after):
        keep, send, last = forward(
            h, owners, place, leaf_rhs, leaf_inv, leaf_off, ancestors, fronts, rows, part, after
        )
        last = crossed(last, "front", 1)
        return keep, (crossed(send, "front", 1), last)

    def send_first(keep, near, after):
        if not square:
            sums = first_sums([(j, 0, parts) for j in range(1, pairs)], keep, near, after)
            return sums[0], [crossed(value, "front", 2 * (j + 1)) for j, value in enumerate(sums)]
        to_x, to_y = first_sums([(3, 0, parts // 2), (3, parts // 2, parts)], keep, near[1:], after)
        return to_x, [crossed(to_x, "front", 2), crossed(to_y, "front", 4)]

    def send_second(h, keep, near, got, after):
        if not square:
            return got[0], got
        to_x, to_y = second_sums(h, parts // 2, keep, near[0], *got, after)
        return to_x, [crossed(to_x, "front", 2), crossed(to_y, "front", 4)]

    def over_slabs(values):
        return [values[0]] + [crossed(values[mask], "slab", mask) for mask in range(1, slabs)]

    def share_first(own):
        return [crossed(own, "front", mask) for mask in ((2, 4) if square else range(2, fronts, 2))]

    def share_second(h, own, got, after):
        if not square:
            return got[0], []
        to_y, to_x, held = relay(h, own, *got, after)
        return to_y, [crossed(to_y, "front", 4), crossed(to_x, "front", 2), crossed(held, "front", 1)]

    def near_jobs(h, own, got, more):
        mine = [own] + got
        if square:
            fields = [field for at, value in enumerate(mine) for field in ([value], [(more[2], at)])]
        else:
            fields = [[field] for value in mine for field in (value, crossed(value, "front", 1))]
        return [(h, dist, field) for dist, field in enumerate(fields)]

    def far_jobs(mores, after):
        far = join([value for more in mores for value in more[:2]], after, "interface_join")
        there = crossed(far, "front", 1)
        jobs = []
        for h in range(len(mores)):
            span = pl.ds(h * parts, parts)
            jobs += [(h, fronts - 2, [(far, span)]), (h, fronts - 1, [(there, span)])]
        return jobs

    keep0, near0 = start_forward(0, ())
    same, other = pack(place, root_inv, coupling, [keep0])
    have, step = [same, crossed(other, "slab", 1)], 2
    token, got0 = send_first(keep0, near0, [same])
    keep1, near1 = start_forward(1, [token, have[1]])
    token, far0 = send_second(0, keep0, near0, got0, [keep1])
    token, got1 = send_first(keep1, near1, [token, near1[0]])
    while step < slabs:
        token = join(have, [token])
        have = have + [crossed(token, "slab", step)]
        step *= 2
    token, far1 = send_second(1, keep1, near1, got1, [token])
    pieces0 = reduce(0, place, root_rhs, keep0, near0[0], far0, slabs, blk, [token])
    pieces1 = reduce(1, place, root_rhs, keep1, near1[0], far1, slabs, blk, [pieces0[0]])
    solved0 = chain(place, over_slabs(pieces0), have, [pieces1[0]])
    solved1 = chain(place, over_slabs(pieces1), have, [solved0[0]])
    own0 = collect(place, over_slabs(solved0), rows, [solved1[0]])
    got0 = share_first(own0)
    own1 = collect(place, over_slabs(solved1), rows, [own0])
    got1 = share_first(own1)
    folded = fold(leaf_inv, leaf_off, ancestors, rows, [own1])
    token, more0 = share_second(0, own0, got0, [folded])
    token, more1 = share_second(1, own1, got1, [token])
    leaf_sol, root_sol, token = backward(
        "leaf_backward", owners, place, leaf_rhs, folded, near_jobs(0, own0, got0, more0), fronts, [own0, own1], None, [token]
    )
    (leaf_sol,) = backward(
        "leaf_backward", owners, place, leaf_rhs, folded, near_jobs(1, own1, got1, more1), fronts, [], leaf_sol, ()
    )
    if square:
        jobs = far_jobs((more0, more1), [token])
        (leaf_sol,) = backward("leaf_backward", owners, place, leaf_rhs, folded, jobs, fronts, [], leaf_sol, ())
    return leaf_sol, root_sol


def solution(mesh):
    in_specs = (
        P("slab", None, "front", None, None),
        P("slab", "front", None, None, None),
        P("slab", "front", None, None, None),
        P("slab", "front", None),
        P("slab", "front", None),
        P("slab", None, "front", None),
        P("slab", "front", None, None, None),
        P("slab", "front"),
    )
    out_specs = (P("slab", None, "front", None, None), P("slab", None, "front", None))
    return jax.shard_map(body, mesh=mesh, in_specs=in_specs, out_specs=out_specs, check_vma=False)
```
